32 devices in a mesh: wide: 4 (over y, x), narrow: 2 (over core), rep: 4 (over z).
Axes of the slice: x: 2, y: 2, z: 4, core: 2. Of those that a mesh axis runs over, the one named last changes fastest.
Arguments:
- queries: bfloat16 [4096, 2048], P(('rep', 'wide'), 'narrow'), parts along dimension 0, may hold values from -20 to 20
- key_rows: bfloat16 [4096, 512], P(('rep', 'wide'), 'narrow'), parts along dimension 0, may hold values from -20 to 20
- value_rows: bfloat16 [4096, 512], P(('rep', 'wide'), 'narrow'), parts along dimension 0, may hold values from -20 to 20
- residual: bfloat16 [4096, 4096], P(('rep', 'wide', 'narrow')), parts along dimension 0, may hold values from -9 to 9
- out_weight: bfloat16 [2048, 4096], P('narrow'), may hold values from -0.125 to 0.125
- norm_gain: bfloat16 [4096], replicated, may hold values from 0.099609375 to 1.8984375
- span_map: int32 [4], replicated, may hold values from 0 to 3, each once
- segments: int32 [16, 128], P(('rep', 'wide')), parts along dimension 0, may hold values from 0 to 8, as said below
- row_owner: int32 [4096, 1], P(('rep', 'wide', 'narrow')), parts along dimension 0, may hold values from 0 to 3; in each aligned block of 128 rows (0 to 127, 128 to 255, ...) at most 64 rows name the same one
Outputs:
- hidden: bfloat16 [4096, 4096], P(('rep', 'wide', 'narrow')), parts along dimension 0
- ffn_in: bfloat16 [16, 2, 4, 64, 4096], P(('rep', 'wide'), 'narrow'), parts along dimension 0
The draws below stay inside these ranges and needn't reach their ends.
There are 4 independent parts, one for each index of `rep`. The reference program is written for one: setup_inputs(seed, part) draws one part's arguments, and reference() takes and returns one part's arrays. A program takes and returns all parts, laid end to end along the dimension named above; an argument that names none is the same for every part. Nothing has to cross between parts.
Inputs may be any that keep to these rules, and one draw needn't show every extreme that they name: `segments`: in each token block the short document numbers start at 0, never fall, and rise by at most one from a row to the next; short rows 0 and 1 lie in the same document; some token block reaches the largest number. `row_owner`: within each aligned block of 128 rows no owner is named by more than 64 rows; in some blocks an owner is named by exactly 64 rows.
All inputs are finite; a program needn't handle non-finite values.
Results may differ from the reference program's by a relative error of at most 0.012.
Values may be sent and summed in bfloat16 or wider, within the bound.
A program may use at most 64 MiB of HBM per device.

```python
import math
import jax
import jax.numpy as jnp
import numpy as np
from jax import lax

D = 4096
HEAD = 128
QH = 16
KVH = 4
LONG_DEV = 128
SHORT_DEV = 128
TOK_DEV = 256
ROWS_DEV = 128
CAP = 64
TOKENS = 1024
N_WIDE = 4
N_NARROW = 2


def draw_queries(key, part):
    base = 2.0 * jnp.clip(jax.random.normal(jax.random.fold_in(key, 7), (TOKENS, QH * HEAD), jnp.float32), -6.0, 6.0)
    return base.astype(jnp.bfloat16)


def draw_key_rows(key, part):
    base = jnp.clip(jax.random.normal(jax.random.fold_in(key, 9), (TOKENS, KVH * HEAD), jnp.float32), -6.0, 6.0)
    return base.astype(jnp.bfloat16)


def draw_residual(key, part):
    columns = jnp.arange(D, dtype=jnp.float32) / D
    column_scale = jnp.exp(columns * math.log(3.0))[None, :]
    base = 0.3 * column_scale * jnp.clip(jax.random.normal(jax.random.fold_in(key, 15), (TOKENS, D), jnp.float32), -6.0, 6.0)
    return base.astype(jnp.bfloat16)


def draw_segments(key, part):
    wide_count = TOKENS // TOK_DEV
    odds = max(4, SHORT_DEV // 2)
    bound = max(2, SHORT_DEV // 16)
    step = (SHORT_DEV - 2) // bound
    starts = (jax.random.randint(jax.random.fold_in(key, 31), (wide_count, SHORT_DEV), 0, odds) == 0).astype(jnp.int32)
    starts = starts.at[:, :2].set(0)
    places = jnp.arange(SHORT_DEV, dtype=jnp.int32)
    forced = ((places >= 2) & ((places - 2) % step == 0) & ((places - 2) // step < bound)).astype(jnp.int32)
    forced_block = jax.random.randint(jax.random.fold_in(key, 33), (), 0, wide_count)
    selected = (jnp.arange(wide_count, dtype=jnp.int32) == forced_block)[:, None]
    starts = jnp.where(selected, jnp.maximum(starts, forced[None, :]), starts)
    return jnp.minimum(jnp.cumsum(starts, axis=1), bound).astype(jnp.int32)


def block_levels(own_key, shape, pieces, least, top_value):
    gain = 1.0
    for dim, blocks in pieces:
        heights = jax.random.uniform(jax.random.fold_in(jax.random.fold_in(own_key, 6), dim), (blocks,), jnp.float32, least / len(pieces), top_value / len(pieces))
        gain = gain * jnp.repeat(jnp.exp(heights), shape[dim] // blocks).reshape((-1,) + (1,) * (len(shape) - 1 - dim))
    return gain


def deal_out(key, own, number, rows, amount, top, reach, slope):
    ranking = jax.random.permutation(key, amount)
    crowded, ordinary = portions_of(amount, rows * top, reach, slope, True), portions_of(amount, rows * top, reach, slope, False)
    places = jnp.arange(amount)

    def named(tallies, offset_by):
        used = int((tallies > 0).sum())
        fixed = max(1, used // 4)
        moved = fixed + (places - fixed + offset_by * (used - fixed)) % max(1, amount - fixed)
        return jnp.zeros((amount,), jnp.int32).at[ranking[jnp.where(places < fixed, places, moved)]].set(jnp.asarray(tallies, jnp.int32))

    tallies = jnp.where(number % 4 == 0, named(crowded, number // 4), named(ordinary, number - number // 4 - 1))
    mixed = jax.random.permutation(jax.random.fold_in(own, 3), amount)
    giver, taker = mixed[0:amount // 2 * 2:2], mixed[1:amount // 2 * 2:2]
    slack = jnp.minimum(tallies[giver] - 1, reach - tallies[taker]) // 2
    slack = jnp.where((giver == ranking[0]) | (taker == ranking[0]) | (tallies[taker] == 0), 0, jnp.maximum(slack, 0))
    moved = jax.random.randint(jax.random.fold_in(own, 4), (amount // 2,), 0, 1 << 20) % (slack + 1)
    tallies = tallies.at[giver].add(-moved).at[taker].add(moved)
    labels = jnp.searchsorted(jnp.cumsum(tallies), jnp.arange(rows * top), side="right").astype(jnp.int32)
    table = labels.reshape(top, rows).T
    table = table[jax.random.permutation(jax.random.fold_in(own, 1), rows)]
    offset_by = jax.random.randint(jax.random.fold_in(own, 2), (rows, 1), 0, top)
    return jnp.take_along_axis(table, (jnp.arange(top)[None, :] + offset_by) % top, axis=1)


def portions_of(amount, total, most, lean, full):
    weights = [(1 << 20) // math.isqrt(grade ** lean) + 1 for grade in range(1, amount + 1)]
    largest = most if full else min(most, max(-(-total // amount), total * weights[0] // sum(weights)))
    least = 1 if total - largest >= amount - 1 else 0
    counts, rest = [largest] + [least] * (amount - 1), total - largest - least * (amount - 1)
    while rest > 0:
        candidates = [i for i in range(1, amount) if counts[i] < largest] or [i for i in range(1, amount) if counts[i] < most]
        mass, left = sum([weights[i] for i in candidates]), rest
        for i in candidates:
            addition = min(most - counts[i], max(1, left * weights[i] // mass), rest)
            counts[i] = counts[i] + addition
            rest = rest - addition
    return np.array(counts)


def centred(rng, shape, deviation, limit, shards=(), kind=jnp.bfloat16):
    gain = block_levels(rng, shape, shards, -0.22, 0.18) if shards else 1.0
    values = jax.random.normal(rng, shape, jnp.float32) * deviation * gain
    return jnp.minimum(jnp.maximum(values, -limit), limit).astype(kind)


def setup_inputs(seed: int = 0, part: int = 0) -> dict:
    keys = jax.random.split(jax.random.key(seed), 10)
    own_keys = jax.random.split(jax.random.fold_in(keys[9], part), 10)
    queries = draw_queries(jax.random.fold_in(jax.random.fold_in(keys[9], part), 71), part)
    key_rows = draw_key_rows(jax.random.fold_in(jax.random.fold_in(keys[9], part), 71), part)
    value_rows = centred(own_keys[2], (TOKENS, KVH * HEAD), 4.0, 20.0, ((0, 4), (1, 2)))
    residual = draw_residual(jax.random.fold_in(jax.random.fold_in(keys[9], part), 71), part)
    out_weight = centred(keys[4], (QH * HEAD, D), (QH * HEAD) ** -0.5, 0.125, ((0, 2),))
    norm_gain = jnp.clip(1.0 + 0.18 * jax.random.normal(keys[5], (D,), jnp.float32), 0.099609375, 1.8984375).astype(jnp.bfloat16)
    span_map = jax.random.permutation(keys[6], N_WIDE).astype(jnp.int32)
    segments = draw_segments(jax.random.fold_in(jax.random.fold_in(keys[9], part), 71), part)
    row_owner_keys = jax.random.split(jax.random.fold_in(own_keys[8], 1), TOKENS // ROWS_DEV)
    row_owner_turns = jax.random.permutation(jax.random.fold_in(own_keys[8], 3), TOKENS // ROWS_DEV)
    row_owner = jax.vmap(lambda own, number: deal_out(jax.random.fold_in(own_keys[8], 2), own, number, ROWS_DEV, N_WIDE, 1, CAP, 0))(row_owner_keys, row_owner_turns).reshape((TOKENS, 1))
    return {"queries": queries, "key_rows": key_rows, "value_rows": value_rows, "residual": residual, "out_weight": out_weight, "norm_gain": norm_gain, "span_map": span_map, "segments": segments, "row_owner": row_owner}


def attend(scores, visible, vals):
    masked = jnp.where(visible[:, None, None, :], scores, -1e+30)
    row_max = lax.optimization_barrier(jnp.max(masked, axis=-1, keepdims=True))
    weights = jnp.where(visible[:, None, None, :], jnp.exp(masked - row_max), 0.0)
    weight_sum = lax.optimization_barrier(jnp.sum(weights, axis=-1))
    rounded = weights.astype(jnp.bfloat16)
    mixed = jnp.einsum('qgjk,kgd->qgjd', rounded.astype(jnp.float32), vals.astype(jnp.float32))
    return (mixed / weight_sum[..., None]).astype(jnp.bfloat16)

def reference(queries, key_rows, value_rows, residual, out_weight, norm_gain, span_map, segments, row_owner):
    wide_count = TOKENS // TOK_DEV
    group_size = QH // KVH
    score_scale = HEAD ** (-0.5)
    shaped_q = queries.reshape(wide_count, TOK_DEV, KVH, group_size, HEAD)
    shaped_k = key_rows.reshape(wide_count, TOK_DEV, KVH, HEAD)
    shaped_v = value_rows.reshape(wide_count, TOK_DEV, KVH, HEAD)
    long_keys = shaped_k[:, :LONG_DEV].reshape(wide_count * LONG_DEV, KVH, HEAD).astype(jnp.float32)
    long_values = shaped_v[:, :LONG_DEV].reshape(wide_count * LONG_DEV, KVH, HEAD).astype(jnp.float32)
    key_index = jnp.arange(wide_count * LONG_DEV, dtype=jnp.int32)
    key_pos = span_map[key_index // LONG_DEV] * LONG_DEV + key_index % LONG_DEV
    short_index = jnp.arange(SHORT_DEV, dtype=jnp.int32)

    def per_block(inputs):
        block, q_long, q_short, k_short, v_short, documents = inputs
        query_pos = span_map[block] * LONG_DEV + jnp.arange(LONG_DEV, dtype=jnp.int32)
        scores = jnp.einsum('qgjd,kgd->qgjk', q_long.astype(jnp.float32), long_keys) * score_scale
        long_out = attend(scores, key_pos[None, :] <= query_pos[:, None], long_values)
        short_scores = jnp.einsum('qgjd,kgd->qgjk', q_short.astype(jnp.float32), k_short.astype(jnp.float32)) * score_scale
        visible = (documents[None, :] == documents[:, None]) & (short_index[None, :] <= short_index[:, None])
        short_out = attend(short_scores, visible, v_short)
        return jnp.concatenate([long_out, short_out], axis=0).reshape(TOK_DEV, QH * HEAD)
    attended = lax.map(per_block, (jnp.arange(wide_count, dtype=jnp.int32), shaped_q[:, :LONG_DEV], shaped_q[:, LONG_DEV:], shaped_k[:, LONG_DEV:], shaped_v[:, LONG_DEV:], segments))
    attended = attended.reshape(TOKENS, QH * HEAD)
    group_cols = QH * HEAD // N_NARROW
    summed = jnp.zeros((TOKENS, D), jnp.float32)
    for lane in range(N_NARROW):
        product = jnp.dot(attended[:, lane * group_cols:(lane + 1) * group_cols], out_weight[lane * group_cols:(lane + 1) * group_cols], preferred_element_type=jnp.float32)
        summed = summed + lax.optimization_barrier(product.astype(jnp.bfloat16)).astype(jnp.float32)
    hidden = (residual.astype(jnp.float32) + summed).astype(jnp.bfloat16)
    widened = hidden.astype(jnp.float32)
    normed = (widened * lax.rsqrt(lax.optimization_barrier(jnp.mean(widened * widened, axis=1, keepdims=True)) + 1e-05) * norm_gain.astype(jnp.float32)).astype(jnp.bfloat16)
    blocks = TOKENS // ROWS_DEV
    owners = row_owner[:, 0]
    chosen = (owners[:, None] == jnp.arange(N_WIDE, dtype=jnp.int32)[None, :]).astype(jnp.int32).reshape(blocks, ROWS_DEV, N_WIDE)
    earlier = jnp.cumsum(chosen, axis=1) - chosen
    slot_index = lax.optimization_barrier(jnp.sum(earlier * chosen, axis=-1)).reshape(TOKENS)
    block_of = jnp.arange(TOKENS, dtype=jnp.int32) // ROWS_DEV
    source = block_of // N_NARROW
    lane_of = block_of % N_NARROW
    ffn_in = jnp.zeros((N_WIDE, N_NARROW, N_WIDE, CAP, D), jnp.bfloat16).at[owners, lane_of, source, slot_index].set(normed)
    return (hidden, ffn_in)
```

```python
import functools

import jax
import jax.numpy as jnp
from jax import lax
from jax.experimental import pallas as pl
from jax.experimental.pallas import tpu as pltpu
from jax.sharding import PartitionSpec as P

HEAD = 128
LONG_DEV = 128


def attend_block(
    partial_state, long_queries, key_block, value_block, key_pos, query_pos, score_scale
):
    running_max, weight_sum, weighted = partial_state
    scores = (
        jnp.einsum("qgjd,kgd->qgjk", long_queries, key_block, preferred_element_type=jnp.float32)
        * score_scale
    )
    visible = (key_pos[None, :] <= query_pos[:, None])[:, None, None, :]
    masked = jnp.where(visible, scores, -1e30)
    newest = jnp.maximum(running_max, jnp.max(masked, axis=-1))
    weights = jnp.where(visible, jnp.exp(masked - newest[..., None]), 0.0)
    factor = jnp.exp(running_max - newest)
    weight_sum = weight_sum * factor + jnp.sum(weights, axis=-1)
    weighted = weighted * factor[..., None] + jnp.einsum(
        "qgjk,kgd->qgjd",
        weights.astype(jnp.bfloat16),
        value_block,
        preferred_element_type=jnp.float32,
    )
    return (newest, weight_sum, weighted)


def rounded_term(attended, out_weight):
    product = jnp.dot(attended, out_weight, preferred_element_type=jnp.float32)
    return lax.optimization_barrier(product.astype(jnp.bfloat16)).astype(jnp.float32)


def general_on_device(
    queries, key_rows, value_rows, residual, out_weight, norm_gain, span_map, segments, row_owner
):
    wide_count = lax.axis_size("wide")
    narrow_count = lax.axis_size("narrow")
    wide_index = lax.axis_index("wide")
    local_heads = queries.shape[1] // HEAD
    local_kv = key_rows.shape[1] // HEAD
    group_size = local_heads // local_kv
    token_count = queries.shape[0]
    short_count = token_count - LONG_DEV
    score_scale = HEAD ** (-0.5)
    own_span = lax.dynamic_slice_in_dim(span_map, wide_index, 1, 0)[0]
    query_pos = own_span * LONG_DEV + jnp.arange(LONG_DEV, dtype=jnp.int32)
    long_queries = queries[:LONG_DEV].reshape(LONG_DEV, local_kv, group_size, HEAD)
    wide_ids = jnp.arange(wide_count, dtype=jnp.int32)
    start_state = (
        jnp.full((LONG_DEV, local_kv, group_size), -1e30, jnp.float32),
        jnp.zeros((LONG_DEV, local_kv, group_size), jnp.float32),
        jnp.zeros((LONG_DEV, local_kv, group_size, HEAD), jnp.float32),
    )
    key_piece = lax.all_gather(key_rows[:LONG_DEV], "wide", axis=0, tiled=True)
    value_piece = lax.all_gather(value_rows[:LONG_DEV], "wide", axis=0, tiled=True)
    row_count = key_piece.shape[0]
    key_index = jnp.arange(row_count, dtype=jnp.int32)
    holder = key_index // LONG_DEV
    span_of = jnp.sum(jnp.where(holder[:, None] == wide_ids[None, :], span_map[None, :], 0), axis=1)
    key_pos = span_of * LONG_DEV + key_index % LONG_DEV
    key_block = key_piece.reshape(row_count, local_kv, HEAD)
    value_block = value_piece.reshape(row_count, local_kv, HEAD)

    def advance(partial_state):
        if row_count > 512 and row_count % 512 == 0:
            splits = row_count // 512

            def advance_block(inner_state, sliced):
                return (
                    attend_block(
                        inner_state,
                        long_queries,
                        sliced[0],
                        sliced[1],
                        sliced[2],
                        query_pos,
                        score_scale,
                    ),
                    None,
                )

            finished, unused = lax.scan(
                advance_block,
                partial_state,
                (
                    key_block.reshape(splits, 512, local_kv, HEAD),
                    value_block.reshape(splits, 512, local_kv, HEAD),
                    key_pos.reshape(splits, 512),
                ),
            )
            return finished
        return attend_block(
            partial_state, long_queries, key_block, value_block, key_pos, query_pos, score_scale
        )

    running_max, weight_sum, weighted = advance(start_state)
    long_out = (
        (weighted / weight_sum[..., None])
        .astype(jnp.bfloat16)
        .reshape(LONG_DEV, local_heads * HEAD)
    )
    short_queries = queries[LONG_DEV:].reshape(short_count, local_kv, group_size, HEAD)
    short_keys = key_rows[LONG_DEV:].reshape(short_count, local_kv, HEAD)
    short_values = value_rows[LONG_DEV:].reshape(short_count, local_kv, HEAD)
    documents = segments[0]
    positions = jnp.arange(short_count, dtype=jnp.int32)
    visible = (
        (documents[None, :] == documents[:, None]) & (positions[None, :] <= positions[:, None])
    )[:, None, None, :]
    scores = (
        jnp.einsum("qgjd,kgd->qgjk", short_queries, short_keys, preferred_element_type=jnp.float32)
        * score_scale
    )
    masked = jnp.where(visible, scores, -1e30)
    row_max = jnp.max(masked, axis=-1, keepdims=True)
    weights = jnp.where(visible, jnp.exp(masked - row_max), 0.0)
    short_sum = jnp.sum(weights, axis=-1)
    mixed = jnp.einsum(
        "qgjk,kgd->qgjd",
        weights.astype(jnp.bfloat16),
        short_values,
        preferred_element_type=jnp.float32,
    )
    short_out = (
        (mixed / short_sum[..., None]).astype(jnp.bfloat16).reshape(short_count, local_heads * HEAD)
    )
    attended = jnp.concatenate([long_out, short_out], axis=0)
    rows_dev = token_count // narrow_count
    sliced = attended
    summed = lax.psum_scatter(
        rounded_term(sliced, out_weight).astype(jnp.bfloat16),
        "narrow",
        scatter_dimension=0,
        tiled=True,
    ).astype(jnp.float32)
    hidden = (residual.astype(jnp.float32) + summed).astype(jnp.bfloat16)
    widened = hidden.astype(jnp.float32)
    normed = (
        widened
        * lax.rsqrt(jnp.mean(widened * widened, axis=1, keepdims=True) + 1e-05)
        * norm_gain.astype(jnp.float32)
    ).astype(jnp.bfloat16)
    capacity = max(2, 2 * rows_dev // wide_count)
    owners = row_owner[:, 0]
    chosen = (owners[:, None] == wide_ids[None, :]).astype(jnp.int32)
    earlier = jnp.cumsum(chosen, axis=0) - chosen
    slot_index = jnp.sum(earlier * chosen, axis=1)
    target = owners * capacity + slot_index
    dispatch = (
        target[None, :] == jnp.arange(wide_count * capacity, dtype=jnp.int32)[:, None]
    ).astype(jnp.bfloat16)
    outgoing = jnp.dot(dispatch, normed, preferred_element_type=jnp.float32).astype(jnp.bfloat16)
    outgoing = outgoing.reshape(wide_count, 1, 1, capacity, normed.shape[1])
    arrived = lax.all_to_all(outgoing, "wide", split_axis=0, concat_axis=2, tiled=True)
    return (hidden, arrived)


PIECES = 8
SENDS = 4
MESH = pl.DeviceIdType.MESH


def attend_heads(q_buf, keys, values, visible, rows, out_buf, lane, local_kv, group_size):
    score_scale = HEAD ** (-0.5)
    count = rows.stop - rows.start
    tiled = jnp.concatenate([visible] * group_size, axis=0)
    for g in range(local_kv):
        heads = [g * group_size + j for j in range(group_size)]
        stacked = jnp.concatenate([q_buf[rows, h * HEAD : (h + 1) * HEAD] for h in heads], axis=0)
        scores = (
            lax.dot_general(
                stacked, keys(g), (((1,), (1,)), ((), ())), preferred_element_type=jnp.float32
            )
            * score_scale
        )
        masked = jnp.where(tiled, scores, -1e30)
        weights = jnp.exp(masked - jnp.max(masked, axis=1, keepdims=True))
        total = jnp.sum(weights, axis=1, keepdims=True)
        mixed = jnp.dot(
            weights.astype(jnp.bfloat16), values(g), preferred_element_type=jnp.float32
        )
        mixed = (mixed / total).astype(jnp.bfloat16)
        for j, h in enumerate(heads):
            out_buf[lane, :, h * HEAD : (h + 1) * HEAD] = mixed[j * count : (j + 1) * count]


def fused_kernel(
    sizes,
    span_ref,
    seg_ref,
    owner_ref,
    q_hbm,
    k_hbm,
    v_hbm,
    res_hbm,
    w_hbm,
    gain_ref,
    hidden_hbm,
    ffn_hbm,
    q_buf,
    ks_buf,
    vs_buf,
    k_buf,
    v_buf,
    w_buf,
    res_buf,
    att_buf,
    part_buf,
    recv_buf,
    hid_buf,
    out_buf,
    in_sem,
    w_sem,
    k_send,
    k_recv,
    v_send,
    v_recv,
    p_send,
    p_recv,
    o_send,
    o_recv,
    own_sem,
    hid_sem,
):
    wide_count, capacity, local_kv, group_size = sizes
    rows, model = res_hbm.shape
    piece = model // PIECES
    span = model // SENDS
    me = lax.axis_index("wide")
    lane = lax.axis_index("narrow")
    other = 1 - lane
    peers = [lax.rem(me + k, wide_count) for k in range(1, wide_count)]
    long_rows, short_rows = slice(0, rows), slice(rows, 2 * rows)

    loads = [
        pltpu.make_async_copy(q_hbm, q_buf, in_sem.at[0]),
        pltpu.make_async_copy(k_hbm.at[pl.ds(rows, rows)], ks_buf, in_sem.at[1]),
        pltpu.make_async_copy(v_hbm.at[pl.ds(rows, rows)], vs_buf, in_sem.at[2]),
    ]
    late_loads = [
        pltpu.make_async_copy(k_hbm.at[pl.ds(0, rows)], k_buf.at[me], in_sem.at[3]),
        pltpu.make_async_copy(v_hbm.at[pl.ds(0, rows)], v_buf.at[me], in_sem.at[4]),
    ]
    res_load = pltpu.make_async_copy(res_hbm, res_buf, in_sem.at[5])
    w_loads = [
        pltpu.make_async_copy(
            w_hbm.at[:, pl.ds(c * piece, piece)], w_buf.at[c], w_sem.at[c]
        )
        for c in range(PIECES)
    ]
    for load in loads + w_loads + [res_load] + late_loads:
        load.start()

    barrier = pltpu.get_barrier_semaphore()
    for peer in peers:
        pl.semaphore_signal(barrier, inc=1, device_id={"wide": peer}, device_id_type=MESH)
    pl.semaphore_signal(barrier, inc=1, device_id={"narrow": other}, device_id_type=MESH)
    pl.semaphore_wait(barrier, wide_count)

    def kv_copy(source, peer):
        return [
            pltpu.make_async_remote_copy(
                src_ref=hbm.at[pl.ds(0, rows)],
                dst_ref=buf.at[source],
                send_sem=send.at[peer],
                recv_sem=recv.at[source],
                device_id={"wide": peer},
                device_id_type=MESH,
            )
            for hbm, buf, send, recv in (
                (k_hbm, k_buf, k_send, k_recv),
                (v_hbm, v_buf, v_send, v_recv),
            )
        ]

    for peer in peers:
        for copy in kv_copy(me, peer):
            copy.start()

    row_id = lax.broadcasted_iota(jnp.int32, (rows, rows), 0)
    col_id = lax.broadcasted_iota(jnp.int32, (rows, rows), 1)

    owner_down = jnp.broadcast_to(owner_ref[...], (rows, rows)).astype(jnp.float32)
    owner_across = owner_down.T
    same = jnp.where((owner_down == owner_across) & (row_id < col_id), 1.0, 0.0)
    slot = jnp.sum(same, axis=0, keepdims=True)
    target = (owner_across[0:1] * capacity + slot).astype(jnp.int32)
    slots = lax.broadcasted_iota(jnp.int32, (wide_count * capacity, rows), 0)
    dispatch = jnp.where(slots == target, 1.0, 0.0).astype(jnp.bfloat16)

    def part_copy(c, phase):
        return pltpu.make_async_remote_copy(
            src_ref=part_buf.at[phase, c],
            dst_ref=recv_buf.at[c],
            send_sem=p_send.at[c],
            recv_sem=p_recv.at[c],
            device_id={"narrow": other},
            device_id_type=MESH,
        )

    def project(phase, first):
        def step(c, carry):
            if first:
                pltpu.make_async_copy(
                    w_hbm.at[:, pl.ds(pl.multiple_of(c * piece, piece), piece)],
                    w_buf.at[c],
                    w_sem.at[c],
                ).wait()
            product = jnp.dot(att_buf[phase], w_buf[c], preferred_element_type=jnp.float32)
            part_buf[phase, c] = product.astype(jnp.bfloat16)

            @pl.when(lane != phase)
            def _():
                part_copy(c, phase).start()

            return carry

        lax.fori_loop(0, PIECES, step, 0)

    def out_copy(c, source, peer):
        return pltpu.make_async_remote_copy(
            src_ref=out_buf.at[c, peer],
            dst_ref=ffn_hbm.at[source, :, pl.ds(pl.multiple_of(c * span, span), span)],
            send_sem=o_send.at[c, peer],
            recv_sem=o_recv.at[c, source],
            device_id={"wide": peer},
            device_id_type=MESH,
        )

    def own_copy(c):
        return pltpu.make_async_copy(
            out_buf.at[c, me],
            ffn_hbm.at[me, :, pl.ds(pl.multiple_of(c * span, span), span)],
            own_sem.at[c],
        )

    hid_copy = pltpu.make_async_copy(hid_buf, hidden_hbm, hid_sem.at[0])

    def finish(phase):
        res_load.wait()

        def add_piece(c, squares):
            part_copy(c, phase).wait_recv()
            cols = pl.ds(pl.multiple_of(c * piece, piece), piece)
            summed = part_buf[phase, c].astype(jnp.float32) + recv_buf[c].astype(jnp.float32)
            hidden = (res_buf[:, cols].astype(jnp.float32) + summed).astype(jnp.bfloat16)
            hid_buf[:, cols] = hidden
            widened = hidden.astype(jnp.float32)
            return squares + jnp.sum(widened * widened, axis=1, keepdims=True)

        squares = lax.fori_loop(0, PIECES, add_piece, jnp.zeros((rows, 1), jnp.float32))
        hid_copy.start()
        factor = lax.rsqrt(squares / model + 1e-05)

        def send_piece(c, carry):
            cols = pl.ds(pl.multiple_of(c * span, span), span)
            normed = (
                hid_buf[:, cols].astype(jnp.float32) * factor * gain_ref[:, cols].astype(jnp.float32)
            ).astype(jnp.bfloat16)
            outgoing = jnp.dot(dispatch, normed, preferred_element_type=jnp.float32)
            out_buf[c] = outgoing.astype(jnp.bfloat16).reshape(wide_count, capacity, span)
            for peer in peers:
                out_copy(c, me, peer).start()
            own_copy(c).start()
            return carry

        lax.fori_loop(0, SENDS, send_piece, 0)

    for load in loads:
        load.wait()
    seg_across = jnp.broadcast_to(seg_ref[...], (rows, rows)).astype(jnp.float32)
    short_visible = (seg_across == seg_across.T) & (col_id <= row_id)
    attend_heads(
        q_buf,
        lambda g: ks_buf[:, g * HEAD : (g + 1) * HEAD],
        lambda g: vs_buf[:, g * HEAD : (g + 1) * HEAD],
        short_visible,
        short_rows,
        att_buf,
        1,
        local_kv,
        group_size,
    )
    project(1, True)

    @pl.when(lane == 1)
    def _():
        finish(1)

    for load in late_loads:
        load.wait()
    for peer in peers:
        for copy in kv_copy(peer, peer):
            copy.wait_recv()
    own_span = span_ref[me]
    long_visible = jnp.concatenate(
        [
            (span_ref[b] * rows + col_id) <= (own_span * rows + row_id)
            for b in range(wide_count)
        ],
        axis=1,
    )
    attend_heads(
        q_buf,
        lambda g: k_buf[:, :, g * HEAD : (g + 1) * HEAD].reshape(wide_count * rows, HEAD),
        lambda g: v_buf[:, :, g * HEAD : (g + 1) * HEAD].reshape(wide_count * rows, HEAD),
        long_visible,
        long_rows,
        att_buf,
        0,
        local_kv,
        group_size,
    )
    project(0, False)

    @pl.when(lane == 0)
    def _():
        finish(0)

    for peer in peers:
        for copy in kv_copy(me, peer):
            copy.wait_send()

    def drain_parts(c, carry):
        part_copy(c, 0).wait_send()
        return carry

    lax.fori_loop(0, PIECES, drain_parts, 0)

    def drain_sends(c, carry):
        for peer in peers:
            out_copy(c, me, peer).wait_send()
            out_copy(c, peer, peer).wait_recv()
        own_copy(c).wait()
        return carry

    lax.fori_loop(0, SENDS, drain_sends, 0)
    hid_copy.wait()


def fused_on_device(
    queries, key_rows, value_rows, residual, out_weight, norm_gain, span_map, segments, row_owner
):
    wide_count = lax.axis_size("wide")
    local_heads = queries.shape[1] // HEAD
    local_kv = key_rows.shape[1] // HEAD
    rows, model = residual.shape
    capacity = max(2, 2 * rows // wide_count)
    sizes = (wide_count, capacity, local_kv, local_heads // local_kv)
    bf16 = jnp.bfloat16
    dma = pltpu.SemaphoreType.DMA
    any_spec = pl.BlockSpec(memory_space=pl.ANY)
    vmem_spec = pl.BlockSpec(memory_space=pltpu.VMEM)
    piece, span = model // PIECES, model // SENDS
    hidden, arrived = pl.pallas_call(
        functools.partial(fused_kernel, sizes),
        out_shape=(
            jax.ShapeDtypeStruct((rows, model), bf16),
            jax.ShapeDtypeStruct((wide_count, capacity, model), bf16),
        ),
        in_specs=[pl.BlockSpec(memory_space=pltpu.SMEM), vmem_spec, vmem_spec]
        + [any_spec] * 5
        + [vmem_spec],
        out_specs=(any_spec, any_spec),
        scratch_shapes=[
            pltpu.VMEM(queries.shape, bf16),
            pltpu.VMEM((rows, key_rows.shape[1]), bf16),
            pltpu.VMEM((rows, key_rows.shape[1]), bf16),
            pltpu.VMEM((wide_count, rows, key_rows.shape[1]), bf16),
            pltpu.VMEM((wide_count, rows, key_rows.shape[1]), bf16),
            pltpu.VMEM((PIECES, out_weight.shape[0], piece), bf16),
            pltpu.VMEM((rows, model), bf16),
            pltpu.VMEM((2, rows, queries.shape[1]), bf16),
            pltpu.VMEM((2, PIECES, rows, piece), bf16),
            pltpu.VMEM((PIECES, rows, piece), bf16),
            pltpu.VMEM((rows, model), bf16),
            pltpu.VMEM((SENDS, wide_count, capacity, span), bf16),
            dma((6,)),
            dma((PIECES,)),
            dma((wide_count,)),
            dma((wide_count,)),
            dma((wide_count,)),
            dma((wide_count,)),
            dma((PIECES,)),
            dma((PIECES,)),
            dma((SENDS, wide_count)),
            dma((SENDS, wide_count)),
            dma((SENDS,)),
            dma((1,)),
        ],
        compiler_params=pltpu.CompilerParams(
            collective_id=0, has_side_effects=True, vmem_limit_bytes=56 * 1024 * 1024
        ),
    )(
        span_map,
        segments,
        row_owner,
        queries,
        key_rows,
        value_rows,
        residual,
        out_weight,
        norm_gain.reshape(1, model),
    )
    return hidden, arrived.reshape(1, 1, wide_count, capacity, model)


def on_device(*args):
    queries, residual = args[0], args[3]
    rows, model = residual.shape
    wide_count = lax.axis_size("wide")
    fits = (
        lax.axis_size("narrow") == 2
        and rows == LONG_DEV
        and queries.shape[0] == 2 * LONG_DEV
        and (2 * rows) % (16 * wide_count) == 0
        and model % (PIECES * HEAD) == 0
    )
    return (fused_on_device if fits else general_on_device)(*args)


def solution(mesh):
    placed = (
        P(("rep", "wide"), "narrow"),
        P(("rep", "wide"), "narrow"),
        P(("rep", "wide"), "narrow"),
        P(("rep", "wide", "narrow"), None),
        P("narrow", None),
        P(),
        P(),
        P(("rep", "wide"), None),
        P(("rep", "wide", "narrow"), None),
    )
    return jax.shard_map(
        on_device,
        mesh=mesh,
        in_specs=placed,
        out_specs=(
            P(("rep", "wide", "narrow"), None),
            P(("rep", "wide"), "narrow", None, None, None),
        ),
        check_vma=False,
    )
```

```python
import functools

import jax
import jax.numpy as jnp
from jax import lax
from jax.experimental import pallas as pl
from jax.experimental.pallas import tpu as pltpu
from jax.sharding import PartitionSpec as P

HEAD = 128
LONG_DEV = 128


def attend_block(
    partial_state, long_queries, key_block, value_block, key_pos, query_pos, score_scale
):
    running_max, weight_sum, weighted = partial_state
    scores = (
        jnp.einsum("qgjd,kgd->qgjk", long_queries, key_block, preferred_element_type=jnp.float32)
        * score_scale
    )
    visible = (key_pos[None, :] <= query_pos[:, None])[:, None, None, :]
    masked = jnp.where(visible, scores, -1e30)
    newest = jnp.maximum(running_max, jnp.max(masked, axis=-1))
    weights = jnp.where(visible, jnp.exp(masked - newest[..., None]), 0.0)
    factor = jnp.exp(running_max - newest)
    weight_sum = weight_sum * factor + jnp.sum(weights, axis=-1)
    weighted = weighted * factor[..., None] + jnp.einsum(
        "qgjk,kgd->qgjd",
        weights.astype(jnp.bfloat16),
        value_block,
        preferred_element_type=jnp.float32,
    )
    return (newest, weight_sum, weighted)


def rounded_term(attended, out_weight):
    product = jnp.dot(attended, out_weight, preferred_element_type=jnp.float32)
    return lax.optimization_barrier(product.astype(jnp.bfloat16)).astype(jnp.float32)


def general_on_device(
    queries, key_rows, value_rows, residual, out_weight, norm_gain, span_map, segments, row_owner
):
    wide_count = lax.axis_size("wide")
    narrow_count = lax.axis_size("narrow")
    wide_index = lax.axis_index("wide")
    local_heads = queries.shape[1] // HEAD
    local_kv = key_rows.shape[1] // HEAD
    group_size = local_heads // local_kv
    token_count = queries.shape[0]
    short_count = token_count - LONG_DEV
    score_scale = HEAD ** (-0.5)
    own_span = lax.dynamic_slice_in_dim(span_map, wide_index, 1, 0)[0]
    query_pos = own_span * LONG_DEV + jnp.arange(LONG_DEV, dtype=jnp.int32)
    long_queries = queries[:LONG_DEV].reshape(LONG_DEV, local_kv, group_size, HEAD)
    wide_ids = jnp.arange(wide_count, dtype=jnp.int32)
    start_state = (
        jnp.full((LONG_DEV, local_kv, group_size), -1e30, jnp.float32),
        jnp.zeros((LONG_DEV, local_kv, group_size), jnp.float32),
        jnp.zeros((LONG_DEV, local_kv, group_size, HEAD), jnp.float32),
    )
    key_piece = lax.all_gather(key_rows[:LONG_DEV], "wide", axis=0, tiled=True)
    value_piece = lax.all_gather(value_rows[:LONG_DEV], "wide", axis=0, tiled=True)
    row_count = key_piece.shape[0]
    key_index = jnp.arange(row_count, dtype=jnp.int32)
    holder = key_index // LONG_DEV
    span_of = jnp.sum(jnp.where(holder[:, None] == wide_ids[None, :], span_map[None, :], 0), axis=1)
    key_pos = span_of * LONG_DEV + key_index % LONG_DEV
    key_block = key_piece.reshape(row_count, local_kv, HEAD)
    value_block = value_piece.reshape(row_count, local_kv, HEAD)

    def advance(partial_state):
        if row_count > 512 and row_count % 512 == 0:
            splits = row_count // 512

            def advance_block(inner_state, sliced):
                return (
                    attend_block(
                        inner_state,
                        long_queries,
                        sliced[0],
                        sliced[1],
                        sliced[2],
                        query_pos,
                        score_scale,
                    ),
                    None,
                )

            finished, unused = lax.scan(
                advance_block,
                partial_state,
                (
                    key_block.reshape(splits, 512, local_kv, HEAD),
                    value_block.reshape(splits, 512, local_kv, HEAD),
                    key_pos.reshape(splits, 512),
                ),
            )
            return finished
        return attend_block(
            partial_state, long_queries, key_block, value_block, key_pos, query_pos, score_scale
        )

    running_max, weight_sum, weighted = advance(start_state)
    long_out = (
        (weighted / weight_sum[..., None])
        .astype(jnp.bfloat16)
        .reshape(LONG_DEV, local_heads * HEAD)
    )
    short_queries = queries[LONG_DEV:].reshape(short_count, local_kv, group_size, HEAD)
    short_keys = key_rows[LONG_DEV:].reshape(short_count, local_kv, HEAD)
    short_values = value_rows[LONG_DEV:].reshape(short_count, local_kv, HEAD)
    documents = segments[0]
    positions = jnp.arange(short_count, dtype=jnp.int32)
    visible = (
        (documents[None, :] == documents[:, None]) & (positions[None, :] <= positions[:, None])
    )[:, None, None, :]
    scores = (
        jnp.einsum("qgjd,kgd->qgjk", short_queries, short_keys, preferred_element_type=jnp.float32)
        * score_scale
    )
    masked = jnp.where(visible, scores, -1e30)
    row_max = jnp.max(masked, axis=-1, keepdims=True)
    weights = jnp.where(visible, jnp.exp(masked - row_max), 0.0)
    short_sum = jnp.sum(weights, axis=-1)
    mixed = jnp.einsum(
        "qgjk,kgd->qgjd",
        weights.astype(jnp.bfloat16),
        short_values,
        preferred_element_type=jnp.float32,
    )
    short_out = (
        (mixed / short_sum[..., None]).astype(jnp.bfloat16).reshape(short_count, local_heads * HEAD)
    )
    attended = jnp.concatenate([long_out, short_out], axis=0)
    rows_dev = token_count // narrow_count
    sliced = attended
    summed = lax.psum_scatter(
        rounded_term(sliced, out_weight).astype(jnp.bfloat16),
        "narrow",
        scatter_dimension=0,
        tiled=True,
    ).astype(jnp.float32)
    hidden = (residual.astype(jnp.float32) + summed).astype(jnp.bfloat16)
    widened = hidden.astype(jnp.float32)
    normed = (
        widened
        * lax.rsqrt(jnp.mean(widened * widened, axis=1, keepdims=True) + 1e-05)
        * norm_gain.astype(jnp.float32)
    ).astype(jnp.bfloat16)
    capacity = max(2, 2 * rows_dev // wide_count)
    owners = row_owner[:, 0]
    chosen = (owners[:, None] == wide_ids[None, :]).astype(jnp.int32)
    earlier = jnp.cumsum(chosen, axis=0) - chosen
    slot_index = jnp.sum(earlier * chosen, axis=1)
    target = owners * capacity + slot_index
    dispatch = (
        target[None, :] == jnp.arange(wide_count * capacity, dtype=jnp.int32)[:, None]
    ).astype(jnp.bfloat16)
    outgoing = jnp.dot(dispatch, normed, preferred_element_type=jnp.float32).astype(jnp.bfloat16)
    outgoing = outgoing.reshape(wide_count, 1, 1, capacity, normed.shape[1])
    arrived = lax.all_to_all(outgoing, "wide", split_axis=0, concat_axis=2, tiled=True)
    return (hidden, arrived)


PIECES = 8
SENDS = 4
MESH = pl.DeviceIdType.MESH


def attend_heads(q_buf, keys, values, visible, rows, out_buf, lane, local_kv, group_size):
    score_scale = HEAD ** (-0.5)
    count = rows.stop - rows.start
    tiled = jnp.concatenate([visible] * group_size, axis=0)
    for g in range(local_kv):
        heads = [g * group_size + j for j in range(group_size)]
        stacked = jnp.concatenate([q_buf[rows, h * HEAD : (h + 1) * HEAD] for h in heads], axis=0)
        scores = (
            lax.dot_general(
                stacked, keys(g), (((1,), (1,)), ((), ())), preferred_element_type=jnp.float32
            )
            * score_scale
        )
        masked = jnp.where(tiled, scores, -1e30)
        weights = jnp.exp(masked - jnp.max(masked, axis=1, keepdims=True))
        total = jnp.sum(weights, axis=1, keepdims=True)
        mixed = jnp.dot(
            weights.astype(jnp.bfloat16), values(g), preferred_element_type=jnp.float32
        )
        mixed = (mixed / total).astype(jnp.bfloat16)
        for j, h in enumerate(heads):
            out_buf[lane, :, h * HEAD : (h + 1) * HEAD] = mixed[j * count : (j + 1) * count]


def fused_kernel(
    sizes,
    span_ref,
    seg_ref,
    owner_ref,
    q_hbm,
    k_hbm,
    v_hbm,
    res_hbm,
    w_hbm,
    gain_ref,
    hidden_ref,
    ffn_ref,
    q_buf,
    ks_buf,
    vs_buf,
    k_buf,
    v_buf,
    w_buf,
    res_buf,
    att_buf,
    part_buf,
    recv_buf,
    out_buf,
    in_sem,
    w_sem,
    k_send,
    k_recv,
    v_send,
    v_recv,
    p_send,
    p_recv,
    o_send,
    o_recv,
    own_sem,
):
    wide_count, capacity, local_kv, group_size = sizes
    rows, model = res_hbm.shape
    piece = model // PIECES
    span = model // SENDS
    me = lax.axis_index("wide")
    lane = lax.axis_index("narrow")
    other = 1 - lane
    peers = [lax.rem(me + k, wide_count) for k in range(1, wide_count)]
    long_rows, short_rows = slice(0, rows), slice(rows, 2 * rows)

    loads = [
        pltpu.make_async_copy(q_hbm, q_buf, in_sem.at[0]),
        pltpu.make_async_copy(k_hbm.at[pl.ds(rows, rows)], ks_buf, in_sem.at[1]),
        pltpu.make_async_copy(v_hbm.at[pl.ds(rows, rows)], vs_buf, in_sem.at[2]),
    ]
    late_loads = [
        pltpu.make_async_copy(k_hbm.at[pl.ds(0, rows)], k_buf.at[me], in_sem.at[3]),
        pltpu.make_async_copy(v_hbm.at[pl.ds(0, rows)], v_buf.at[me], in_sem.at[4]),
    ]
    res_load = pltpu.make_async_copy(res_hbm, res_buf, in_sem.at[5])
    w_loads = [
        pltpu.make_async_copy(
            w_hbm.at[:, pl.ds(c * piece, piece)], w_buf.at[c], w_sem.at[c]
        )
        for c in range(PIECES)
    ]
    for load in loads + w_loads + [res_load] + late_loads:
        load.start()

    barrier = pltpu.get_barrier_semaphore()
    for peer in peers:
        pl.semaphore_signal(barrier, inc=1, device_id={"wide": peer}, device_id_type=MESH)
    pl.semaphore_signal(barrier, inc=1, device_id={"narrow": other}, device_id_type=MESH)
    pl.semaphore_wait(barrier, wide_count)

    def kv_copy(source, peer):
        return [
            pltpu.make_async_remote_copy(
                src_ref=hbm.at[pl.ds(0, rows)],
                dst_ref=buf.at[source],
                send_sem=send.at[peer],
                recv_sem=recv.at[source],
                device_id={"wide": peer},
                device_id_type=MESH,
            )
            for hbm, buf, send, recv in (
                (k_hbm, k_buf, k_send, k_recv),
                (v_hbm, v_buf, v_send, v_recv),
            )
        ]

    for peer in peers:
        for copy in kv_copy(me, peer):
            copy.start()

    row_id = lax.broadcasted_iota(jnp.int32, (rows, rows), 0)
    col_id = lax.broadcasted_iota(jnp.int32, (rows, rows), 1)

    owner_across = jnp.broadcast_to(owner_ref[...], (rows, rows)).astype(jnp.float32)
    owner_down = owner_across.T
    same = jnp.where((owner_down == owner_across) & (row_id < col_id), 1.0, 0.0)
    slot = jnp.sum(same, axis=0, keepdims=True)
    target = (owner_across[0:1] * capacity + slot).astype(jnp.int32)
    slots = lax.broadcasted_iota(jnp.int32, (wide_count * capacity, rows), 0)
    dispatch = jnp.where(slots == target, 1.0, 0.0).astype(jnp.bfloat16)

    def part_copy(c, phase):
        return pltpu.make_async_remote_copy(
            src_ref=part_buf.at[phase, c],
            dst_ref=recv_buf.at[c],
            send_sem=p_send.at[c],
            recv_sem=p_recv.at[c],
            device_id={"narrow": other},
            device_id_type=MESH,
        )

    def project(phase, c):
        if phase == 1:
            w_loads[c].wait()
        product = jnp.dot(att_buf[phase], w_buf[c], preferred_element_type=jnp.float32)
        part_buf[phase, c] = product.astype(jnp.bfloat16)

    def lend(phase):
        for c in range(PIECES):
            project(phase, c)
            part_copy(c, phase).start()

    def out_copy(c, source, peer):
        return pltpu.make_async_remote_copy(
            src_ref=out_buf.at[c, peer],
            dst_ref=ffn_ref.at[source, :, pl.ds(c * span, span)],
            send_sem=o_send.at[c, peer],
            recv_sem=o_recv.at[c, source],
            device_id={"wide": peer},
            device_id_type=MESH,
        )

    def own_copy(c):
        return pltpu.make_async_copy(
            out_buf.at[c, me],
            ffn_ref.at[me, :, pl.ds(c * span, span)],
            own_sem.at[c],
        )

    def finish(phase):
        res_load.wait()
        squares = jnp.zeros((rows, 1), jnp.float32)
        for step in range(PIECES + 1):
            if step < PIECES:
                project(phase, step)
            if step == 0:
                continue
            c = step - 1
            part_copy(c, phase).wait_recv()
            cols = slice(c * piece, (c + 1) * piece)
            summed = part_buf[phase, c].astype(jnp.float32) + recv_buf[c].astype(jnp.float32)
            hidden = (res_buf[:, cols].astype(jnp.float32) + summed).astype(jnp.bfloat16)
            hidden_ref[:, cols] = hidden
            widened = hidden.astype(jnp.float32)
            squares += jnp.sum(widened * widened, axis=1, keepdims=True)
        factor = lax.rsqrt(squares / model + 1e-05)
        lines = span // HEAD
        for c in range(SENDS):
            cols = slice(c * span, (c + 1) * span)
            gains = gain_ref[c * lines : (c + 1) * lines, :].astype(jnp.float32)
            gain = jnp.concatenate([gains[i : i + 1] for i in range(lines)], axis=1)
            normed = (hidden_ref[:, cols].astype(jnp.float32) * factor * gain).astype(jnp.bfloat16)
            outgoing = jnp.dot(dispatch, normed, preferred_element_type=jnp.float32)
            out_buf[c] = outgoing.astype(jnp.bfloat16).reshape(wide_count, capacity, span)
            for peer in peers:
                out_copy(c, me, peer).start()
            own_copy(c).start()

    def both(phase):
        @pl.when(lane == phase)
        def _():
            finish(phase)

        @pl.when(lane != phase)
        def _():
            lend(phase)

    for load in loads:
        load.wait()
    seg_across = jnp.broadcast_to(seg_ref[...], (rows, rows)).astype(jnp.float32)
    short_visible = (seg_across == seg_across.T) & (col_id <= row_id)
    attend_heads(
        q_buf,
        lambda g: ks_buf[:, g * HEAD : (g + 1) * HEAD],
        lambda g: vs_buf[:, g * HEAD : (g + 1) * HEAD],
        short_visible,
        short_rows,
        att_buf,
        1,
        local_kv,
        group_size,
    )
    both(1)

    for load in late_loads:
        load.wait()
    for peer in peers:
        for copy in kv_copy(peer, peer):
            copy.wait_recv()
    own_span = span_ref[me]
    long_visible = jnp.concatenate(
        [
            (span_ref[b] * rows + col_id) <= (own_span * rows + row_id)
            for b in range(wide_count)
        ],
        axis=1,
    )
    attend_heads(
        q_buf,
        lambda g: k_buf[:, :, g * HEAD : (g + 1) * HEAD].reshape(wide_count * rows, HEAD),
        lambda g: v_buf[:, :, g * HEAD : (g + 1) * HEAD].reshape(wide_count * rows, HEAD),
        long_visible,
        long_rows,
        att_buf,
        0,
        local_kv,
        group_size,
    )
    both(0)

    for peer in peers:
        for copy in kv_copy(me, peer):
            copy.wait_send()

    for c in range(PIECES):
        part_copy(c, 0).wait_send()
    for c in range(SENDS):
        for peer in peers:
            out_copy(c, me, peer).wait_send()
            out_copy(c, peer, peer).wait_recv()
        own_copy(c).wait()


def store_kernel(hidden_ref, ffn_ref, hidden_out, ffn_out, sems):
    copies = [pltpu.make_async_copy(hidden_ref, hidden_out, sems.at[0])]
    for s in range(ffn_ref.shape[0]):
        copies.append(pltpu.make_async_copy(ffn_ref.at[s], ffn_out.at[s], sems.at[1 + s]))
    for copy in copies:
        copy.start()
    for copy in copies:
        copy.wait()


def fused_on_device(
    queries, key_rows, value_rows, residual, out_weight, norm_gain, span_map, segments, row_owner
):
    wide_count = lax.axis_size("wide")
    local_heads = queries.shape[1] // HEAD
    local_kv = key_rows.shape[1] // HEAD
    rows, model = residual.shape
    capacity = max(2, 2 * rows // wide_count)
    sizes = (wide_count, capacity, local_kv, local_heads // local_kv)
    bf16 = jnp.bfloat16
    dma = pltpu.SemaphoreType.DMA
    any_spec = pl.BlockSpec(memory_space=pl.ANY)
    vmem_spec = pl.BlockSpec(memory_space=pltpu.VMEM)
    piece, span = model // PIECES, model // SENDS
    hidden, arrived = pl.pallas_call(
        functools.partial(fused_kernel, sizes),
        out_shape=(
            pltpu.VMEM((rows, model), bf16),
            pltpu.VMEM((wide_count, capacity, model), bf16),
        ),
        in_specs=[pl.BlockSpec(memory_space=pltpu.SMEM), vmem_spec, vmem_spec]
        + [any_spec] * 5
        + [vmem_spec],
        out_specs=(vmem_spec, vmem_spec),
        scratch_shapes=[
            pltpu.VMEM(queries.shape, bf16),
            pltpu.VMEM((rows, key_rows.shape[1]), bf16),
            pltpu.VMEM((rows, key_rows.shape[1]), bf16),
            pltpu.VMEM((wide_count, rows, key_rows.shape[1]), bf16),
            pltpu.VMEM((wide_count, rows, key_rows.shape[1]), bf16),
            pltpu.VMEM((PIECES, out_weight.shape[0], piece), bf16),
            pltpu.VMEM((rows, model), bf16),
            pltpu.VMEM((2, rows, queries.shape[1]), bf16),
            pltpu.VMEM((2, PIECES, rows, piece), bf16),
            pltpu.VMEM((PIECES, rows, piece), bf16),
            pltpu.VMEM((SENDS, wide_count, capacity, span), bf16),
            dma((6,)),
            dma((PIECES,)),
            dma((wide_count,)),
            dma((wide_count,)),
            dma((wide_count,)),
            dma((wide_count,)),
            dma((PIECES,)),
            dma((PIECES,)),
            dma((SENDS, wide_count)),
            dma((SENDS, wide_count)),
            dma((SENDS,)),
        ],
        compiler_params=pltpu.CompilerParams(
            collective_id=0, has_side_effects=True, vmem_limit_bytes=60 * 1024 * 1024
        ),
    )(
        span_map,
        segments,
        row_owner.reshape(1, rows),
        queries,
        key_rows,
        value_rows,
        residual,
        out_weight,
        norm_gain.reshape(model // HEAD, HEAD),
    )
    hidden, arrived = pl.pallas_call(
        store_kernel,
        out_shape=(
            jax.ShapeDtypeStruct(hidden.shape, bf16),
            jax.ShapeDtypeStruct(arrived.shape, bf16),
        ),
        in_specs=[any_spec] * 2,
        out_specs=(any_spec, any_spec),
        scratch_shapes=[dma((1 + wide_count,))],
    )(hidden, arrived)
    return hidden, arrived.reshape(1, 1, wide_count, capacity, model)


def on_device(*args):
    queries, residual = args[0], args[3]
    rows, model = residual.shape
    wide_count = lax.axis_size("wide")
    fits = (
        lax.axis_size("narrow") == 2
        and rows == LONG_DEV
        and queries.shape[0] == 2 * LONG_DEV
        and (2 * rows) % (16 * wide_count) == 0
        and model % (PIECES * HEAD) == 0
    )
    return (fused_on_device if fits else general_on_device)(*args)


def solution(mesh):
    placed = (
        P(("rep", "wide"), "narrow"),
        P(("rep", "wide"), "narrow"),
        P(("rep", "wide"), "narrow"),
        P(("rep", "wide", "narrow"), None),
        P("narrow", None),
        P(),
        P(),
        P(("rep", "wide"), None),
        P(("rep", "wide", "narrow"), None),
    )
    return jax.shard_map(
        on_device,
        mesh=mesh,
        in_specs=placed,
        out_specs=(
            P(("rep", "wide", "narrow"), None),
            P(("rep", "wide"), "narrow", None, None, None),
        ),
        check_vma=False,
    )
```

```python
import functools

import jax
import jax.numpy as jnp
from jax import lax
from jax.experimental import pallas as pl
from jax.experimental.pallas import tpu as pltpu
from jax.sharding import PartitionSpec as P

HEAD = 128
LONG_DEV = 128


def attend_block(
    partial_state, long_queries, key_block, value_block, key_pos, query_pos, score_scale
):
    running_max, weight_sum, weighted = partial_state
    scores = (
        jnp.einsum("qgjd,kgd->qgjk", long_queries, key_block, preferred_element_type=jnp.float32)
        * score_scale
    )
    visible = (key_pos[None, :] <= query_pos[:, None])[:, None, None, :]
    masked = jnp.where(visible, scores, -1e30)
    newest = jnp.maximum(running_max, jnp.max(masked, axis=-1))
    weights = jnp.where(visible, jnp.exp(masked - newest[..., None]), 0.0)
    factor = jnp.exp(running_max - newest)
    weight_sum = weight_sum * factor + jnp.sum(weights, axis=-1)
    weighted = weighted * factor[..., None] + jnp.einsum(
        "qgjk,kgd->qgjd",
        weights.astype(jnp.bfloat16),
        value_block,
        preferred_element_type=jnp.float32,
    )
    return (newest, weight_sum, weighted)


def rounded_term(attended, out_weight):
    product = jnp.dot(attended, out_weight, preferred_element_type=jnp.float32)
    return lax.optimization_barrier(product.astype(jnp.bfloat16)).astype(jnp.float32)


def general_on_device(
    queries, key_rows, value_rows, residual, out_weight, norm_gain, span_map, segments, row_owner
):
    wide_count = lax.axis_size("wide")
    narrow_count = lax.axis_size("narrow")
    wide_index = lax.axis_index("wide")
    local_heads = queries.shape[1] // HEAD
    local_kv = key_rows.shape[1] // HEAD
    group_size = local_heads // local_kv
    token_count = queries.shape[0]
    short_count = token_count - LONG_DEV
    score_scale = HEAD ** (-0.5)
    own_span = lax.dynamic_slice_in_dim(span_map, wide_index, 1, 0)[0]
    query_pos = own_span * LONG_DEV + jnp.arange(LONG_DEV, dtype=jnp.int32)
    long_queries = queries[:LONG_DEV].reshape(LONG_DEV, local_kv, group_size, HEAD)
    wide_ids = jnp.arange(wide_count, dtype=jnp.int32)
    start_state = (
        jnp.full((LONG_DEV, local_kv, group_size), -1e30, jnp.float32),
        jnp.zeros((LONG_DEV, local_kv, group_size), jnp.float32),
        jnp.zeros((LONG_DEV, local_kv, group_size, HEAD), jnp.float32),
    )
    key_piece = lax.all_gather(key_rows[:LONG_DEV], "wide", axis=0, tiled=True)
    value_piece = lax.all_gather(value_rows[:LONG_DEV], "wide", axis=0, tiled=True)
    row_count = key_piece.shape[0]
    key_index = jnp.arange(row_count, dtype=jnp.int32)
    holder = key_index // LONG_DEV
    span_of = jnp.sum(jnp.where(holder[:, None] == wide_ids[None, :], span_map[None, :], 0), axis=1)
    key_pos = span_of * LONG_DEV + key_index % LONG_DEV
    key_block = key_piece.reshape(row_count, local_kv, HEAD)
    value_block = value_piece.reshape(row_count, local_kv, HEAD)

    def advance(partial_state):
        if row_count > 512 and row_count % 512 == 0:
            splits = row_count // 512

            def advance_block(inner_state, sliced):
                return (
                    attend_block(
                        inner_state,
                        long_queries,
                        sliced[0],
                        sliced[1],
                        sliced[2],
                        query_pos,
                        score_scale,
                    ),
                    None,
                )

            finished, unused = lax.scan(
                advance_block,
                partial_state,
                (
                    key_block.reshape(splits, 512, local_kv, HEAD),
                    value_block.reshape(splits, 512, local_kv, HEAD),
                    key_pos.reshape(splits, 512),
                ),
            )
            return finished
        return attend_block(
            partial_state, long_queries, key_block, value_block, key_pos, query_pos, score_scale
        )

    running_max, weight_sum, weighted = advance(start_state)
    long_out = (
        (weighted / weight_sum[..., None])
        .astype(jnp.bfloat16)
        .reshape(LONG_DEV, local_heads * HEAD)
    )
    short_queries = queries[LONG_DEV:].reshape(short_count, local_kv, group_size, HEAD)
    short_keys = key_rows[LONG_DEV:].reshape(short_count, local_kv, HEAD)
    short_values = value_rows[LONG_DEV:].reshape(short_count, local_kv, HEAD)
    documents = segments[0]
    positions = jnp.arange(short_count, dtype=jnp.int32)
    visible = (
        (documents[None, :] == documents[:, None]) & (positions[None, :] <= positions[:, None])
    )[:, None, None, :]
    scores = (
        jnp.einsum("qgjd,kgd->qgjk", short_queries, short_keys, preferred_element_type=jnp.float32)
        * score_scale
    )
    masked = jnp.where(visible, scores, -1e30)
    row_max = jnp.max(masked, axis=-1, keepdims=True)
    weights = jnp.where(visible, jnp.exp(masked - row_max), 0.0)
    short_sum = jnp.sum(weights, axis=-1)
    mixed = jnp.einsum(
        "qgjk,kgd->qgjd",
        weights.astype(jnp.bfloat16),
        short_values,
        preferred_element_type=jnp.float32,
    )
    short_out = (
        (mixed / short_sum[..., None]).astype(jnp.bfloat16).reshape(short_count, local_heads * HEAD)
    )
    attended = jnp.concatenate([long_out, short_out], axis=0)
    rows_dev = token_count // narrow_count
    sliced = attended
    summed = lax.psum_scatter(
        rounded_term(sliced, out_weight).astype(jnp.bfloat16),
        "narrow",
        scatter_dimension=0,
        tiled=True,
    ).astype(jnp.float32)
    hidden = (residual.astype(jnp.float32) + summed).astype(jnp.bfloat16)
    widened = hidden.astype(jnp.float32)
    normed = (
        widened
        * lax.rsqrt(jnp.mean(widened * widened, axis=1, keepdims=True) + 1e-05)
        * norm_gain.astype(jnp.float32)
    ).astype(jnp.bfloat16)
    capacity = max(2, 2 * rows_dev // wide_count)
    owners = row_owner[:, 0]
    chosen = (owners[:, None] == wide_ids[None, :]).astype(jnp.int32)
    earlier = jnp.cumsum(chosen, axis=0) - chosen
    slot_index = jnp.sum(earlier * chosen, axis=1)
    target = owners * capacity + slot_index
    dispatch = (
        target[None, :] == jnp.arange(wide_count * capacity, dtype=jnp.int32)[:, None]
    ).astype(jnp.bfloat16)
    outgoing = jnp.dot(dispatch, normed, preferred_element_type=jnp.float32).astype(jnp.bfloat16)
    outgoing = outgoing.reshape(wide_count, 1, 1, capacity, normed.shape[1])
    arrived = lax.all_to_all(outgoing, "wide", split_axis=0, concat_axis=2, tiled=True)
    return (hidden, arrived)


PIECES = 8
SENDS = 4
MESH = pl.DeviceIdType.MESH


def attend_heads(q_buf, keys, values, visible, rows, out_buf, lane, local_kv, group_size):
    score_scale = HEAD ** (-0.5)
    count = rows.stop - rows.start
    tiled = jnp.concatenate([visible] * group_size, axis=0)

    def attend_group(g, carry):
        heads = [
            pl.ds(pl.multiple_of((g * group_size + j) * HEAD, HEAD), HEAD) for j in range(group_size)
        ]
        group = pl.ds(pl.multiple_of(g * HEAD, HEAD), HEAD)
        stacked = jnp.concatenate([q_buf[rows, h] for h in heads], axis=0)
        scores = (
            lax.dot_general(
                stacked, keys(group), (((1,), (1,)), ((), ())), preferred_element_type=jnp.float32
            )
            * score_scale
        )
        masked = jnp.where(tiled, scores, -1e30)
        weights = jnp.exp(masked - jnp.max(masked, axis=1, keepdims=True))
        total = jnp.sum(weights, axis=1, keepdims=True)
        mixed = jnp.dot(
            weights.astype(jnp.bfloat16), values(group), preferred_element_type=jnp.float32
        )
        mixed = (mixed / total).astype(jnp.bfloat16)
        for j, h in enumerate(heads):
            out_buf[lane, :, h] = mixed[j * count : (j + 1) * count]
        return carry

    lax.fori_loop(0, local_kv, attend_group, 0)


def fused_kernel(
    sizes,
    span_ref,
    seg_ref,
    owner_ref,
    q_hbm,
    k_hbm,
    v_hbm,
    res_hbm,
    w_hbm,
    gain_ref,
    hidden_ref,
    ffn_ref,
    q_buf,
    ks_buf,
    vs_buf,
    k_buf,
    v_buf,
    w_buf,
    res_buf,
    att_buf,
    part_buf,
    recv_buf,
    out_buf,
    gain_buf,
    in_sem,
    w_sem,
    k_send,
    k_recv,
    v_send,
    v_recv,
    p_send,
    p_recv,
    o_send,
    o_recv,
    own_sem,
):
    wide_count, capacity, local_kv, group_size = sizes
    rows, model = res_hbm.shape
    piece = model // PIECES
    span = model // SENDS
    me = lax.axis_index("wide")
    lane = lax.axis_index("narrow")
    other = 1 - lane
    peers = [lax.rem(me + k, wide_count) for k in range(1, wide_count)]
    long_rows, short_rows = slice(0, rows), slice(rows, 2 * rows)

    loads = [
        pltpu.make_async_copy(q_hbm, q_buf, in_sem.at[0]),
        pltpu.make_async_copy(k_hbm.at[pl.ds(rows, rows)], ks_buf, in_sem.at[1]),
        pltpu.make_async_copy(v_hbm.at[pl.ds(rows, rows)], vs_buf, in_sem.at[2]),
    ]
    late_loads = [
        pltpu.make_async_copy(k_hbm.at[pl.ds(0, rows)], k_buf.at[me], in_sem.at[3]),
        pltpu.make_async_copy(v_hbm.at[pl.ds(0, rows)], v_buf.at[me], in_sem.at[4]),
    ]
    res_load = pltpu.make_async_copy(res_hbm, res_buf, in_sem.at[5])
    w_loads = [
        pltpu.make_async_copy(
            w_hbm.at[:, pl.ds(c * piece, piece)], w_buf.at[c], w_sem.at[c]
        )
        for c in range(PIECES)
    ]
    for load in loads + w_loads + [res_load] + late_loads:
        load.start()

    barrier = pltpu.get_barrier_semaphore()
    for peer in peers:
        pl.semaphore_signal(barrier, inc=1, device_id={"wide": peer}, device_id_type=MESH)
    pl.semaphore_signal(barrier, inc=1, device_id={"narrow": other}, device_id_type=MESH)
    pl.semaphore_wait(barrier, wide_count)

    def kv_copy(source, peer):
        return [
            pltpu.make_async_remote_copy(
                src_ref=hbm.at[pl.ds(0, rows)],
                dst_ref=buf.at[source],
                send_sem=send.at[peer],
                recv_sem=recv.at[source],
                device_id={"wide": peer},
                device_id_type=MESH,
            )
            for hbm, buf, send, recv in (
                (k_hbm, k_buf, k_send, k_recv),
                (v_hbm, v_buf, v_send, v_recv),
            )
        ]

    for peer in peers:
        for copy in kv_copy(me, peer):
            copy.start()

    row_id = lax.broadcasted_iota(jnp.int32, (rows, rows), 0)
    col_id = lax.broadcasted_iota(jnp.int32, (rows, rows), 1)

    owner_across = jnp.broadcast_to(owner_ref[...], (rows, rows)).astype(jnp.float32)
    owner_down = owner_across.T
    same = jnp.where((owner_down == owner_across) & (row_id < col_id), 1.0, 0.0)
    slot = jnp.sum(same, axis=0, keepdims=True)
    target = (owner_across[0:1] * capacity + slot).astype(jnp.int32)
    slots = lax.broadcasted_iota(jnp.int32, (wide_count * capacity, rows), 0)
    dispatch = jnp.where(slots == target, 1.0, 0.0).astype(jnp.bfloat16)

    def part_copy(c, phase):
        return pltpu.make_async_remote_copy(
            src_ref=part_buf.at[phase, c],
            dst_ref=recv_buf.at[c],
            send_sem=p_send.at[c],
            recv_sem=p_recv.at[c],
            device_id={"narrow": other},
            device_id_type=MESH,
        )

    def project(phase, c):
        if phase == 1:
            pltpu.make_async_copy(
                w_hbm.at[:, pl.ds(pl.multiple_of(c * piece, piece), piece)],
                w_buf.at[c],
                w_sem.at[c],
            ).wait()
        product = jnp.dot(att_buf[phase], w_buf[c], preferred_element_type=jnp.float32)
        part_buf[phase, c] = product.astype(jnp.bfloat16)

    def lend(phase):
        def step(c, carry):
            project(phase, c)
            part_copy(c, phase).start()
            return carry

        lax.fori_loop(0, PIECES, step, 0)

    def out_copy(c, source, peer):
        return pltpu.make_async_remote_copy(
            src_ref=out_buf.at[c, peer],
            dst_ref=ffn_ref.at[source, :, pl.ds(pl.multiple_of(c * span, span), span)],
            send_sem=o_send.at[c, peer],
            recv_sem=o_recv.at[c, source],
            device_id={"wide": peer},
            device_id_type=MESH,
        )

    def own_copy(c):
        return pltpu.make_async_copy(
            out_buf.at[c, me],
            ffn_ref.at[me, :, pl.ds(pl.multiple_of(c * span, span), span)],
            own_sem.at[c],
        )

    def finish(phase):
        res_load.wait()

        def add_piece(c, squares):
            part_copy(c, phase).wait_recv()
            cols = pl.ds(pl.multiple_of(c * piece, piece), piece)
            summed = part_buf[phase, c].astype(jnp.float32) + recv_buf[c].astype(jnp.float32)
            hidden = (res_buf[:, cols].astype(jnp.float32) + summed).astype(jnp.bfloat16)
            hidden_ref[:, cols] = hidden
            widened = hidden.astype(jnp.float32)
            return squares + jnp.sum(widened * widened, axis=1, keepdims=True)

        def step(c, squares):
            project(phase, c)
            return add_piece(c - 1, squares)

        project(phase, 0)
        squares = lax.fori_loop(1, PIECES, step, jnp.zeros((rows, 1), jnp.float32))
        squares = add_piece(PIECES - 1, squares)
        factor = lax.rsqrt(squares / model + 1e-05)
        lines = span // HEAD
        gain_buf[...] = gain_ref[...].astype(jnp.float32)

        def send_piece(c, carry):
            cols = pl.ds(pl.multiple_of(c * span, span), span)
            gains = gain_buf[pl.ds(pl.multiple_of(c * lines, lines), lines), :]
            gain = jnp.concatenate([gains[i : i + 1] for i in range(lines)], axis=1)
            normed = (hidden_ref[:, cols].astype(jnp.float32) * factor * gain).astype(jnp.bfloat16)
            outgoing = jnp.dot(dispatch, normed, preferred_element_type=jnp.float32)
            out_buf[c] = outgoing.astype(jnp.bfloat16).reshape(wide_count, capacity, span)
            for peer in peers:
                out_copy(c, me, peer).start()
            own_copy(c).start()
            return carry

        lax.fori_loop(0, SENDS, send_piece, 0)

    def both(phase):
        @pl.when(lane == phase)
        def _():
            finish(phase)

        @pl.when(lane != phase)
        def _():
            lend(phase)

    for load in loads:
        load.wait()
    seg_across = jnp.broadcast_to(seg_ref[...], (rows, rows)).astype(jnp.float32)
    short_visible = (seg_across == seg_across.T) & (col_id <= row_id)
    attend_heads(
        q_buf,
        lambda group: ks_buf[:, group],
        lambda group: vs_buf[:, group],
        short_visible,
        short_rows,
        att_buf,
        1,
        local_kv,
        group_size,
    )
    both(1)

    for load in late_loads:
        load.wait()
    for peer in peers:
        for copy in kv_copy(peer, peer):
            copy.wait_recv()
    own_span = span_ref[me]
    long_visible = jnp.concatenate(
        [
            (span_ref[b] * rows + col_id) <= (own_span * rows + row_id)
            for b in range(wide_count)
        ],
        axis=1,
    )
    attend_heads(
        q_buf,
        lambda group: k_buf[:, :, group].reshape(wide_count * rows, HEAD),
        lambda group: v_buf[:, :, group].reshape(wide_count * rows, HEAD),
        long_visible,
        long_rows,
        att_buf,
        0,
        local_kv,
        group_size,
    )
    both(0)

    for peer in peers:
        for copy in kv_copy(me, peer):
            copy.wait_send()

    def drain_parts(c, carry):
        part_copy(c, 0).wait_send()
        return carry

    lax.fori_loop(0, PIECES, drain_parts, 0)

    def drain_sends(c, carry):
        for peer in peers:
            out_copy(c, me, peer).wait_send()
            out_copy(c, peer, peer).wait_recv()
        own_copy(c).wait()
        return carry

    lax.fori_loop(0, SENDS, drain_sends, 0)


def store_kernel(hidden_ref, ffn_ref, hidden_out, ffn_out, sems):
    copies = [pltpu.make_async_copy(hidden_ref, hidden_out, sems.at[0])]
    for s in range(ffn_ref.shape[0]):
        copies.append(pltpu.make_async_copy(ffn_ref.at[s], ffn_out.at[s], sems.at[1 + s]))
    for copy in copies:
        copy.start()
    for copy in copies:
        copy.wait()


def fused_on_device(
    queries, key_rows, value_rows, residual, out_weight, norm_gain, span_map, segments, row_owner
):
    wide_count = lax.axis_size("wide")
    local_heads = queries.shape[1] // HEAD
    local_kv = key_rows.shape[1] // HEAD
    rows, model = residual.shape
    capacity = max(2, 2 * rows // wide_count)
    sizes = (wide_count, capacity, local_kv, local_heads // local_kv)
    bf16 = jnp.bfloat16
    dma = pltpu.SemaphoreType.DMA
    any_spec = pl.BlockSpec(memory_space=pl.ANY)
    vmem_spec = pl.BlockSpec(memory_space=pltpu.VMEM)
    piece, span = model // PIECES, model // SENDS
    hidden, arrived = pl.pallas_call(
        functools.partial(fused_kernel, sizes),
        out_shape=(
            pltpu.VMEM((rows, model), bf16),
            pltpu.VMEM((wide_count, capacity, model), bf16),
        ),
        in_specs=[pl.BlockSpec(memory_space=pltpu.SMEM), vmem_spec, vmem_spec]
        + [any_spec] * 5
        + [vmem_spec],
        out_specs=(vmem_spec, vmem_spec),
        scratch_shapes=[
            pltpu.VMEM(queries.shape, bf16),
            pltpu.VMEM((rows, key_rows.shape[1]), bf16),
            pltpu.VMEM((rows, key_rows.shape[1]), bf16),
            pltpu.VMEM((wide_count, rows, key_rows.shape[1]), bf16),
            pltpu.VMEM((wide_count, rows, key_rows.shape[1]), bf16),
            pltpu.VMEM((PIECES, out_weight.shape[0], piece), bf16),
            pltpu.VMEM((rows, model), bf16),
            pltpu.VMEM((2, rows, queries.shape[1]), bf16),
            pltpu.VMEM((2, PIECES, rows, piece), bf16),
            pltpu.VMEM((PIECES, rows, piece), bf16),
            pltpu.VMEM((SENDS, wide_count, capacity, span), bf16),
            pltpu.VMEM((model // HEAD, HEAD), jnp.float32),
            dma((6,)),
            dma((PIECES,)),
            dma((wide_count,)),
            dma((wide_count,)),
            dma((wide_count,)),
            dma((wide_count,)),
            dma((PIECES,)),
            dma((PIECES,)),
            dma((SENDS, wide_count)),
            dma((SENDS, wide_count)),
            dma((SENDS,)),
        ],
        compiler_params=pltpu.CompilerParams(
            collective_id=0, has_side_effects=True, vmem_limit_bytes=60 * 1024 * 1024
        ),
    )(
        span_map,
        segments,
        row_owner.reshape(1, rows),
        queries,
        key_rows,
        value_rows,
        residual,
        out_weight,
        norm_gain.reshape(model // HEAD, HEAD),
    )
    hidden, arrived = pl.pallas_call(
        store_kernel,
        out_shape=(
            jax.ShapeDtypeStruct(hidden.shape, bf16),
            jax.ShapeDtypeStruct(arrived.shape, bf16),
        ),
        in_specs=[any_spec] * 2,
        out_specs=(any_spec, any_spec),
        scratch_shapes=[dma((1 + wide_count,))],
        compiler_params=pltpu.CompilerParams(vmem_limit_bytes=1024 * 1024),
    )(hidden, arrived)
    return hidden, arrived.reshape(1, 1, wide_count, capacity, model)


def on_device(*args):
    queries, residual = args[0], args[3]
    rows, model = residual.shape
    wide_count = lax.axis_size("wide")
    fits = (
        lax.axis_size("narrow") == 2
        and rows == LONG_DEV
        and queries.shape[0] == 2 * LONG_DEV
        and (2 * rows) % (16 * wide_count) == 0
        and model % (PIECES * HEAD) == 0
    )
    return (fused_on_device if fits else general_on_device)(*args)


def solution(mesh):
    placed = (
        P(("rep", "wide"), "narrow"),
        P(("rep", "wide"), "narrow"),
        P(("rep", "wide"), "narrow"),
        P(("rep", "wide", "narrow"), None),
        P("narrow", None),
        P(),
        P(),
        P(("rep", "wide"), None),
        P(("rep", "wide", "narrow"), None),
    )
    return jax.shard_map(
        on_device,
        mesh=mesh,
        in_specs=placed,
        out_specs=(
            P(("rep", "wide", "narrow"), None),
            P(("rep", "wide"), "narrow", None, None, None),
        ),
        check_vma=False,
    )
```

```python
import functools

import jax
import jax.numpy as jnp
from jax import lax
from jax.experimental import pallas as pl
from jax.experimental.pallas import tpu as pltpu
from jax.sharding import PartitionSpec as P

HEAD = 128
LONG_DEV = 128


def attend_block(
    partial_state, long_queries, key_block, value_block, key_pos, query_pos, score_scale
):
    running_max, weight_sum, weighted = partial_state
    scores = (
        jnp.einsum("qgjd,kgd->qgjk", long_queries, key_block, preferred_element_type=jnp.float32)
        * score_scale
    )
    visible = (key_pos[None, :] <= query_pos[:, None])[:, None, None, :]
    masked = jnp.where(visible, scores, -1e30)
    newest = jnp.maximum(running_max, jnp.max(masked, axis=-1))
    weights = jnp.where(visible, jnp.exp(masked - newest[..., None]), 0.0)
    factor = jnp.exp(running_max - newest)
    weight_sum = weight_sum * factor + jnp.sum(weights, axis=-1)
    weighted = weighted * factor[..., None] + jnp.einsum(
        "qgjk,kgd->qgjd",
        weights.astype(jnp.bfloat16),
        value_block,
        preferred_element_type=jnp.float32,
    )
    return (newest, weight_sum, weighted)


def rounded_term(attended, out_weight):
    product = jnp.dot(attended, out_weight, preferred_element_type=jnp.float32)
    return lax.optimization_barrier(product.astype(jnp.bfloat16)).astype(jnp.float32)


def general_on_device(
    queries, key_rows, value_rows, residual, out_weight, norm_gain, span_map, segments, row_owner
):
    wide_count = lax.axis_size("wide")
    narrow_count = lax.axis_size("narrow")
    wide_index = lax.axis_index("wide")
    local_heads = queries.shape[1] // HEAD
    local_kv = key_rows.shape[1] // HEAD
    group_size = local_heads // local_kv
    token_count = queries.shape[0]
    short_count = token_count - LONG_DEV
    score_scale = HEAD ** (-0.5)
    own_span = lax.dynamic_slice_in_dim(span_map, wide_index, 1, 0)[0]
    query_pos = own_span * LONG_DEV + jnp.arange(LONG_DEV, dtype=jnp.int32)
    long_queries = queries[:LONG_DEV].reshape(LONG_DEV, local_kv, group_size, HEAD)
    wide_ids = jnp.arange(wide_count, dtype=jnp.int32)
    start_state = (
        jnp.full((LONG_DEV, local_kv, group_size), -1e30, jnp.float32),
        jnp.zeros((LONG_DEV, local_kv, group_size), jnp.float32),
        jnp.zeros((LONG_DEV, local_kv, group_size, HEAD), jnp.float32),
    )
    key_piece = lax.all_gather(key_rows[:LONG_DEV], "wide", axis=0, tiled=True)
    value_piece = lax.all_gather(value_rows[:LONG_DEV], "wide", axis=0, tiled=True)
    row_count = key_piece.shape[0]
    key_index = jnp.arange(row_count, dtype=jnp.int32)
    holder = key_index // LONG_DEV
    span_of = jnp.sum(jnp.where(holder[:, None] == wide_ids[None, :], span_map[None, :], 0), axis=1)
    key_pos = span_of * LONG_DEV + key_index % LONG_DEV
    key_block = key_piece.reshape(row_count, local_kv, HEAD)
    value_block = value_piece.reshape(row_count, local_kv, HEAD)

    def advance(partial_state):
        if row_count > 512 and row_count % 512 == 0:
            splits = row_count // 512

            def advance_block(inner_state, sliced):
                return (
                    attend_block(
                        inner_state,
                        long_queries,
                        sliced[0],
                        sliced[1],
                        sliced[2],
                        query_pos,
                        score_scale,
                    ),
                    None,
                )

            finished, unused = lax.scan(
                advance_block,
                partial_state,
                (
                    key_block.reshape(splits, 512, local_kv, HEAD),
                    value_block.reshape(splits, 512, local_kv, HEAD),
                    key_pos.reshape(splits, 512),
                ),
            )
            return finished
        return attend_block(
            partial_state, long_queries, key_block, value_block, key_pos, query_pos, score_scale
        )

    running_max, weight_sum, weighted = advance(start_state)
    long_out = (
        (weighted / weight_sum[..., None])
        .astype(jnp.bfloat16)
        .reshape(LONG_DEV, local_heads * HEAD)
    )
    short_queries = queries[LONG_DEV:].reshape(short_count, local_kv, group_size, HEAD)
    short_keys = key_rows[LONG_DEV:].reshape(short_count, local_kv, HEAD)
    short_values = value_rows[LONG_DEV:].reshape(short_count, local_kv, HEAD)
    documents = segments[0]
    positions = jnp.arange(short_count, dtype=jnp.int32)
    visible = (
        (documents[None, :] == documents[:, None]) & (positions[None, :] <= positions[:, None])
    )[:, None, None, :]
    scores = (
        jnp.einsum("qgjd,kgd->qgjk", short_queries, short_keys, preferred_element_type=jnp.float32)
        * score_scale
    )
    masked = jnp.where(visible, scores, -1e30)
    row_max = jnp.max(masked, axis=-1, keepdims=True)
    weights = jnp.where(visible, jnp.exp(masked - row_max), 0.0)
    short_sum = jnp.sum(weights, axis=-1)
    mixed = jnp.einsum(
        "qgjk,kgd->qgjd",
        weights.astype(jnp.bfloat16),
        short_values,
        preferred_element_type=jnp.float32,
    )
    short_out = (
        (mixed / short_sum[..., None]).astype(jnp.bfloat16).reshape(short_count, local_heads * HEAD)
    )
    attended = jnp.concatenate([long_out, short_out], axis=0)
    rows_dev = token_count // narrow_count
    sliced = attended
    summed = lax.psum_scatter(
        rounded_term(sliced, out_weight).astype(jnp.bfloat16),
        "narrow",
        scatter_dimension=0,
        tiled=True,
    ).astype(jnp.float32)
    hidden = (residual.astype(jnp.float32) + summed).astype(jnp.bfloat16)
    widened = hidden.astype(jnp.float32)
    normed = (
        widened
        * lax.rsqrt(jnp.mean(widened * widened, axis=1, keepdims=True) + 1e-05)
        * norm_gain.astype(jnp.float32)
    ).astype(jnp.bfloat16)
    capacity = max(2, 2 * rows_dev // wide_count)
    owners = row_owner[:, 0]
    chosen = (owners[:, None] == wide_ids[None, :]).astype(jnp.int32)
    earlier = jnp.cumsum(chosen, axis=0) - chosen
    slot_index = jnp.sum(earlier * chosen, axis=1)
    target = owners * capacity + slot_index
    dispatch = (
        target[None, :] == jnp.arange(wide_count * capacity, dtype=jnp.int32)[:, None]
    ).astype(jnp.bfloat16)
    outgoing = jnp.dot(dispatch, normed, preferred_element_type=jnp.float32).astype(jnp.bfloat16)
    outgoing = outgoing.reshape(wide_count, 1, 1, capacity, normed.shape[1])
    arrived = lax.all_to_all(outgoing, "wide", split_axis=0, concat_axis=2, tiled=True)
    return (hidden, arrived)


PIECES = 8
SENDS = 4
MESH = pl.DeviceIdType.MESH


def attend_heads(q_buf, keys, values, visible, rows, out_buf, lane, local_kv, group_size):
    score_scale = HEAD ** (-0.5)
    count = rows.stop - rows.start
    tiled = jnp.concatenate([visible] * group_size, axis=0)

    def attend_group(g, carry):
        heads = [
            pl.ds(pl.multiple_of((g * group_size + j) * HEAD, HEAD), HEAD) for j in range(group_size)
        ]
        group = pl.ds(pl.multiple_of(g * HEAD, HEAD), HEAD)
        stacked = jnp.concatenate([q_buf[rows, h] for h in heads], axis=0)
        scores = (
            lax.dot_general(
                stacked, keys(group), (((1,), (1,)), ((), ())), preferred_element_type=jnp.float32
            )
            * score_scale
        )
        masked = jnp.where(tiled, scores, -1e30)
        weights = jnp.exp(masked - jnp.max(masked, axis=1, keepdims=True))
        total = jnp.sum(weights, axis=1, keepdims=True)
        mixed = jnp.dot(
            weights.astype(jnp.bfloat16), values(group), preferred_element_type=jnp.float32
        )
        mixed = (mixed / total).astype(jnp.bfloat16)
        for j, h in enumerate(heads):
            out_buf[lane, :, h] = mixed[j * count : (j + 1) * count]
        return carry

    lax.fori_loop(0, local_kv, attend_group, 0)


def fused_kernel(
    sizes,
    span_ref,
    seg_ref,
    owner_ref,
    q_hbm,
    k_hbm,
    v_hbm,
    res_hbm,
    w_hbm,
    gain_ref,
    hidden_ref,
    ffn_ref,
    q_buf,
    ks_buf,
    vs_buf,
    k_buf,
    v_buf,
    w_buf,
    res_buf,
    att_buf,
    part_buf,
    recv_buf,
    out_buf,
    relay_buf,
    gain_buf,
    in_sem,
    w_sem,
    kv_send,
    kv_recv,
    p_send,
    p_recv,
    o_send,
    o_recv,
    own_sem,
):
    wide_count, capacity, local_kv, group_size = sizes
    rows, model = res_hbm.shape
    piece = model // PIECES
    span = model // SENDS
    me = lax.axis_index("wide")
    lane = lax.axis_index("narrow")
    other = 1 - lane
    half = capacity // 2
    along, across = lax.rem(me, 2), me // 2
    near = [across * 2 + 1 - along, (1 - across) * 2 + along]
    far = (1 - across) * 2 + 1 - along
    long_rows, short_rows = slice(0, rows), slice(rows, 2 * rows)

    loads = [
        pltpu.make_async_copy(q_hbm, q_buf, in_sem.at[0]),
        pltpu.make_async_copy(k_hbm.at[pl.ds(rows, rows)], ks_buf, in_sem.at[1]),
        pltpu.make_async_copy(v_hbm.at[pl.ds(rows, rows)], vs_buf, in_sem.at[2]),
    ]
    late_loads = [
        pltpu.make_async_copy(k_hbm.at[pl.ds(0, rows)], k_buf.at[me], in_sem.at[3]),
        pltpu.make_async_copy(v_hbm.at[pl.ds(0, rows)], v_buf.at[me], in_sem.at[4]),
    ]
    res_load = pltpu.make_async_copy(res_hbm, res_buf, in_sem.at[5])
    w_loads = [
        pltpu.make_async_copy(
            w_hbm.at[:, pl.ds(c * piece, piece)], w_buf.at[c], w_sem.at[c]
        )
        for c in range(PIECES)
    ]
    for load in loads + w_loads + [res_load] + late_loads:
        load.start()

    barrier = pltpu.get_barrier_semaphore()
    for peer in near:
        pl.semaphore_signal(barrier, inc=1, device_id={"wide": peer}, device_id_type=MESH)
    pl.semaphore_signal(barrier, inc=1, device_id={"narrow": other}, device_id_type=MESH)

    def kv_copy(i, source, peer, first, sem):
        hbm, buf = ((k_hbm, k_buf), (v_hbm, v_buf))[i]
        return pltpu.make_async_remote_copy(
            src_ref=hbm.at[pl.ds(0, rows)] if first else buf.at[source],
            dst_ref=buf.at[source],
            send_sem=kv_send.at[i, sem],
            recv_sem=kv_recv.at[i, source],
            device_id={"wide": peer},
            device_id_type=MESH,
        )

    kv_first = [kv_copy(i, me, near[j], True, j) for i in range(2) for j in range(2)]
    kv_forward = [kv_copy(i, near[i], near[1 - i], False, 2) for i in range(2)]

    row_id = lax.broadcasted_iota(jnp.int32, (rows, rows), 0)
    col_id = lax.broadcasted_iota(jnp.int32, (rows, rows), 1)

    owner_across = jnp.broadcast_to(owner_ref[...], (rows, rows)).astype(jnp.float32)
    owner_down = owner_across.T
    same = jnp.where((owner_down == owner_across) & (row_id < col_id), 1.0, 0.0)
    slot = jnp.sum(same, axis=0, keepdims=True)
    target = (owner_across[0:1] * capacity + slot).astype(jnp.int32)
    slots = lax.broadcasted_iota(jnp.int32, (wide_count * capacity, rows), 0)
    dispatch = jnp.where(slots == target, 1.0, 0.0).astype(jnp.bfloat16)

    pl.semaphore_wait(barrier, 3)
    for copy in kv_first:
        copy.start()

    def part_copy(c, phase):
        return pltpu.make_async_remote_copy(
            src_ref=part_buf.at[phase, c],
            dst_ref=recv_buf.at[c],
            send_sem=p_send.at[c],
            recv_sem=p_recv.at[c],
            device_id={"narrow": other},
            device_id_type=MESH,
        )

    def project(phase, c):
        if phase == 1:
            pltpu.make_async_copy(
                w_hbm.at[:, pl.ds(pl.multiple_of(c * piece, piece), piece)],
                w_buf.at[c],
                w_sem.at[c],
            ).wait()
        product = jnp.dot(att_buf[phase], w_buf[c], preferred_element_type=jnp.float32)
        part_buf[phase, c] = product.astype(jnp.bfloat16)

    def send_values_on():
        kv_copy(1, near[1], near[1], True, 1).wait_recv()
        kv_forward[1].start()

    def lend(phase):
        def step(c, carry):
            project(phase, c)
            part_copy(c, phase).start()
            return carry

        lax.fori_loop(0, PIECES, step, 0)
        if phase == 1:
            send_values_on()

    def direct_copy(c, j, source):
        return pltpu.make_async_remote_copy(
            src_ref=out_buf.at[c, near[j]],
            dst_ref=ffn_ref.at[source, :, pl.ds(pl.multiple_of(c * span, span), span)],
            send_sem=o_send.at[c, j],
            recv_sem=o_recv.at[c, j],
            device_id={"wide": near[j]},
            device_id_type=MESH,
        )

    def relay_copy(c, j):
        return pltpu.make_async_remote_copy(
            src_ref=out_buf.at[c, far, pl.ds(j * half, half)],
            dst_ref=relay_buf.at[c, j],
            send_sem=o_send.at[c, 2 + j],
            recv_sem=o_recv.at[c, 2 + j],
            device_id={"wide": near[j]},
            device_id_type=MESH,
        )

    def forward_copy(c, j, source):
        cols = pl.ds(pl.multiple_of(c * span, span), span)
        return pltpu.make_async_remote_copy(
            src_ref=relay_buf.at[c, j],
            dst_ref=ffn_ref.at[source, pl.ds(j * half, half), cols],
            send_sem=o_send.at[c, 4 + j],
            recv_sem=o_recv.at[c, 4 + j],
            device_id={"wide": near[1 - j]},
            device_id_type=MESH,
        )

    def own_copy(c):
        return pltpu.make_async_copy(
            out_buf.at[c, me],
            ffn_ref.at[me, :, pl.ds(pl.multiple_of(c * span, span), span)],
            own_sem.at[c],
        )

    def finish(phase):
        res_load.wait()

        def add_piece(c, squares):
            part_copy(c, phase).wait_recv()
            cols = pl.ds(pl.multiple_of(c * piece, piece), piece)
            summed = part_buf[phase, c].astype(jnp.float32) + recv_buf[c].astype(jnp.float32)
            hidden = (res_buf[:, cols].astype(jnp.float32) + summed).astype(jnp.bfloat16)
            hidden_ref[:, cols] = hidden
            widened = hidden.astype(jnp.float32)
            return squares + jnp.sum(widened * widened, axis=1, keepdims=True)

        def step(c, squares):
            project(phase, c)
            return add_piece(c - 1, squares)

        project(phase, 0)
        squares = lax.fori_loop(1, PIECES, step, jnp.zeros((rows, 1), jnp.float32))
        if phase == 1:
            send_values_on()
        squares = add_piece(PIECES - 1, squares)
        factor = lax.rsqrt(squares / model + 1e-05)
        lines = span // HEAD
        gain_buf[...] = gain_ref[...].astype(jnp.float32)

        def send_piece(c, carry):
            cols = pl.ds(pl.multiple_of(c * span, span), span)
            gains = gain_buf[pl.ds(pl.multiple_of(c * lines, lines), lines), :]
            gain = jnp.concatenate([gains[i : i + 1] for i in range(lines)], axis=1)
            normed = (hidden_ref[:, cols].astype(jnp.float32) * factor * gain).astype(jnp.bfloat16)
            outgoing = jnp.dot(dispatch, normed, preferred_element_type=jnp.float32)
            out_buf[c] = outgoing.astype(jnp.bfloat16).reshape(wide_count, capacity, span)
            for j in range(2):
                relay_copy(c, j).start()
            for j in range(2):
                direct_copy(c, j, me).start()
            own_copy(c).start()
            return carry

        lax.fori_loop(0, SENDS, send_piece, 0)

    def both(phase):
        @pl.when(lane == phase)
        def _():
            finish(phase)

        @pl.when(lane != phase)
        def _():
            lend(phase)

    for load in loads:
        load.wait()
    seg_across = jnp.broadcast_to(seg_ref[...], (rows, rows)).astype(jnp.float32)
    short_visible = (seg_across == seg_across.T) & (col_id <= row_id)
    attend_heads(
        q_buf,
        lambda group: ks_buf[:, group],
        lambda group: vs_buf[:, group],
        short_visible,
        short_rows,
        att_buf,
        1,
        local_kv,
        group_size,
    )
    kv_copy(0, near[0], near[0], True, 0).wait_recv()
    kv_forward[0].start()
    both(1)

    for load in late_loads:
        load.wait()
    kv_copy(0, near[1], near[1], True, 1).wait_recv()
    kv_copy(1, near[0], near[0], True, 0).wait_recv()
    for i in range(2):
        kv_copy(i, far, near[1 - i], False, 2).wait_recv()
    own_span = span_ref[me]
    long_visible = jnp.concatenate(
        [
            (span_ref[b] * rows + col_id) <= (own_span * rows + row_id)
            for b in range(wide_count)
        ],
        axis=1,
    )
    attend_heads(
        q_buf,
        lambda group: k_buf[:, :, group].reshape(wide_count * rows, HEAD),
        lambda group: v_buf[:, :, group].reshape(wide_count * rows, HEAD),
        long_visible,
        long_rows,
        att_buf,
        0,
        local_kv,
        group_size,
    )
    both(0)

    def forward(c, carry):
        for j in range(2):
            relay_copy(c, j).wait_recv()
            forward_copy(c, j, near[j]).start()
        return carry

    lax.fori_loop(0, SENDS, forward, 0)

    for copy in kv_first + kv_forward:
        copy.wait_send()

    def drain_parts(c, carry):
        part_copy(c, 0).wait_send()
        return carry

    lax.fori_loop(0, PIECES, drain_parts, 0)

    def drain_sends(c, carry):
        for j in range(2):
            relay_copy(c, j).wait_send()
            direct_copy(c, j, me).wait_send()
            direct_copy(c, j, near[j]).wait_recv()
            forward_copy(c, j, near[j]).wait_send()
            forward_copy(c, j, far).wait_recv()
        own_copy(c).wait()
        return carry

    lax.fori_loop(0, SENDS, drain_sends, 0)


def store_kernel(hidden_ref, ffn_ref, hidden_out, ffn_out, sems):
    copies = [pltpu.make_async_copy(hidden_ref, hidden_out, sems.at[0])]
    for s in range(ffn_ref.shape[0]):
        copies.append(pltpu.make_async_copy(ffn_ref.at[s], ffn_out.at[s], sems.at[1 + s]))
    for copy in copies:
        copy.start()
    for copy in copies:
        copy.wait()


def fused_on_device(
    queries, key_rows, value_rows, residual, out_weight, norm_gain, span_map, segments, row_owner
):
    wide_count = lax.axis_size("wide")
    local_heads = queries.shape[1] // HEAD
    local_kv = key_rows.shape[1] // HEAD
    rows, model = residual.shape
    capacity = max(2, 2 * rows // wide_count)
    sizes = (wide_count, capacity, local_kv, local_heads // local_kv)
    bf16 = jnp.bfloat16
    dma = pltpu.SemaphoreType.DMA
    any_spec = pl.BlockSpec(memory_space=pl.ANY)
    vmem_spec = pl.BlockSpec(memory_space=pltpu.VMEM)
    piece, span = model // PIECES, model // SENDS
    hidden, arrived = pl.pallas_call(
        functools.partial(fused_kernel, sizes),
        out_shape=(
            pltpu.VMEM((rows, model), bf16),
            pltpu.VMEM((wide_count, capacity, model), bf16),
        ),
        in_specs=[pl.BlockSpec(memory_space=pltpu.SMEM), vmem_spec, vmem_spec]
        + [any_spec] * 5
        + [vmem_spec],
        out_specs=(vmem_spec, vmem_spec),
        scratch_shapes=[
            pltpu.VMEM(queries.shape, bf16),
            pltpu.VMEM((rows, key_rows.shape[1]), bf16),
            pltpu.VMEM((rows, key_rows.shape[1]), bf16),
            pltpu.VMEM((wide_count, rows, key_rows.shape[1]), bf16),
            pltpu.VMEM((wide_count, rows, key_rows.shape[1]), bf16),
            pltpu.VMEM((PIECES, out_weight.shape[0], piece), bf16),
            pltpu.VMEM((rows, model), bf16),
            pltpu.VMEM((2, rows, queries.shape[1]), bf16),
            pltpu.VMEM((2, PIECES, rows, piece), bf16),
            pltpu.VMEM((PIECES, rows, piece), bf16),
            pltpu.VMEM((SENDS, wide_count, capacity, span), bf16),
            pltpu.VMEM((SENDS, 2, capacity // 2, span), bf16),
            pltpu.VMEM((model // HEAD, HEAD), jnp.float32),
            dma((6,)),
            dma((PIECES,)),
            dma((2, 3)),
            dma((2, wide_count)),
            dma((PIECES,)),
            dma((PIECES,)),
            dma((SENDS, 6)),
            dma((SENDS, 6)),
            dma((SENDS,)),
        ],
        compiler_params=pltpu.CompilerParams(
            collective_id=0, has_side_effects=True, vmem_limit_bytes=60 * 1024 * 1024
        ),
    )(
        span_map,
        segments,
        row_owner.reshape(1, rows),
        queries,
        key_rows,
        value_rows,
        residual,
        out_weight,
        norm_gain.reshape(model // HEAD, HEAD),
    )
    hidden, arrived = pl.pallas_call(
        store_kernel,
        out_shape=(
            jax.ShapeDtypeStruct(hidden.shape, bf16),
            jax.ShapeDtypeStruct(arrived.shape, bf16),
        ),
        in_specs=[any_spec] * 2,
        out_specs=(any_spec, any_spec),
        scratch_shapes=[dma((1 + wide_count,))],
        compiler_params=pltpu.CompilerParams(vmem_limit_bytes=1024 * 1024),
    )(hidden, arrived)
    return hidden, arrived.reshape(1, 1, wide_count, capacity, model)


def on_device(*args):
    queries, residual = args[0], args[3]
    rows, model = residual.shape
    wide_count = lax.axis_size("wide")
    fits = (
        lax.axis_size("narrow") == 2
        and rows == LONG_DEV
        and queries.shape[0] == 2 * LONG_DEV
        and wide_count == 4
        and (2 * rows) % (32 * wide_count) == 0
        and model % (PIECES * HEAD) == 0
    )
    return (fused_on_device if fits else general_on_device)(*args)


def solution(mesh):
    placed = (
        P(("rep", "wide"), "narrow"),
        P(("rep", "wide"), "narrow"),
        P(("rep", "wide"), "narrow"),
        P(("rep", "wide", "narrow"), None),
        P("narrow", None),
        P(),
        P(),
        P(("rep", "wide"), None),
        P(("rep", "wide", "narrow"), None),
    )
    return jax.shard_map(
        on_device,
        mesh=mesh,
        in_specs=placed,
        out_specs=(
            P(("rep", "wide", "narrow"), None),
            P(("rep", "wide"), "narrow", None, None, None),
        ),
        check_vma=False,
    )
```

```python
import functools

import jax
import jax.numpy as jnp
from jax import lax
from jax.experimental import pallas as pl
from jax.experimental.pallas import tpu as pltpu
from jax.sharding import PartitionSpec as P

HEAD = 128
LONG_DEV = 128


def attend_block(
    partial_state, long_queries, key_block, value_block, key_pos, query_pos, score_scale
):
    running_max, weight_sum, weighted = partial_state
    scores = (
        jnp.einsum("qgjd,kgd->qgjk", long_queries, key_block, preferred_element_type=jnp.float32)
        * score_scale
    )
    visible = (key_pos[None, :] <= query_pos[:, None])[:, None, None, :]
    masked = jnp.where(visible, scores, -1e30)
    newest = jnp.maximum(running_max, jnp.max(masked, axis=-1))
    weights = jnp.where(visible, jnp.exp(masked - newest[..., None]), 0.0)
    factor = jnp.exp(running_max - newest)
    weight_sum = weight_sum * factor + jnp.sum(weights, axis=-1)
    weighted = weighted * factor[..., None] + jnp.einsum(
        "qgjk,kgd->qgjd",
        weights.astype(jnp.bfloat16),
        value_block,
        preferred_element_type=jnp.float32,
    )
    return (newest, weight_sum, weighted)


def rounded_term(attended, out_weight):
    product = jnp.dot(attended, out_weight, preferred_element_type=jnp.float32)
    return lax.optimization_barrier(product.astype(jnp.bfloat16)).astype(jnp.float32)


def general_on_device(
    queries, key_rows, value_rows, residual, out_weight, norm_gain, span_map, segments, row_owner
):
    wide_count = lax.axis_size("wide")
    narrow_count = lax.axis_size("narrow")
    wide_index = lax.axis_index("wide")
    local_heads = queries.shape[1] // HEAD
    local_kv = key_rows.shape[1] // HEAD
    group_size = local_heads // local_kv
    token_count = queries.shape[0]
    short_count = token_count - LONG_DEV
    score_scale = HEAD ** (-0.5)
    own_span = lax.dynamic_slice_in_dim(span_map, wide_index, 1, 0)[0]
    query_pos = own_span * LONG_DEV + jnp.arange(LONG_DEV, dtype=jnp.int32)
    long_queries = queries[:LONG_DEV].reshape(LONG_DEV, local_kv, group_size, HEAD)
    wide_ids = jnp.arange(wide_count, dtype=jnp.int32)
    start_state = (
        jnp.full((LONG_DEV, local_kv, group_size), -1e30, jnp.float32),
        jnp.zeros((LONG_DEV, local_kv, group_size), jnp.float32),
        jnp.zeros((LONG_DEV, local_kv, group_size, HEAD), jnp.float32),
    )
    key_piece = lax.all_gather(key_rows[:LONG_DEV], "wide", axis=0, tiled=True)
    value_piece = lax.all_gather(value_rows[:LONG_DEV], "wide", axis=0, tiled=True)
    row_count = key_piece.shape[0]
    key_index = jnp.arange(row_count, dtype=jnp.int32)
    holder = key_index // LONG_DEV
    span_of = jnp.sum(jnp.where(holder[:, None] == wide_ids[None, :], span_map[None, :], 0), axis=1)
    key_pos = span_of * LONG_DEV + key_index % LONG_DEV
    key_block = key_piece.reshape(row_count, local_kv, HEAD)
    value_block = value_piece.reshape(row_count, local_kv, HEAD)

    def advance(partial_state):
        if row_count > 512 and row_count % 512 == 0:
            splits = row_count // 512

            def advance_block(inner_state, sliced):
                return (
                    attend_block(
                        inner_state,
                        long_queries,
                        sliced[0],
                        sliced[1],
                        sliced[2],
                        query_pos,
                        score_scale,
                    ),
                    None,
                )

            finished, unused = lax.scan(
                advance_block,
                partial_state,
                (
                    key_block.reshape(splits, 512, local_kv, HEAD),
                    value_block.reshape(splits, 512, local_kv, HEAD),
                    key_pos.reshape(splits, 512),
                ),
            )
            return finished
        return attend_block(
            partial_state, long_queries, key_block, value_block, key_pos, query_pos, score_scale
        )

    running_max, weight_sum, weighted = advance(start_state)
    long_out = (
        (weighted / weight_sum[..., None])
        .astype(jnp.bfloat16)
        .reshape(LONG_DEV, local_heads * HEAD)
    )
    short_queries = queries[LONG_DEV:].reshape(short_count, local_kv, group_size, HEAD)
    short_keys = key_rows[LONG_DEV:].reshape(short_count, local_kv, HEAD)
    short_values = value_rows[LONG_DEV:].reshape(short_count, local_kv, HEAD)
    documents = segments[0]
    positions = jnp.arange(short_count, dtype=jnp.int32)
    visible = (
        (documents[None, :] == documents[:, None]) & (positions[None, :] <= positions[:, None])
    )[:, None, None, :]
    scores = (
        jnp.einsum("qgjd,kgd->qgjk", short_queries, short_keys, preferred_element_type=jnp.float32)
        * score_scale
    )
    masked = jnp.where(visible, scores, -1e30)
    row_max = jnp.max(masked, axis=-1, keepdims=True)
    weights = jnp.where(visible, jnp.exp(masked - row_max), 0.0)
    short_sum = jnp.sum(weights, axis=-1)
    mixed = jnp.einsum(
        "qgjk,kgd->qgjd",
        weights.astype(jnp.bfloat16),
        short_values,
        preferred_element_type=jnp.float32,
    )
    short_out = (
        (mixed / short_sum[..., None]).astype(jnp.bfloat16).reshape(short_count, local_heads * HEAD)
    )
    attended = jnp.concatenate([long_out, short_out], axis=0)
    rows_dev = token_count // narrow_count
    sliced = attended
    summed = lax.psum_scatter(
        rounded_term(sliced, out_weight).astype(jnp.bfloat16),
        "narrow",
        scatter_dimension=0,
        tiled=True,
    ).astype(jnp.float32)
    hidden = (residual.astype(jnp.float32) + summed).astype(jnp.bfloat16)
    widened = hidden.astype(jnp.float32)
    normed = (
        widened
        * lax.rsqrt(jnp.mean(widened * widened, axis=1, keepdims=True) + 1e-05)
        * norm_gain.astype(jnp.float32)
    ).astype(jnp.bfloat16)
    capacity = max(2, 2 * rows_dev // wide_count)
    owners = row_owner[:, 0]
    chosen = (owners[:, None] == wide_ids[None, :]).astype(jnp.int32)
    earlier = jnp.cumsum(chosen, axis=0) - chosen
    slot_index = jnp.sum(earlier * chosen, axis=1)
    target = owners * capacity + slot_index
    dispatch = (
        target[None, :] == jnp.arange(wide_count * capacity, dtype=jnp.int32)[:, None]
    ).astype(jnp.bfloat16)
    outgoing = jnp.dot(dispatch, normed, preferred_element_type=jnp.float32).astype(jnp.bfloat16)
    outgoing = outgoing.reshape(wide_count, 1, 1, capacity, normed.shape[1])
    arrived = lax.all_to_all(outgoing, "wide", split_axis=0, concat_axis=2, tiled=True)
    return (hidden, arrived)


PIECES = 8
SENDS = 4
MESH = pl.DeviceIdType.MESH


def attend_heads(q_buf, keys, values, visible, rows, out_buf, lane, local_kv, group_size):
    score_scale = HEAD ** (-0.5)
    count = rows.stop - rows.start
    tiled = jnp.concatenate([visible] * group_size, axis=0)

    def attend_group(g, carry):
        heads = [
            pl.ds(pl.multiple_of((g * group_size + j) * HEAD, HEAD), HEAD) for j in range(group_size)
        ]
        group = pl.ds(pl.multiple_of(g * HEAD, HEAD), HEAD)
        stacked = jnp.concatenate([q_buf[rows, h] for h in heads], axis=0)
        scores = (
            lax.dot_general(
                stacked, keys(group), (((1,), (1,)), ((), ())), preferred_element_type=jnp.float32
            )
            * score_scale
        )
        masked = jnp.where(tiled, scores, -1e30)
        weights = jnp.exp(masked - jnp.max(masked, axis=1, keepdims=True))
        total = jnp.sum(weights, axis=1, keepdims=True)
        mixed = jnp.dot(
            weights.astype(jnp.bfloat16), values(group), preferred_element_type=jnp.float32
        )
        mixed = (mixed / total).astype(jnp.bfloat16)
        for j, h in enumerate(heads):
            out_buf[lane, :, h] = mixed[j * count : (j + 1) * count]
        return carry

    lax.fori_loop(0, local_kv, attend_group, 0)


def fused_kernel(
    sizes,
    span_hbm,
    seg_hbm,
    owner_hbm,
    q_hbm,
    k_hbm,
    v_hbm,
    res_hbm,
    w_hbm,
    gain_hbm,
    hidden_ref,
    ffn_ref,
    q_buf,
    ks_buf,
    vs_buf,
    k_buf,
    v_buf,
    w_buf,
    res_buf,
    att_buf,
    part_buf,
    recv_buf,
    out_buf,
    gain_ref,
    span_ref,
    seg_ref,
    owner_ref,
    in_sem,
    w_sem,
    k_send,
    k_recv,
    v_send,
    v_recv,
    p_send,
    p_recv,
    o_send,
    o_recv,
    own_sem,
):
    wide_count, capacity, local_kv, group_size = sizes
    rows, model = res_hbm.shape
    piece = model // PIECES
    span = model // SENDS
    me = lax.axis_index("wide")
    lane = lax.axis_index("narrow")
    other = 1 - lane
    peers = [lax.rem(me + k, wide_count) for k in range(1, wide_count)]
    long_rows, short_rows = slice(0, rows), slice(rows, 2 * rows)

    barrier = pltpu.get_barrier_semaphore()
    for peer in peers:
        pl.semaphore_signal(barrier, inc=1, device_id={"wide": peer}, device_id_type=MESH)
    pl.semaphore_signal(barrier, inc=1, device_id={"narrow": other}, device_id_type=MESH)

    loads = [
        pltpu.make_async_copy(q_hbm.at[pl.ds(rows, rows)], q_buf.at[pl.ds(rows, rows)], in_sem.at[0]),
        pltpu.make_async_copy(k_hbm.at[pl.ds(rows, rows)], ks_buf, in_sem.at[1]),
        pltpu.make_async_copy(v_hbm.at[pl.ds(rows, rows)], vs_buf, in_sem.at[2]),
        pltpu.make_async_copy(seg_hbm, seg_ref, in_sem.at[6]),
    ]
    owner_load = pltpu.make_async_copy(owner_hbm, owner_ref, in_sem.at[7])
    gain_load = pltpu.make_async_copy(gain_hbm, gain_ref, in_sem.at[9])
    late_loads = [
        pltpu.make_async_copy(k_hbm.at[pl.ds(0, rows)], k_buf.at[me], in_sem.at[3]),
        pltpu.make_async_copy(v_hbm.at[pl.ds(0, rows)], v_buf.at[me], in_sem.at[4]),
        pltpu.make_async_copy(span_hbm, span_ref, in_sem.at[8]),
        pltpu.make_async_copy(q_hbm.at[pl.ds(0, rows)], q_buf.at[pl.ds(0, rows)], in_sem.at[10]),
    ]
    res_load = pltpu.make_async_copy(res_hbm, res_buf, in_sem.at[5])
    w_loads = [
        pltpu.make_async_copy(
            w_hbm.at[:, pl.ds(c * piece, piece)], w_buf.at[c], w_sem.at[c]
        )
        for c in range(PIECES)
    ]
    for load in loads + [owner_load] + w_loads + [res_load, gain_load] + late_loads:
        load.start()

    pl.semaphore_wait(barrier, wide_count)

    def kv_copy(source, peer):
        return [
            pltpu.make_async_remote_copy(
                src_ref=hbm.at[pl.ds(0, rows)],
                dst_ref=buf.at[source],
                send_sem=send.at[peer],
                recv_sem=recv.at[source],
                device_id={"wide": peer},
                device_id_type=MESH,
            )
            for hbm, buf, send, recv in (
                (k_hbm, k_buf, k_send, k_recv),
                (v_hbm, v_buf, v_send, v_recv),
            )
        ]

    for peer in peers:
        for copy in kv_copy(me, peer):
            copy.start()

    row_id = lax.broadcasted_iota(jnp.int32, (rows, rows), 0)
    col_id = lax.broadcasted_iota(jnp.int32, (rows, rows), 1)

    owner_load.wait()
    owner_across = jnp.broadcast_to(owner_ref[...], (rows, rows)).astype(jnp.float32)
    owner_down = owner_across.T
    same = jnp.where((owner_down == owner_across) & (row_id < col_id), 1.0, 0.0)
    slot = jnp.sum(same, axis=0, keepdims=True)
    target = (owner_across[0:1] * capacity + slot).astype(jnp.int32)
    slots = lax.broadcasted_iota(jnp.int32, (wide_count * capacity, rows), 0)
    dispatch = jnp.where(slots == target, 1.0, 0.0).astype(jnp.bfloat16)

    def part_copy(c, phase):
        return pltpu.make_async_remote_copy(
            src_ref=part_buf.at[phase, c],
            dst_ref=recv_buf.at[c],
            send_sem=p_send.at[c],
            recv_sem=p_recv.at[c],
            device_id={"narrow": other},
            device_id_type=MESH,
        )

    def project(phase, c):
        if phase == 1:
            w_loads[c].wait()
        product = jnp.dot(att_buf[phase], w_buf[c], preferred_element_type=jnp.float32)
        part_buf[phase, c] = product.astype(jnp.bfloat16)

    def lend(phase):
        for c in range(PIECES):
            project(phase, c)
            part_copy(c, phase).start()

    def out_copy(c, source, peer):
        return pltpu.make_async_remote_copy(
            src_ref=out_buf.at[c, peer],
            dst_ref=ffn_ref.at[source, :, pl.ds(pl.multiple_of(c * span, span), span)],
            send_sem=o_send.at[c, peer],
            recv_sem=o_recv.at[c, source],
            device_id={"wide": peer},
            device_id_type=MESH,
        )

    def own_copy(c):
        return pltpu.make_async_copy(
            out_buf.at[c, me],
            ffn_ref.at[me, :, pl.ds(pl.multiple_of(c * span, span), span)],
            own_sem.at[c],
        )

    def finish(phase):
        res_load.wait()
        gain_load.wait()
        squares = jnp.zeros((rows, 1), jnp.float32)
        for step in range(PIECES + 1):
            if step < PIECES:
                project(phase, step)
            if step == 0:
                continue
            c = step - 1
            part_copy(c, phase).wait_recv()
            cols = slice(c * piece, (c + 1) * piece)
            summed = part_buf[phase, c].astype(jnp.float32) + recv_buf[c].astype(jnp.float32)
            hidden = (res_buf[:, cols].astype(jnp.float32) + summed).astype(jnp.bfloat16)
            hidden_ref[:, cols] = hidden
            widened = hidden.astype(jnp.float32)
            squares += jnp.sum(widened * widened, axis=1, keepdims=True)
        factor = lax.rsqrt(squares / model + 1e-05)
        lines = span // HEAD
        for c in range(SENDS):
            cols = slice(c * span, (c + 1) * span)
            gains = gain_ref[c * lines : (c + 1) * lines, :].astype(jnp.float32)
            gain = jnp.concatenate([gains[i : i + 1] for i in range(lines)], axis=1)
            normed = (hidden_ref[:, cols].astype(jnp.float32) * factor * gain).astype(jnp.bfloat16)
            outgoing = jnp.dot(dispatch, normed, preferred_element_type=jnp.float32)
            out_buf[c] = outgoing.astype(jnp.bfloat16).reshape(wide_count, capacity, span)
            for peer in peers:
                out_copy(c, me, peer).start()
            own_copy(c).start()

    def both(phase):
        @pl.when(lane == phase)
        def _():
            finish(phase)

        @pl.when(lane != phase)
        def _():
            lend(phase)

    for load in loads:
        load.wait()
    seg_across = jnp.broadcast_to(seg_ref[...], (rows, rows)).astype(jnp.float32)
    short_visible = (seg_across == seg_across.T) & (col_id <= row_id)
    attend_heads(
        q_buf,
        lambda group: ks_buf[:, group],
        lambda group: vs_buf[:, group],
        short_visible,
        short_rows,
        att_buf,
        1,
        local_kv,
        group_size,
    )
    both(1)

    for load in late_loads:
        load.wait()
    for peer in peers:
        for copy in kv_copy(peer, peer):
            copy.wait_recv()
    spans = span_ref[...]
    wide_ids = lax.broadcasted_iota(jnp.int32, (1, wide_count), 1)
    own_span = jnp.sum(jnp.where(wide_ids == me, spans, 0), axis=1, keepdims=True)
    long_visible = jnp.concatenate(
        [
            (spans[:, b : b + 1] * rows + col_id) <= (own_span * rows + row_id)
            for b in range(wide_count)
        ],
        axis=1,
    )
    attend_heads(
        q_buf,
        lambda group: k_buf[:, :, group].reshape(wide_count * rows, HEAD),
        lambda group: v_buf[:, :, group].reshape(wide_count * rows, HEAD),
        long_visible,
        long_rows,
        att_buf,
        0,
        local_kv,
        group_size,
    )
    both(0)

    for peer in peers:
        for copy in kv_copy(me, peer):
            copy.wait_send()

    def drain_parts(c, carry):
        part_copy(c, 0).wait_send()
        return carry

    lax.fori_loop(0, PIECES, drain_parts, 0)

    def drain_sends(c, carry):
        for peer in peers:
            out_copy(c, me, peer).wait_send()
            out_copy(c, peer, peer).wait_recv()
        own_copy(c).wait()
        return carry

    lax.fori_loop(0, SENDS, drain_sends, 0)


def store_kernel(hidden_ref, ffn_ref, hidden_out, ffn_out, sems):
    parts = ffn_ref.shape[0]
    count = hidden_ref.shape[0] // parts
    half = ffn_ref.shape[1] // 2
    copies = []
    for s in range(parts):
        some = pl.ds(s * count, count)
        copies.append(
            pltpu.make_async_copy(hidden_ref.at[some], hidden_out.at[some], sems.at[3 * s])
        )
        for j in range(2):
            some = pl.ds(j * half, half)
            copies.append(
                pltpu.make_async_copy(
                    ffn_ref.at[s, some], ffn_out.at[s, some], sems.at[3 * s + 1 + j]
                )
            )
    for copy in copies:
        copy.start()
    for copy in copies:
        copy.wait()


def fused_on_device(
    queries, key_rows, value_rows, residual, out_weight, norm_gain, span_map, segments, row_owner
):
    wide_count = lax.axis_size("wide")
    local_heads = queries.shape[1] // HEAD
    local_kv = key_rows.shape[1] // HEAD
    rows, model = residual.shape
    capacity = max(2, 2 * rows // wide_count)
    sizes = (wide_count, capacity, local_kv, local_heads // local_kv)
    bf16 = jnp.bfloat16
    dma = pltpu.SemaphoreType.DMA
    any_spec = pl.BlockSpec(memory_space=pl.ANY)
    vmem_spec = pl.BlockSpec(memory_space=pltpu.VMEM)
    piece, span = model // PIECES, model // SENDS
    hidden, arrived = pl.pallas_call(
        functools.partial(fused_kernel, sizes),
        out_shape=(
            pltpu.VMEM((rows, model), bf16),
            pltpu.VMEM((wide_count, capacity, model), bf16),
        ),
        in_specs=[any_spec] * 9,
        out_specs=(vmem_spec, vmem_spec),
        scratch_shapes=[
            pltpu.VMEM(queries.shape, bf16),
            pltpu.VMEM((rows, key_rows.shape[1]), bf16),
            pltpu.VMEM((rows, key_rows.shape[1]), bf16),
            pltpu.VMEM((wide_count, rows, key_rows.shape[1]), bf16),
            pltpu.VMEM((wide_count, rows, key_rows.shape[1]), bf16),
            pltpu.VMEM((PIECES, out_weight.shape[0], piece), bf16),
            pltpu.VMEM((rows, model), bf16),
            pltpu.VMEM((2, rows, queries.shape[1]), bf16),
            pltpu.VMEM((2, PIECES, rows, piece), bf16),
            pltpu.VMEM((PIECES, rows, piece), bf16),
            pltpu.VMEM((SENDS, wide_count, capacity, span), bf16),
            pltpu.VMEM((model // HEAD, HEAD), bf16),
            pltpu.VMEM((1, wide_count), jnp.int32),
            pltpu.VMEM((1, rows), jnp.int32),
            pltpu.VMEM((1, rows), jnp.int32),
            dma((11,)),
            dma((PIECES,)),
            dma((wide_count,)),
            dma((wide_count,)),
            dma((wide_count,)),
            dma((wide_count,)),
            dma((PIECES,)),
            dma((PIECES,)),
            dma((SENDS, wide_count)),
            dma((SENDS, wide_count)),
            dma((SENDS,)),
        ],
        compiler_params=pltpu.CompilerParams(
            collective_id=0, has_side_effects=True, vmem_limit_bytes=60 * 1024 * 1024
        ),
    )(
        span_map.reshape(1, wide_count),
        segments,
        row_owner.reshape(1, rows),
        queries,
        key_rows,
        value_rows,
        residual,
        out_weight,
        norm_gain.reshape(model // HEAD, HEAD),
    )
    hidden, arrived = pl.pallas_call(
        store_kernel,
        out_shape=(
            jax.ShapeDtypeStruct(hidden.shape, bf16),
            jax.ShapeDtypeStruct(arrived.shape, bf16),
        ),
        in_specs=[any_spec] * 2,
        out_specs=(any_spec, any_spec),
        scratch_shapes=[dma((3 * wide_count,))],
        compiler_params=pltpu.CompilerParams(vmem_limit_bytes=1024 * 1024),
    )(hidden, arrived)
    return hidden, arrived.reshape(1, 1, wide_count, capacity, model)


def on_device(*args):
    queries, residual = args[0], args[3]
    rows, model = residual.shape
    wide_count = lax.axis_size("wide")
    fits = (
        lax.axis_size("narrow") == 2
        and rows == LONG_DEV
        and queries.shape[0] == 2 * LONG_DEV
        and (2 * rows) % (32 * wide_count) == 0
        and rows % (16 * wide_count) == 0
        and model % (PIECES * HEAD) == 0
    )
    return (fused_on_device if fits else general_on_device)(*args)


def solution(mesh):
    placed = (
        P(("rep", "wide"), "narrow"),
        P(("rep", "wide"), "narrow"),
        P(("rep", "wide"), "narrow"),
        P(("rep", "wide", "narrow"), None),
        P("narrow", None),
        P(),
        P(),
        P(("rep", "wide"), None),
        P(("rep", "wide", "narrow"), None),
    )
    return jax.shard_map(
        on_device,
        mesh=mesh,
        in_specs=placed,
        out_specs=(
            P(("rep", "wide", "narrow"), None),
            P(("rep", "wide"), "narrow", None, None, None),
        ),
        check_vma=False,
    )
```

```python
import functools

import jax
import jax.numpy as jnp
from jax import lax
from jax.experimental import pallas as pl
from jax.experimental.pallas import tpu as pltpu
from jax.sharding import PartitionSpec as P

HEAD = 128
LONG_DEV = 128


def attend_block(
    partial_state, long_queries, key_block, value_block, key_pos, query_pos, score_scale
):
    running_max, weight_sum, weighted = partial_state
    scores = (
        jnp.einsum("qgjd,kgd->qgjk", long_queries, key_block, preferred_element_type=jnp.float32)
        * score_scale
    )
    visible = (key_pos[None, :] <= query_pos[:, None])[:, None, None, :]
    masked = jnp.where(visible, scores, -1e30)
    newest = jnp.maximum(running_max, jnp.max(masked, axis=-1))
    weights = jnp.where(visible, jnp.exp(masked - newest[..., None]), 0.0)
    factor = jnp.exp(running_max - newest)
    weight_sum = weight_sum * factor + jnp.sum(weights, axis=-1)
    weighted = weighted * factor[..., None] + jnp.einsum(
        "qgjk,kgd->qgjd",
        weights.astype(jnp.bfloat16),
        value_block,
        preferred_element_type=jnp.float32,
    )
    return (newest, weight_sum, weighted)


def rounded_term(attended, out_weight):
    product = jnp.dot(attended, out_weight, preferred_element_type=jnp.float32)
    return lax.optimization_barrier(product.astype(jnp.bfloat16)).astype(jnp.float32)


def general_on_device(
    queries, key_rows, value_rows, residual, out_weight, norm_gain, span_map, segments, row_owner
):
    wide_count = lax.axis_size("wide")
    narrow_count = lax.axis_size("narrow")
    wide_index = lax.axis_index("wide")
    local_heads = queries.shape[1] // HEAD
    local_kv = key_rows.shape[1] // HEAD
    group_size = local_heads // local_kv
    token_count = queries.shape[0]
    short_count = token_count - LONG_DEV
    score_scale = HEAD ** (-0.5)
    own_span = lax.dynamic_slice_in_dim(span_map, wide_index, 1, 0)[0]
    query_pos = own_span * LONG_DEV + jnp.arange(LONG_DEV, dtype=jnp.int32)
    long_queries = queries[:LONG_DEV].reshape(LONG_DEV, local_kv, group_size, HEAD)
    wide_ids = jnp.arange(wide_count, dtype=jnp.int32)
    start_state = (
        jnp.full((LONG_DEV, local_kv, group_size), -1e30, jnp.float32),
        jnp.zeros((LONG_DEV, local_kv, group_size), jnp.float32),
        jnp.zeros((LONG_DEV, local_kv, group_size, HEAD), jnp.float32),
    )
    key_piece = lax.all_gather(key_rows[:LONG_DEV], "wide", axis=0, tiled=True)
    value_piece = lax.all_gather(value_rows[:LONG_DEV], "wide", axis=0, tiled=True)
    row_count = key_piece.shape[0]
    key_index = jnp.arange(row_count, dtype=jnp.int32)
    holder = key_index // LONG_DEV
    span_of = jnp.sum(jnp.where(holder[:, None] == wide_ids[None, :], span_map[None, :], 0), axis=1)
    key_pos = span_of * LONG_DEV + key_index % LONG_DEV
    key_block = key_piece.reshape(row_count, local_kv, HEAD)
    value_block = value_piece.reshape(row_count, local_kv, HEAD)

    def advance(partial_state):
        if row_count > 512 and row_count % 512 == 0:
            splits = row_count // 512

            def advance_block(inner_state, sliced):
                return (
                    attend_block(
                        inner_state,
                        long_queries,
                        sliced[0],
                        sliced[1],
                        sliced[2],
                        query_pos,
                        score_scale,
                    ),
                    None,
                )

            finished, unused = lax.scan(
                advance_block,
                partial_state,
                (
                    key_block.reshape(splits, 512, local_kv, HEAD),
                    value_block.reshape(splits, 512, local_kv, HEAD),
                    key_pos.reshape(splits, 512),
                ),
            )
            return finished
        return attend_block(
            partial_state, long_queries, key_block, value_block, key_pos, query_pos, score_scale
        )

    running_max, weight_sum, weighted = advance(start_state)
    long_out = (
        (weighted / weight_sum[..., None])
        .astype(jnp.bfloat16)
        .reshape(LONG_DEV, local_heads * HEAD)
    )
    short_queries = queries[LONG_DEV:].reshape(short_count, local_kv, group_size, HEAD)
    short_keys = key_rows[LONG_DEV:].reshape(short_count, local_kv, HEAD)
    short_values = value_rows[LONG_DEV:].reshape(short_count, local_kv, HEAD)
    documents = segments[0]
    positions = jnp.arange(short_count, dtype=jnp.int32)
    visible = (
        (documents[None, :] == documents[:, None]) & (positions[None, :] <= positions[:, None])
    )[:, None, None, :]
    scores = (
        jnp.einsum("qgjd,kgd->qgjk", short_queries, short_keys, preferred_element_type=jnp.float32)
        * score_scale
    )
    masked = jnp.where(visible, scores, -1e30)
    row_max = jnp.max(masked, axis=-1, keepdims=True)
    weights = jnp.where(visible, jnp.exp(masked - row_max), 0.0)
    short_sum = jnp.sum(weights, axis=-1)
    mixed = jnp.einsum(
        "qgjk,kgd->qgjd",
        weights.astype(jnp.bfloat16),
        short_values,
        preferred_element_type=jnp.float32,
    )
    short_out = (
        (mixed / short_sum[..., None]).astype(jnp.bfloat16).reshape(short_count, local_heads * HEAD)
    )
    attended = jnp.concatenate([long_out, short_out], axis=0)
    rows_dev = token_count // narrow_count
    sliced = attended
    summed = lax.psum_scatter(
        rounded_term(sliced, out_weight).astype(jnp.bfloat16),
        "narrow",
        scatter_dimension=0,
        tiled=True,
    ).astype(jnp.float32)
    hidden = (residual.astype(jnp.float32) + summed).astype(jnp.bfloat16)
    widened = hidden.astype(jnp.float32)
    normed = (
        widened
        * lax.rsqrt(jnp.mean(widened * widened, axis=1, keepdims=True) + 1e-05)
        * norm_gain.astype(jnp.float32)
    ).astype(jnp.bfloat16)
    capacity = max(2, 2 * rows_dev // wide_count)
    owners = row_owner[:, 0]
    chosen = (owners[:, None] == wide_ids[None, :]).astype(jnp.int32)
    earlier = jnp.cumsum(chosen, axis=0) - chosen
    slot_index = jnp.sum(earlier * chosen, axis=1)
    target = owners * capacity + slot_index
    dispatch = (
        target[None, :] == jnp.arange(wide_count * capacity, dtype=jnp.int32)[:, None]
    ).astype(jnp.bfloat16)
    outgoing = jnp.dot(dispatch, normed, preferred_element_type=jnp.float32).astype(jnp.bfloat16)
    outgoing = outgoing.reshape(wide_count, 1, 1, capacity, normed.shape[1])
    arrived = lax.all_to_all(outgoing, "wide", split_axis=0, concat_axis=2, tiled=True)
    return (hidden, arrived)


PIECES = 8
SENDS = 4
MESH = pl.DeviceIdType.MESH


def attend_heads(q_buf, keys, values, visible, rows, out_buf, lane, local_kv, group_size, unroll):
    score_scale = HEAD ** (-0.5)
    count = rows.stop - rows.start
    tiled = jnp.concatenate([visible] * group_size, axis=0)

    def attend_group(g, carry):
        heads = [
            pl.ds(pl.multiple_of((g * group_size + j) * HEAD, HEAD), HEAD) for j in range(group_size)
        ]
        group = pl.ds(pl.multiple_of(g * HEAD, HEAD), HEAD)
        stacked = jnp.concatenate([q_buf[rows, h] for h in heads], axis=0)
        scores = (
            lax.dot_general(
                stacked, keys(group), (((1,), (1,)), ((), ())), preferred_element_type=jnp.float32
            )
            * score_scale
        )
        masked = jnp.where(tiled, scores, -1e30)
        weights = jnp.exp(masked - jnp.max(masked, axis=1, keepdims=True))
        total = jnp.sum(weights, axis=1, keepdims=True)
        mixed = jnp.dot(
            weights.astype(jnp.bfloat16), values(group), preferred_element_type=jnp.float32
        )
        mixed = (mixed / total).astype(jnp.bfloat16)
        for j, h in enumerate(heads):
            out_buf[lane, :, h] = mixed[j * count : (j + 1) * count]
        return carry

    lax.fori_loop(0, local_kv, attend_group, 0, unroll=unroll)


def fused_kernel(
    sizes,
    span_hbm,
    seg_hbm,
    owner_hbm,
    q_hbm,
    k_hbm,
    v_hbm,
    res_hbm,
    w_hbm,
    gain_hbm,
    hidden_ref,
    ffn_ref,
    q_buf,
    ks_buf,
    vs_buf,
    k_buf,
    v_buf,
    w_buf,
    res_buf,
    att_buf,
    part_buf,
    recv_buf,
    out_buf,
    gain_ref,
    span_ref,
    seg_ref,
    owner_ref,
    in_sem,
    w_sem,
    kv_send,
    kv_recv,
    p_send,
    p_recv,
    o_send,
    o_recv,
    own_sem,
):
    wide_count, capacity, local_kv, group_size = sizes
    rows, model = res_hbm.shape
    piece = model // PIECES
    span = model // SENDS
    me = lax.axis_index("wide")
    lane = lax.axis_index("narrow")
    other = 1 - lane
    along, across = lax.rem(me, 2), me // 2
    near = [across * 2 + 1 - along, (1 - across) * 2 + along]
    far = (1 - across) * 2 + 1 - along
    peers = [far] + near
    long_rows, short_rows = slice(0, rows), slice(rows, 2 * rows)

    barrier = pltpu.get_barrier_semaphore()
    for peer in peers:
        pl.semaphore_signal(barrier, inc=1, device_id={"wide": peer}, device_id_type=MESH)
    pl.semaphore_signal(barrier, inc=1, device_id={"narrow": other}, device_id_type=MESH)

    loads = [
        pltpu.make_async_copy(q_hbm.at[pl.ds(rows, rows)], q_buf.at[pl.ds(rows, rows)], in_sem.at[0]),
        pltpu.make_async_copy(k_hbm.at[pl.ds(rows, rows)], ks_buf, in_sem.at[1]),
        pltpu.make_async_copy(v_hbm.at[pl.ds(rows, rows)], vs_buf, in_sem.at[2]),
    ]
    seg_load = pltpu.make_async_copy(seg_hbm, seg_ref, in_sem.at[6])
    owner_load = pltpu.make_async_copy(owner_hbm, owner_ref, in_sem.at[7])
    gain_load = pltpu.make_async_copy(gain_hbm, gain_ref, in_sem.at[9])
    late_loads = [
        pltpu.make_async_copy(k_hbm.at[pl.ds(0, rows)], k_buf.at[me], in_sem.at[3]),
        pltpu.make_async_copy(v_hbm.at[pl.ds(0, rows)], v_buf.at[me], in_sem.at[4]),
        pltpu.make_async_copy(span_hbm, span_ref, in_sem.at[8]),
        pltpu.make_async_copy(q_hbm.at[pl.ds(0, rows)], q_buf.at[pl.ds(0, rows)], in_sem.at[10]),
    ]
    res_load = pltpu.make_async_copy(res_hbm, res_buf, in_sem.at[5])
    w_loads = [
        pltpu.make_async_copy(
            w_hbm.at[:, pl.ds(c * piece, piece)], w_buf.at[c], w_sem.at[c]
        )
        for c in range(PIECES)
    ]
    for load in [owner_load, seg_load] + loads + w_loads + [res_load, gain_load] + late_loads:
        load.start()

    def kv_copy(i, source, peer, first, sem):
        hbm, buf = ((k_hbm, k_buf), (v_hbm, v_buf))[i]
        return pltpu.make_async_remote_copy(
            src_ref=hbm.at[pl.ds(0, rows)] if first else buf.at[source],
            dst_ref=buf.at[source],
            send_sem=kv_send.at[i, sem],
            recv_sem=kv_recv.at[i, source],
            device_id={"wide": peer},
            device_id_type=MESH,
        )

    kv_first = [kv_copy(i, me, near[j], True, j) for i in range(2) for j in range(2)]
    kv_forward = [kv_copy(i, near[i], near[1 - i], False, 2) for i in range(2)]

    def pass_on(i):
        kv_copy(i, near[i], near[i], True, i).wait_recv()
        kv_forward[i].start()

    row_id = lax.broadcasted_iota(jnp.int32, (rows, rows), 0)
    col_id = lax.broadcasted_iota(jnp.int32, (rows, rows), 1)

    owner_load.wait()
    owner_across = jnp.broadcast_to(owner_ref[...], (rows, rows)).astype(jnp.float32)
    owner_down = owner_across.T
    same = jnp.where((owner_down == owner_across) & (row_id < col_id), 1.0, 0.0)
    slot = jnp.sum(same, axis=0, keepdims=True)
    target = (owner_across[0:1] * capacity + slot).astype(jnp.int32)
    slots = lax.broadcasted_iota(jnp.int32, (wide_count * capacity, rows), 0)
    dispatch = jnp.where(slots == target, 1.0, 0.0).astype(jnp.bfloat16)

    seg_load.wait()
    seg_across = jnp.broadcast_to(seg_ref[...], (rows, rows)).astype(jnp.float32)
    short_visible = (seg_across == seg_across.T) & (col_id <= row_id)

    pl.semaphore_wait(barrier, wide_count)
    for copy in kv_first:
        copy.start()

    def part_copy(c, phase):
        return pltpu.make_async_remote_copy(
            src_ref=part_buf.at[phase, c],
            dst_ref=recv_buf.at[c],
            send_sem=p_send.at[c],
            recv_sem=p_recv.at[c],
            device_id={"narrow": other},
            device_id_type=MESH,
        )

    def project(phase, c):
        if phase == 1:
            w_loads[c].wait()
            if c == 2:
                pass_on(0)
            if c == 6:
                pass_on(1)
        product = jnp.dot(att_buf[phase], w_buf[c], preferred_element_type=jnp.float32)
        part_buf[phase, c] = product.astype(jnp.bfloat16)

    def lend(phase):
        for c in range(PIECES):
            project(phase, c)
            part_copy(c, phase).start()

    def out_copy(c, source, peer):
        return pltpu.make_async_remote_copy(
            src_ref=out_buf.at[c, peer],
            dst_ref=ffn_ref.at[source, :, pl.ds(pl.multiple_of(c * span, span), span)],
            send_sem=o_send.at[c, peer],
            recv_sem=o_recv.at[c, source],
            device_id={"wide": peer},
            device_id_type=MESH,
        )

    def own_copy(c):
        return pltpu.make_async_copy(
            out_buf.at[c, me],
            ffn_ref.at[me, :, pl.ds(pl.multiple_of(c * span, span), span)],
            own_sem.at[c],
        )

    def finish(phase):
        res_load.wait()
        gain_load.wait()
        squares = jnp.zeros((rows, 1), jnp.float32)
        for step in range(PIECES + 1):
            if step < PIECES:
                project(phase, step)
            if step == 0:
                continue
            c = step - 1
            part_copy(c, phase).wait_recv()
            cols = slice(c * piece, (c + 1) * piece)
            summed = part_buf[phase, c].astype(jnp.float32) + recv_buf[c].astype(jnp.float32)
            hidden = (res_buf[:, cols].astype(jnp.float32) + summed).astype(jnp.bfloat16)
            hidden_ref[:, cols] = hidden
            widened = hidden.astype(jnp.float32)
            squares += jnp.sum(widened * widened, axis=1, keepdims=True)
        factor = lax.rsqrt(squares / model + 1e-05)
        lines = span // HEAD
        for c in range(SENDS):
            cols = slice(c * span, (c + 1) * span)
            gains = gain_ref[c * lines : (c + 1) * lines, :].astype(jnp.float32)
            gain = jnp.concatenate([gains[i : i + 1] for i in range(lines)], axis=1)
            normed = (hidden_ref[:, cols].astype(jnp.float32) * factor * gain).astype(jnp.bfloat16)
            outgoing = jnp.dot(dispatch, normed, preferred_element_type=jnp.float32)
            out_buf[c] = outgoing.astype(jnp.bfloat16).reshape(wide_count, capacity, span)
            for peer in peers:
                out_copy(c, me, peer).start()
            own_copy(c).start()

    def both(phase):
        @pl.when(lane == phase)
        def _():
            finish(phase)

        @pl.when(lane != phase)
        def _():
            lend(phase)

    for load in loads:
        load.wait()
    attend_heads(
        q_buf,
        lambda group: ks_buf[:, group],
        lambda group: vs_buf[:, group],
        short_visible,
        short_rows,
        att_buf,
        1,
        local_kv,
        group_size,
        True,
    )
    both(1)

    for load in late_loads:
        load.wait()
    kv_copy(0, near[1], near[1], True, 1).wait_recv()
    kv_copy(1, near[0], near[0], True, 0).wait_recv()
    for i in range(2):
        kv_copy(i, far, near[1 - i], False, 2).wait_recv()
    spans = span_ref[...]
    wide_ids = lax.broadcasted_iota(jnp.int32, (1, wide_count), 1)
    own_span = jnp.sum(jnp.where(wide_ids == me, spans, 0), axis=1, keepdims=True)
    long_visible = jnp.concatenate(
        [
            (spans[:, b : b + 1] * rows + col_id) <= (own_span * rows + row_id)
            for b in range(wide_count)
        ],
        axis=1,
    )
    attend_heads(
        q_buf,
        lambda group: k_buf[:, :, group].reshape(wide_count * rows, HEAD),
        lambda group: v_buf[:, :, group].reshape(wide_count * rows, HEAD),
        long_visible,
        long_rows,
        att_buf,
        0,
        local_kv,
        group_size,
        False,
    )
    both(0)

    for copy in kv_first + kv_forward:
        copy.wait_send()

    def drain_parts(c, carry):
        part_copy(c, 0).wait_send()
        return carry

    lax.fori_loop(0, PIECES, drain_parts, 0)

    def drain_sends(c, carry):
        for peer in peers:
            out_copy(c, me, peer).wait_send()
            out_copy(c, peer, peer).wait_recv()
        own_copy(c).wait()
        return carry

    lax.fori_loop(0, SENDS, drain_sends, 0)


def store_kernel(hidden_ref, ffn_ref, hidden_out, ffn_out, sems):
    parts = ffn_ref.shape[0]
    count = hidden_ref.shape[0] // parts
    half = ffn_ref.shape[1] // 2
    copies = []
    for s in range(parts):
        some = pl.ds(s * count, count)
        copies.append(
            pltpu.make_async_copy(hidden_ref.at[some], hidden_out.at[some], sems.at[3 * s])
        )
        for j in range(2):
            some = pl.ds(j * half, half)
            copies.append(
                pltpu.make_async_copy(
                    ffn_ref.at[s, some], ffn_out.at[s, some], sems.at[3 * s + 1 + j]
                )
            )
    for copy in copies:
        copy.start()
    for copy in copies:
        copy.wait()


def fused_on_device(
    queries, key_rows, value_rows, residual, out_weight, norm_gain, span_map, segments, row_owner
):
    wide_count = lax.axis_size("wide")
    local_heads = queries.shape[1] // HEAD
    local_kv = key_rows.shape[1] // HEAD
    rows, model = residual.shape
    capacity = max(2, 2 * rows // wide_count)
    sizes = (wide_count, capacity, local_kv, local_heads // local_kv)
    bf16 = jnp.bfloat16
    dma = pltpu.SemaphoreType.DMA
    any_spec = pl.BlockSpec(memory_space=pl.ANY)
    vmem_spec = pl.BlockSpec(memory_space=pltpu.VMEM)
    piece, span = model // PIECES, model // SENDS
    hidden, arrived = pl.pallas_call(
        functools.partial(fused_kernel, sizes),
        out_shape=(
            pltpu.VMEM((rows, model), bf16),
            pltpu.VMEM((wide_count, capacity, model), bf16),
        ),
        in_specs=[any_spec] * 9,
        out_specs=(vmem_spec, vmem_spec),
        scratch_shapes=[
            pltpu.VMEM(queries.shape, bf16),
            pltpu.VMEM((rows, key_rows.shape[1]), bf16),
            pltpu.VMEM((rows, key_rows.shape[1]), bf16),
            pltpu.VMEM((wide_count, rows, key_rows.shape[1]), bf16),
            pltpu.VMEM((wide_count, rows, key_rows.shape[1]), bf16),
            pltpu.VMEM((PIECES, out_weight.shape[0], piece), bf16),
            pltpu.VMEM((rows, model), bf16),
            pltpu.VMEM((2, rows, queries.shape[1]), bf16),
            pltpu.VMEM((2, PIECES, rows, piece), bf16),
            pltpu.VMEM((PIECES, rows, piece), bf16),
            pltpu.VMEM((SENDS, wide_count, capacity, span), bf16),
            pltpu.VMEM((model // HEAD, HEAD), bf16),
            pltpu.VMEM((1, wide_count), jnp.int32),
            pltpu.VMEM((1, rows), jnp.int32),
            pltpu.VMEM((1, rows), jnp.int32),
            dma((11,)),
            dma((PIECES,)),
            dma((2, 3)),
            dma((2, wide_count)),
            dma((PIECES,)),
            dma((PIECES,)),
            dma((SENDS, wide_count)),
            dma((SENDS, wide_count)),
            dma((SENDS,)),
        ],
        compiler_params=pltpu.CompilerParams(
            collective_id=0, has_side_effects=True, vmem_limit_bytes=60 * 1024 * 1024
        ),
    )(
        span_map.reshape(1, wide_count),
        segments,
        row_owner.reshape(1, rows),
        queries,
        key_rows,
        value_rows,
        residual,
        out_weight,
        norm_gain.reshape(model // HEAD, HEAD),
    )
    hidden, arrived = pl.pallas_call(
        store_kernel,
        out_shape=(
            jax.ShapeDtypeStruct(hidden.shape, bf16),
            jax.ShapeDtypeStruct(arrived.shape, bf16),
        ),
        in_specs=[any_spec] * 2,
        out_specs=(any_spec, any_spec),
        scratch_shapes=[dma((3 * wide_count,))],
        compiler_params=pltpu.CompilerParams(vmem_limit_bytes=1024 * 1024),
    )(hidden, arrived)
    return hidden, arrived.reshape(1, 1, wide_count, capacity, model)


def on_device(*args):
    queries, residual = args[0], args[3]
    rows, model = residual.shape
    wide_count = lax.axis_size("wide")
    fits = (
        lax.axis_size("narrow") == 2
        and rows == LONG_DEV
        and queries.shape[0] == 2 * LONG_DEV
        and wide_count == 4
        and (2 * rows) % (32 * wide_count) == 0
        and rows % (16 * wide_count) == 0
        and model % (PIECES * HEAD) == 0
    )
    return (fused_on_device if fits else general_on_device)(*args)


def solution(mesh):
    placed = (
        P(("rep", "wide"), "narrow"),
        P(("rep", "wide"), "narrow"),
        P(("rep", "wide"), "narrow"),
        P(("rep", "wide", "narrow"), None),
        P("narrow", None),
        P(),
        P(),
        P(("rep", "wide"), None),
        P(("rep", "wide", "narrow"), None),
    )
    return jax.shard_map(
        on_device,
        mesh=mesh,
        in_specs=placed,
        out_specs=(
            P(("rep", "wide", "narrow"), None),
            P(("rep", "wide"), "narrow", None, None, None),
        ),
        check_vma=False,
    )
```

```python
import functools

import jax
import jax.numpy as jnp
from jax import lax
from jax.experimental import pallas as pl
from jax.experimental.pallas import tpu as pltpu
from jax.sharding import PartitionSpec as P

HEAD = 128
LONG_DEV = 128


def attend_block(
    partial_state, long_queries, key_block, value_block, key_pos, query_pos, score_scale
):
    running_max, weight_sum, weighted = partial_state
    scores = (
        jnp.einsum("qgjd,kgd->qgjk", long_queries, key_block, preferred_element_type=jnp.float32)
        * score_scale
    )
    visible = (key_pos[None, :] <= query_pos[:, None])[:, None, None, :]
    masked = jnp.where(visible, scores, -1e30)
    newest = jnp.maximum(running_max, jnp.max(masked, axis=-1))
    weights = jnp.where(visible, jnp.exp(masked - newest[..., None]), 0.0)
    factor = jnp.exp(running_max - newest)
    weight_sum = weight_sum * factor + jnp.sum(weights, axis=-1)
    weighted = weighted * factor[..., None] + jnp.einsum(
        "qgjk,kgd->qgjd",
        weights.astype(jnp.bfloat16),
        value_block,
        preferred_element_type=jnp.float32,
    )
    return (newest, weight_sum, weighted)


def rounded_term(attended, out_weight):
    product = jnp.dot(attended, out_weight, preferred_element_type=jnp.float32)
    return lax.optimization_barrier(product.astype(jnp.bfloat16)).astype(jnp.float32)


def general_on_device(
    queries, key_rows, value_rows, residual, out_weight, norm_gain, span_map, segments, row_owner
):
    wide_count = lax.axis_size("wide")
    narrow_count = lax.axis_size("narrow")
    wide_index = lax.axis_index("wide")
    local_heads = queries.shape[1] // HEAD
    local_kv = key_rows.shape[1] // HEAD
    group_size = local_heads // local_kv
    token_count = queries.shape[0]
    short_count = token_count - LONG_DEV
    score_scale = HEAD ** (-0.5)
    own_span = lax.dynamic_slice_in_dim(span_map, wide_index, 1, 0)[0]
    query_pos = own_span * LONG_DEV + jnp.arange(LONG_DEV, dtype=jnp.int32)
    long_queries = queries[:LONG_DEV].reshape(LONG_DEV, local_kv, group_size, HEAD)
    wide_ids = jnp.arange(wide_count, dtype=jnp.int32)
    start_state = (
        jnp.full((LONG_DEV, local_kv, group_size), -1e30, jnp.float32),
        jnp.zeros((LONG_DEV, local_kv, group_size), jnp.float32),
        jnp.zeros((LONG_DEV, local_kv, group_size, HEAD), jnp.float32),
    )
    key_piece = lax.all_gather(key_rows[:LONG_DEV], "wide", axis=0, tiled=True)
    value_piece = lax.all_gather(value_rows[:LONG_DEV], "wide", axis=0, tiled=True)
    row_count = key_piece.shape[0]
    key_index = jnp.arange(row_count, dtype=jnp.int32)
    holder = key_index // LONG_DEV
    span_of = jnp.sum(jnp.where(holder[:, None] == wide_ids[None, :], span_map[None, :], 0), axis=1)
    key_pos = span_of * LONG_DEV + key_index % LONG_DEV
    key_block = key_piece.reshape(row_count, local_kv, HEAD)
    value_block = value_piece.reshape(row_count, local_kv, HEAD)

    def advance(partial_state):
        if row_count > 512 and row_count % 512 == 0:
            splits = row_count // 512

            def advance_block(inner_state, sliced):
                return (
                    attend_block(
                        inner_state,
                        long_queries,
                        sliced[0],
                        sliced[1],
                        sliced[2],
                        query_pos,
                        score_scale,
                    ),
                    None,
                )

            finished, unused = lax.scan(
                advance_block,
                partial_state,
                (
                    key_block.reshape(splits, 512, local_kv, HEAD),
                    value_block.reshape(splits, 512, local_kv, HEAD),
                    key_pos.reshape(splits, 512),
                ),
            )
            return finished
        return attend_block(
            partial_state, long_queries, key_block, value_block, key_pos, query_pos, score_scale
        )

    running_max, weight_sum, weighted = advance(start_state)
    long_out = (
        (weighted / weight_sum[..., None])
        .astype(jnp.bfloat16)
        .reshape(LONG_DEV, local_heads * HEAD)
    )
    short_queries = queries[LONG_DEV:].reshape(short_count, local_kv, group_size, HEAD)
    short_keys = key_rows[LONG_DEV:].reshape(short_count, local_kv, HEAD)
    short_values = value_rows[LONG_DEV:].reshape(short_count, local_kv, HEAD)
    documents = segments[0]
    positions = jnp.arange(short_count, dtype=jnp.int32)
    visible = (
        (documents[None, :] == documents[:, None]) & (positions[None, :] <= positions[:, None])
    )[:, None, None, :]
    scores = (
        jnp.einsum("qgjd,kgd->qgjk", short_queries, short_keys, preferred_element_type=jnp.float32)
        * score_scale
    )
    masked = jnp.where(visible, scores, -1e30)
    row_max = jnp.max(masked, axis=-1, keepdims=True)
    weights = jnp.where(visible, jnp.exp(masked - row_max), 0.0)
    short_sum = jnp.sum(weights, axis=-1)
    mixed = jnp.einsum(
        "qgjk,kgd->qgjd",
        weights.astype(jnp.bfloat16),
        short_values,
        preferred_element_type=jnp.float32,
    )
    short_out = (
        (mixed / short_sum[..., None]).astype(jnp.bfloat16).reshape(short_count, local_heads * HEAD)
    )
    attended = jnp.concatenate([long_out, short_out], axis=0)
    rows_dev = token_count // narrow_count
    sliced = attended
    summed = lax.psum_scatter(
        rounded_term(sliced, out_weight).astype(jnp.bfloat16),
        "narrow",
        scatter_dimension=0,
        tiled=True,
    ).astype(jnp.float32)
    hidden = (residual.astype(jnp.float32) + summed).astype(jnp.bfloat16)
    widened = hidden.astype(jnp.float32)
    normed = (
        widened
        * lax.rsqrt(jnp.mean(widened * widened, axis=1, keepdims=True) + 1e-05)
        * norm_gain.astype(jnp.float32)
    ).astype(jnp.bfloat16)
    capacity = max(2, 2 * rows_dev // wide_count)
    owners = row_owner[:, 0]
    chosen = (owners[:, None] == wide_ids[None, :]).astype(jnp.int32)
    earlier = jnp.cumsum(chosen, axis=0) - chosen
    slot_index = jnp.sum(earlier * chosen, axis=1)
    target = owners * capacity + slot_index
    dispatch = (
        target[None, :] == jnp.arange(wide_count * capacity, dtype=jnp.int32)[:, None]
    ).astype(jnp.bfloat16)
    outgoing = jnp.dot(dispatch, normed, preferred_element_type=jnp.float32).astype(jnp.bfloat16)
    outgoing = outgoing.reshape(wide_count, 1, 1, capacity, normed.shape[1])
    arrived = lax.all_to_all(outgoing, "wide", split_axis=0, concat_axis=2, tiled=True)
    return (hidden, arrived)


PIECES = 8
SENDS = 4
EARLY = 3
MESH = pl.DeviceIdType.MESH


def attend_heads(q_buf, keys, values, visible, rows, out_buf, lane, local_kv, group_size):
    score_scale = HEAD ** (-0.5)
    count = rows.stop - rows.start
    tiled = jnp.concatenate([visible] * group_size, axis=0)

    def attend_group(g, carry):
        heads = [
            pl.ds(pl.multiple_of((g * group_size + j) * HEAD, HEAD), HEAD) for j in range(group_size)
        ]
        group = pl.ds(pl.multiple_of(g * HEAD, HEAD), HEAD)
        stacked = jnp.concatenate([q_buf[rows, h] for h in heads], axis=0)
        scores = (
            lax.dot_general(
                stacked, keys(group), (((1,), (1,)), ((), ())), preferred_element_type=jnp.float32
            )
            * score_scale
        )
        masked = jnp.where(tiled, scores, -1e30)
        weights = jnp.exp(masked - jnp.max(masked, axis=1, keepdims=True))
        total = jnp.sum(weights, axis=1, keepdims=True)
        mixed = jnp.dot(
            weights.astype(jnp.bfloat16), values(group), preferred_element_type=jnp.float32
        )
        mixed = (mixed / total).astype(jnp.bfloat16)
        for j, h in enumerate(heads):
            out_buf[lane, :, h] = mixed[j * count : (j + 1) * count]
        return carry

    lax.fori_loop(0, local_kv, attend_group, 0)


def fused_kernel(
    sizes,
    span_hbm,
    seg_hbm,
    owner_hbm,
    q_hbm,
    k_hbm,
    v_hbm,
    res_hbm,
    w_hbm,
    gain_hbm,
    hidden_ref,
    ffn_ref,
    q_buf,
    ks_buf,
    vs_buf,
    k_buf,
    v_buf,
    w_buf,
    res_buf,
    att_buf,
    part_buf,
    recv_buf,
    out_buf,
    gain_ref,
    span_ref,
    seg_ref,
    owner_ref,
    in_sem,
    w_sem,
    k_send,
    k_recv,
    v_send,
    v_recv,
    p_send,
    p_recv,
    o_send,
    o_recv,
    own_sem,
):
    wide_count, capacity, local_kv, group_size = sizes
    rows, model = res_hbm.shape
    piece = model // PIECES
    span = model // SENDS
    me = lax.axis_index("wide")
    lane = lax.axis_index("narrow")
    other = 1 - lane
    peers = [lax.rem(me + k, wide_count) for k in range(1, wide_count)]
    long_rows, short_rows = slice(0, rows), slice(rows, 2 * rows)

    barrier = pltpu.get_barrier_semaphore()
    for peer in peers:
        pl.semaphore_signal(barrier, inc=1, device_id={"wide": peer}, device_id_type=MESH)
    pl.semaphore_signal(barrier, inc=1, device_id={"narrow": other}, device_id_type=MESH)

    loads = [
        pltpu.make_async_copy(q_hbm.at[pl.ds(rows, rows)], q_buf.at[pl.ds(rows, rows)], in_sem.at[0]),
        pltpu.make_async_copy(k_hbm.at[pl.ds(rows, rows)], ks_buf, in_sem.at[1]),
        pltpu.make_async_copy(v_hbm.at[pl.ds(rows, rows)], vs_buf, in_sem.at[2]),
        pltpu.make_async_copy(seg_hbm, seg_ref, in_sem.at[6]),
    ]
    owner_load = pltpu.make_async_copy(owner_hbm, owner_ref, in_sem.at[7])
    gain_load = pltpu.make_async_copy(gain_hbm, gain_ref, in_sem.at[9])
    late_loads = [
        pltpu.make_async_copy(k_hbm.at[pl.ds(0, rows)], k_buf.at[me], in_sem.at[3]),
        pltpu.make_async_copy(v_hbm.at[pl.ds(0, rows)], v_buf.at[me], in_sem.at[4]),
        pltpu.make_async_copy(span_hbm, span_ref, in_sem.at[8]),
        pltpu.make_async_copy(q_hbm.at[pl.ds(0, rows)], q_buf.at[pl.ds(0, rows)], in_sem.at[10]),
    ]
    res_load = pltpu.make_async_copy(res_hbm, res_buf, in_sem.at[5])
    w_loads = [
        pltpu.make_async_copy(
            w_hbm.at[:, pl.ds(c * piece, piece)], w_buf.at[c], w_sem.at[c]
        )
        for c in range(PIECES)
    ]
    for load in loads + [owner_load] + w_loads[:EARLY]:
        load.start()

    pl.semaphore_wait(barrier, wide_count)

    def kv_copy(source, peer):
        return [
            pltpu.make_async_remote_copy(
                src_ref=hbm.at[pl.ds(0, rows)],
                dst_ref=buf.at[source],
                send_sem=send.at[peer],
                recv_sem=recv.at[source],
                device_id={"wide": peer},
                device_id_type=MESH,
            )
            for hbm, buf, send, recv in (
                (k_hbm, k_buf, k_send, k_recv),
                (v_hbm, v_buf, v_send, v_recv),
            )
        ]

    for peer in peers:
        for copy in kv_copy(me, peer):
            copy.start()
    for load in w_loads[EARLY:] + [res_load, gain_load] + late_loads:
        load.start()

    row_id = lax.broadcasted_iota(jnp.int32, (rows, rows), 0)
    col_id = lax.broadcasted_iota(jnp.int32, (rows, rows), 1)

    owner_load.wait()
    owner_across = jnp.broadcast_to(owner_ref[...], (rows, rows)).astype(jnp.float32)
    owner_down = owner_across.T
    same = jnp.where((owner_down == owner_across) & (row_id < col_id), 1.0, 0.0)
    slot = jnp.sum(same, axis=0, keepdims=True)
    target = (owner_across[0:1] * capacity + slot).astype(jnp.int32)
    slots = lax.broadcasted_iota(jnp.int32, (wide_count * capacity, rows), 0)
    dispatch = jnp.where(slots == target, 1.0, 0.0).astype(jnp.bfloat16)

    def part_copy(c, phase):
        return pltpu.make_async_remote_copy(
            src_ref=part_buf.at[phase, c],
            dst_ref=recv_buf.at[c],
            send_sem=p_send.at[c],
            recv_sem=p_recv.at[c],
            device_id={"narrow": other},
            device_id_type=MESH,
        )

    def project(phase, c):
        if phase == 1:
            w_loads[c].wait()
        product = jnp.dot(att_buf[phase], w_buf[c], preferred_element_type=jnp.float32)
        part_buf[phase, c] = product.astype(jnp.bfloat16)

    def lend(phase):
        for c in range(PIECES):
            project(phase, c)
            part_copy(c, phase).start()

    def out_copy(c, source, peer):
        return pltpu.make_async_remote_copy(
            src_ref=out_buf.at[c, peer],
            dst_ref=ffn_ref.at[source, :, pl.ds(pl.multiple_of(c * span, span), span)],
            send_sem=o_send.at[c, peer],
            recv_sem=o_recv.at[c, source],
            device_id={"wide": peer},
            device_id_type=MESH,
        )

    def own_copy(c):
        return pltpu.make_async_copy(
            out_buf.at[c, me],
            ffn_ref.at[me, :, pl.ds(pl.multiple_of(c * span, span), span)],
            own_sem.at[c],
        )

    def finish(phase):
        res_load.wait()
        gain_load.wait()
        squares = jnp.zeros((rows, 1), jnp.float32)
        for step in range(PIECES + 1):
            if step < PIECES:
                project(phase, step)
            if step == 0:
                continue
            c = step - 1
            part_copy(c, phase).wait_recv()
            cols = slice(c * piece, (c + 1) * piece)
            summed = part_buf[phase, c].astype(jnp.float32) + recv_buf[c].astype(jnp.float32)
            hidden = (res_buf[:, cols].astype(jnp.float32) + summed).astype(jnp.bfloat16)
            hidden_ref[:, cols] = hidden
            widened = hidden.astype(jnp.float32)
            squares += jnp.sum(widened * widened, axis=1, keepdims=True)
        factor = lax.rsqrt(squares / model + 1e-05)
        lines = span // HEAD
        for c in range(SENDS):
            cols = slice(c * span, (c + 1) * span)
            gains = gain_ref[c * lines : (c + 1) * lines, :].astype(jnp.float32)
            gain = jnp.concatenate([gains[i : i + 1] for i in range(lines)], axis=1)
            normed = (hidden_ref[:, cols].astype(jnp.float32) * factor * gain).astype(jnp.bfloat16)
            outgoing = jnp.dot(dispatch, normed, preferred_element_type=jnp.float32)
            out_buf[c] = outgoing.astype(jnp.bfloat16).reshape(wide_count, capacity, span)
            for peer in peers:
                out_copy(c, me, peer).start()
            own_copy(c).start()

    def both(phase):
        @pl.when(lane == phase)
        def _():
            finish(phase)

        @pl.when(lane != phase)
        def _():
            lend(phase)

    for load in loads:
        load.wait()
    seg_across = jnp.broadcast_to(seg_ref[...], (rows, rows)).astype(jnp.float32)
    short_visible = (seg_across == seg_across.T) & (col_id <= row_id)
    attend_heads(
        q_buf,
        lambda group: ks_buf[:, group],
        lambda group: vs_buf[:, group],
        short_visible,
        short_rows,
        att_buf,
        1,
        local_kv,
        group_size,
    )
    both(1)

    for load in late_loads:
        load.wait()
    for peer in peers:
        for copy in kv_copy(peer, peer):
            copy.wait_recv()
    spans = span_ref[...]
    wide_ids = lax.broadcasted_iota(jnp.int32, (1, wide_count), 1)
    own_span = jnp.sum(jnp.where(wide_ids == me, spans, 0), axis=1, keepdims=True)
    long_visible = jnp.concatenate(
        [
            (spans[:, b : b + 1] * rows + col_id) <= (own_span * rows + row_id)
            for b in range(wide_count)
        ],
        axis=1,
    )
    attend_heads(
        q_buf,
        lambda group: k_buf[:, :, group].reshape(wide_count * rows, HEAD),
        lambda group: v_buf[:, :, group].reshape(wide_count * rows, HEAD),
        long_visible,
        long_rows,
        att_buf,
        0,
        local_kv,
        group_size,
    )
    both(0)

    for peer in peers:
        for copy in kv_copy(me, peer):
            copy.wait_send()

    def drain_parts(c, carry):
        part_copy(c, 0).wait_send()
        return carry

    lax.fori_loop(0, PIECES, drain_parts, 0)

    def drain_sends(c, carry):
        for peer in peers:
            out_copy(c, me, peer).wait_send()
            out_copy(c, peer, peer).wait_recv()
        own_copy(c).wait()
        return carry

    lax.fori_loop(0, SENDS, drain_sends, 0)


def store_kernel(hidden_ref, ffn_ref, hidden_out, ffn_out, sems):
    parts = ffn_ref.shape[0]
    count = hidden_ref.shape[0] // parts
    half = ffn_ref.shape[1] // 2
    copies = []
    for s in range(parts):
        some = pl.ds(s * count, count)
        copies.append(
            pltpu.make_async_copy(hidden_ref.at[some], hidden_out.at[some], sems.at[3 * s])
        )
        for j in range(2):
            some = pl.ds(j * half, half)
            copies.append(
                pltpu.make_async_copy(
                    ffn_ref.at[s, some], ffn_out.at[s, some], sems.at[3 * s + 1 + j]
                )
            )
    for copy in copies:
        copy.start()
    for copy in copies:
        copy.wait()


def fused_on_device(
    queries, key_rows, value_rows, residual, out_weight, norm_gain, span_map, segments, row_owner
):
    wide_count = lax.axis_size("wide")
    local_heads = queries.shape[1] // HEAD
    local_kv = key_rows.shape[1] // HEAD
    rows, model = residual.shape
    capacity = max(2, 2 * rows // wide_count)
    sizes = (wide_count, capacity, local_kv, local_heads // local_kv)
    bf16 = jnp.bfloat16
    dma = pltpu.SemaphoreType.DMA
    any_spec = pl.BlockSpec(memory_space=pl.ANY)
    vmem_spec = pl.BlockSpec(memory_space=pltpu.VMEM)
    piece, span = model // PIECES, model // SENDS
    hidden, arrived = pl.pallas_call(
        functools.partial(fused_kernel, sizes),
        out_shape=(
            pltpu.VMEM((rows, model), bf16),
            pltpu.VMEM((wide_count, capacity, model), bf16),
        ),
        in_specs=[any_spec] * 9,
        out_specs=(vmem_spec, vmem_spec),
        scratch_shapes=[
            pltpu.VMEM(queries.shape, bf16),
            pltpu.VMEM((rows, key_rows.shape[1]), bf16),
            pltpu.VMEM((rows, key_rows.shape[1]), bf16),
            pltpu.VMEM((wide_count, rows, key_rows.shape[1]), bf16),
            pltpu.VMEM((wide_count, rows, key_rows.shape[1]), bf16),
            pltpu.VMEM((PIECES, out_weight.shape[0], piece), bf16),
            pltpu.VMEM((rows, model), bf16),
            pltpu.VMEM((2, rows, queries.shape[1]), bf16),
            pltpu.VMEM((2, PIECES, rows, piece), bf16),
            pltpu.VMEM((PIECES, rows, piece), bf16),
            pltpu.VMEM((SENDS, wide_count, capacity, span), bf16),
            pltpu.VMEM((model // HEAD, HEAD), bf16),
            pltpu.VMEM((1, wide_count), jnp.int32),
            pltpu.VMEM((1, rows), jnp.int32),
            pltpu.VMEM((1, rows), jnp.int32),
            dma((11,)),
            dma((PIECES,)),
            dma((wide_count,)),
            dma((wide_count,)),
            dma((wide_count,)),
            dma((wide_count,)),
            dma((PIECES,)),
            dma((PIECES,)),
            dma((SENDS, wide_count)),
            dma((SENDS, wide_count)),
            dma((SENDS,)),
        ],
        compiler_params=pltpu.CompilerParams(
            collective_id=0, has_side_effects=True, vmem_limit_bytes=60 * 1024 * 1024
        ),
    )(
        span_map.reshape(1, wide_count),
        segments,
        row_owner.reshape(1, rows),
        queries,
        key_rows,
        value_rows,
        residual,
        out_weight,
        norm_gain.reshape(model // HEAD, HEAD),
    )
    hidden, arrived = pl.pallas_call(
        store_kernel,
        out_shape=(
            jax.ShapeDtypeStruct(hidden.shape, bf16),
            jax.ShapeDtypeStruct(arrived.shape, bf16),
        ),
        in_specs=[any_spec] * 2,
        out_specs=(any_spec, any_spec),
        scratch_shapes=[dma((3 * wide_count,))],
        compiler_params=pltpu.CompilerParams(vmem_limit_bytes=1024 * 1024),
    )(hidden, arrived)
    return hidden, arrived.reshape(1, 1, wide_count, capacity, model)


def on_device(*args):
    queries, residual = args[0], args[3]
    rows, model = residual.shape
    wide_count = lax.axis_size("wide")
    fits = (
        lax.axis_size("narrow") == 2
        and rows == LONG_DEV
        and queries.shape[0] == 2 * LONG_DEV
        and (2 * rows) % (32 * wide_count) == 0
        and rows % (16 * wide_count) == 0
        and model % (PIECES * HEAD) == 0
    )
    return (fused_on_device if fits else general_on_device)(*args)


def solution(mesh):
    placed = (
        P(("rep", "wide"), "narrow"),
        P(("rep", "wide"), "narrow"),
        P(("rep", "wide"), "narrow"),
        P(("rep", "wide", "narrow"), None),
        P("narrow", None),
        P(),
        P(),
        P(("rep", "wide"), None),
        P(("rep", "wide", "narrow"), None),
    )
    return jax.shard_map(
        on_device,
        mesh=mesh,
        in_specs=placed,
        out_specs=(
            P(("rep", "wide", "narrow"), None),
            P(("rep", "wide"), "narrow", None, None, None),
        ),
        check_vma=False,
    )
```

```python
import functools

import jax
import jax.numpy as jnp
from jax import lax
from jax.experimental import pallas as pl
from jax.experimental.pallas import tpu as pltpu
from jax.sharding import PartitionSpec as P

HEAD = 128
LONG_DEV = 128


def attend_block(
    partial_state, long_queries, key_block, value_block, key_pos, query_pos, score_scale
):
    running_max, weight_sum, weighted = partial_state
    scores = (
        jnp.einsum("qgjd,kgd->qgjk", long_queries, key_block, preferred_element_type=jnp.float32)
        * score_scale
    )
    visible = (key_pos[None, :] <= query_pos[:, None])[:, None, None, :]
    masked = jnp.where(visible, scores, -1e30)
    newest = jnp.maximum(running_max, jnp.max(masked, axis=-1))
    weights = jnp.where(visible, jnp.exp(masked - newest[..., None]), 0.0)
    factor = jnp.exp(running_max - newest)
    weight_sum = weight_sum * factor + jnp.sum(weights, axis=-1)
    weighted = weighted * factor[..., None] + jnp.einsum(
        "qgjk,kgd->qgjd",
        weights.astype(jnp.bfloat16),
        value_block,
        preferred_element_type=jnp.float32,
    )
    return (newest, weight_sum, weighted)


def rounded_term(attended, out_weight):
    product = jnp.dot(attended, out_weight, preferred_element_type=jnp.float32)
    return lax.optimization_barrier(product.astype(jnp.bfloat16)).astype(jnp.float32)


def general_on_device(
    queries, key_rows, value_rows, residual, out_weight, norm_gain, span_map, segments, row_owner
):
    wide_count = lax.axis_size("wide")
    narrow_count = lax.axis_size("narrow")
    wide_index = lax.axis_index("wide")
    local_heads = queries.shape[1] // HEAD
    local_kv = key_rows.shape[1] // HEAD
    group_size = local_heads // local_kv
    token_count = queries.shape[0]
    short_count = token_count - LONG_DEV
    score_scale = HEAD ** (-0.5)
    own_span = lax.dynamic_slice_in_dim(span_map, wide_index, 1, 0)[0]
    query_pos = own_span * LONG_DEV + jnp.arange(LONG_DEV, dtype=jnp.int32)
    long_queries = queries[:LONG_DEV].reshape(LONG_DEV, local_kv, group_size, HEAD)
    wide_ids = jnp.arange(wide_count, dtype=jnp.int32)
    start_state = (
        jnp.full((LONG_DEV, local_kv, group_size), -1e30, jnp.float32),
        jnp.zeros((LONG_DEV, local_kv, group_size), jnp.float32),
        jnp.zeros((LONG_DEV, local_kv, group_size, HEAD), jnp.float32),
    )
    key_piece = lax.all_gather(key_rows[:LONG_DEV], "wide", axis=0, tiled=True)
    value_piece = lax.all_gather(value_rows[:LONG_DEV], "wide", axis=0, tiled=True)
    row_count = key_piece.shape[0]
    key_index = jnp.arange(row_count, dtype=jnp.int32)
    holder = key_index // LONG_DEV
    span_of = jnp.sum(jnp.where(holder[:, None] == wide_ids[None, :], span_map[None, :], 0), axis=1)
    key_pos = span_of * LONG_DEV + key_index % LONG_DEV
    key_block = key_piece.reshape(row_count, local_kv, HEAD)
    value_block = value_piece.reshape(row_count, local_kv, HEAD)

    def advance(partial_state):
        if row_count > 512 and row_count % 512 == 0:
            splits = row_count // 512

            def advance_block(inner_state, sliced):
                return (
                    attend_block(
                        inner_state,
                        long_queries,
                        sliced[0],
                        sliced[1],
                        sliced[2],
                        query_pos,
                        score_scale,
                    ),
                    None,
                )

            finished, unused = lax.scan(
                advance_block,
                partial_state,
                (
                    key_block.reshape(splits, 512, local_kv, HEAD),
                    value_block.reshape(splits, 512, local_kv, HEAD),
                    key_pos.reshape(splits, 512),
                ),
            )
            return finished
        return attend_block(
            partial_state, long_queries, key_block, value_block, key_pos, query_pos, score_scale
        )

    running_max, weight_sum, weighted = advance(start_state)
    long_out = (
        (weighted / weight_sum[..., None])
        .astype(jnp.bfloat16)
        .reshape(LONG_DEV, local_heads * HEAD)
    )
    short_queries = queries[LONG_DEV:].reshape(short_count, local_kv, group_size, HEAD)
    short_keys = key_rows[LONG_DEV:].reshape(short_count, local_kv, HEAD)
    short_values = value_rows[LONG_DEV:].reshape(short_count, local_kv, HEAD)
    documents = segments[0]
    positions = jnp.arange(short_count, dtype=jnp.int32)
    visible = (
        (documents[None, :] == documents[:, None]) & (positions[None, :] <= positions[:, None])
    )[:, None, None, :]
    scores = (
        jnp.einsum("qgjd,kgd->qgjk", short_queries, short_keys, preferred_element_type=jnp.float32)
        * score_scale
    )
    masked = jnp.where(visible, scores, -1e30)
    row_max = jnp.max(masked, axis=-1, keepdims=True)
    weights = jnp.where(visible, jnp.exp(masked - row_max), 0.0)
    short_sum = jnp.sum(weights, axis=-1)
    mixed = jnp.einsum(
        "qgjk,kgd->qgjd",
        weights.astype(jnp.bfloat16),
        short_values,
        preferred_element_type=jnp.float32,
    )
    short_out = (
        (mixed / short_sum[..., None]).astype(jnp.bfloat16).reshape(short_count, local_heads * HEAD)
    )
    attended = jnp.concatenate([long_out, short_out], axis=0)
    rows_dev = token_count // narrow_count
    sliced = attended
    summed = lax.psum_scatter(
        rounded_term(sliced, out_weight).astype(jnp.bfloat16),
        "narrow",
        scatter_dimension=0,
        tiled=True,
    ).astype(jnp.float32)
    hidden = (residual.astype(jnp.float32) + summed).astype(jnp.bfloat16)
    widened = hidden.astype(jnp.float32)
    normed = (
        widened
        * lax.rsqrt(jnp.mean(widened * widened, axis=1, keepdims=True) + 1e-05)
        * norm_gain.astype(jnp.float32)
    ).astype(jnp.bfloat16)
    capacity = max(2, 2 * rows_dev // wide_count)
    owners = row_owner[:, 0]
    chosen = (owners[:, None] == wide_ids[None, :]).astype(jnp.int32)
    earlier = jnp.cumsum(chosen, axis=0) - chosen
    slot_index = jnp.sum(earlier * chosen, axis=1)
    target = owners * capacity + slot_index
    dispatch = (
        target[None, :] == jnp.arange(wide_count * capacity, dtype=jnp.int32)[:, None]
    ).astype(jnp.bfloat16)
    outgoing = jnp.dot(dispatch, normed, preferred_element_type=jnp.float32).astype(jnp.bfloat16)
    outgoing = outgoing.reshape(wide_count, 1, 1, capacity, normed.shape[1])
    arrived = lax.all_to_all(outgoing, "wide", split_axis=0, concat_axis=2, tiled=True)
    return (hidden, arrived)


PIECES = 8
SENDS = 4
EARLY = 4
MESH = pl.DeviceIdType.MESH


def attend_heads(q_buf, keys, values, visible, rows, out_buf, lane, groups, group_size):
    score_scale = HEAD ** (-0.5)
    count = rows.stop - rows.start
    tiled = jnp.concatenate([visible] * group_size, axis=0)

    def attend_group(g, carry):
        heads = [
            pl.ds(pl.multiple_of((g * group_size + j) * HEAD, HEAD), HEAD) for j in range(group_size)
        ]
        group = pl.ds(pl.multiple_of(g * HEAD, HEAD), HEAD)
        stacked = jnp.concatenate([q_buf[rows, h] for h in heads], axis=0)
        scores = (
            lax.dot_general(
                stacked, keys(group), (((1,), (1,)), ((), ())), preferred_element_type=jnp.float32
            )
            * score_scale
        )
        masked = jnp.where(tiled, scores, -1e30)
        weights = jnp.exp(masked - jnp.max(masked, axis=1, keepdims=True))
        total = jnp.sum(weights, axis=1, keepdims=True)
        mixed = jnp.dot(
            weights.astype(jnp.bfloat16), values(group), preferred_element_type=jnp.float32
        )
        mixed = (mixed / total).astype(jnp.bfloat16)
        for j, h in enumerate(heads):
            out_buf[lane, :, h] = mixed[j * count : (j + 1) * count]
        return carry

    lax.fori_loop(*groups, attend_group, 0)


def fused_kernel(
    sizes,
    span_hbm,
    seg_hbm,
    owner_hbm,
    q_hbm,
    k_hbm,
    v_hbm,
    res_hbm,
    w_hbm,
    gain_hbm,
    hidden_ref,
    ffn_ref,
    q_buf,
    ks_buf,
    vs_buf,
    k_buf,
    v_buf,
    w_buf,
    res_buf,
    att_buf,
    part_buf,
    recv_buf,
    out_buf,
    gain_ref,
    span_ref,
    seg_ref,
    owner_ref,
    in_sem,
    w_sem,
    k_send,
    k_recv,
    v_send,
    v_recv,
    p_send,
    p_recv,
    o_send,
    o_recv,
    own_sem,
):
    wide_count, capacity, local_kv, group_size = sizes
    rows, model = res_hbm.shape
    piece = model // PIECES
    span = model // SENDS
    me = lax.axis_index("wide")
    lane = lax.axis_index("narrow")
    other = 1 - lane
    peers = [lax.rem(me + k, wide_count) for k in range(1, wide_count)]
    long_rows, short_rows = slice(0, rows), slice(rows, 2 * rows)

    barrier = pltpu.get_barrier_semaphore()
    for peer in peers:
        pl.semaphore_signal(barrier, inc=1, device_id={"wide": peer}, device_id_type=MESH)
    pl.semaphore_signal(barrier, inc=1, device_id={"narrow": other}, device_id_type=MESH)

    loads = [
        pltpu.make_async_copy(q_hbm.at[pl.ds(rows, rows)], q_buf.at[pl.ds(rows, rows)], in_sem.at[0]),
        pltpu.make_async_copy(k_hbm.at[pl.ds(rows, rows)], ks_buf, in_sem.at[1]),
        pltpu.make_async_copy(v_hbm.at[pl.ds(rows, rows)], vs_buf, in_sem.at[2]),
        pltpu.make_async_copy(seg_hbm, seg_ref, in_sem.at[6]),
    ]
    owner_load = pltpu.make_async_copy(owner_hbm, owner_ref, in_sem.at[7])
    gain_load = pltpu.make_async_copy(gain_hbm, gain_ref, in_sem.at[9])
    late_loads = [
        pltpu.make_async_copy(k_hbm.at[pl.ds(0, rows)], k_buf.at[me], in_sem.at[3]),
        pltpu.make_async_copy(v_hbm.at[pl.ds(0, rows)], v_buf.at[me], in_sem.at[4]),
        pltpu.make_async_copy(span_hbm, span_ref, in_sem.at[8]),
        pltpu.make_async_copy(q_hbm.at[pl.ds(0, rows)], q_buf.at[pl.ds(0, rows)], in_sem.at[10]),
    ]
    res_load = pltpu.make_async_copy(res_hbm, res_buf, in_sem.at[5])
    w_loads = [
        pltpu.make_async_copy(
            w_hbm.at[:, pl.ds(c * piece, piece)], w_buf.at[c], w_sem.at[c]
        )
        for c in range(PIECES)
    ]
    for load in loads + [owner_load] + w_loads[:EARLY]:
        load.start()

    def kv_copy(source, peer):
        return [
            pltpu.make_async_remote_copy(
                src_ref=hbm.at[pl.ds(0, rows)],
                dst_ref=buf.at[source],
                send_sem=send.at[peer],
                recv_sem=recv.at[source],
                device_id={"wide": peer},
                device_id_type=MESH,
            )
            for hbm, buf, send, recv in (
                (k_hbm, k_buf, k_send, k_recv),
                (v_hbm, v_buf, v_send, v_recv),
            )
        ]

    row_id = lax.broadcasted_iota(jnp.int32, (rows, rows), 0)
    col_id = lax.broadcasted_iota(jnp.int32, (rows, rows), 1)

    owner_load.wait()
    owner_across = jnp.broadcast_to(owner_ref[...], (rows, rows)).astype(jnp.float32)
    owner_down = owner_across.T
    same = jnp.where((owner_down == owner_across) & (row_id < col_id), 1.0, 0.0)
    slot = jnp.sum(same, axis=0, keepdims=True)
    target = (owner_across[0:1] * capacity + slot).astype(jnp.int32)
    slots = lax.broadcasted_iota(jnp.int32, (wide_count * capacity, rows), 0)
    dispatch = jnp.where(slots == target, 1.0, 0.0).astype(jnp.bfloat16)

    def part_copy(c, phase):
        return pltpu.make_async_remote_copy(
            src_ref=part_buf.at[phase, c],
            dst_ref=recv_buf.at[c],
            send_sem=p_send.at[c],
            recv_sem=p_recv.at[c],
            device_id={"narrow": other},
            device_id_type=MESH,
        )

    def project(phase, c):
        if phase == 1:
            w_loads[c].wait()
        product = jnp.dot(att_buf[phase], w_buf[c], preferred_element_type=jnp.float32)
        part_buf[phase, c] = product.astype(jnp.bfloat16)

    def lend(phase):
        for c in range(PIECES):
            project(phase, c)
            part_copy(c, phase).start()

    def out_copy(c, source, peer):
        return pltpu.make_async_remote_copy(
            src_ref=out_buf.at[c, peer],
            dst_ref=ffn_ref.at[source, :, pl.ds(pl.multiple_of(c * span, span), span)],
            send_sem=o_send.at[c, peer],
            recv_sem=o_recv.at[c, source],
            device_id={"wide": peer},
            device_id_type=MESH,
        )

    def own_copy(c):
        return pltpu.make_async_copy(
            out_buf.at[c, me],
            ffn_ref.at[me, :, pl.ds(pl.multiple_of(c * span, span), span)],
            own_sem.at[c],
        )

    def finish(phase):
        res_load.wait()
        gain_load.wait()
        squares = jnp.zeros((rows, 1), jnp.float32)
        for step in range(PIECES + 1):
            if step < PIECES:
                project(phase, step)
            if step == 0:
                continue
            c = step - 1
            part_copy(c, phase).wait_recv()
            cols = slice(c * piece, (c + 1) * piece)
            summed = part_buf[phase, c].astype(jnp.float32) + recv_buf[c].astype(jnp.float32)
            hidden = (res_buf[:, cols].astype(jnp.float32) + summed).astype(jnp.bfloat16)
            hidden_ref[:, cols] = hidden
            widened = hidden.astype(jnp.float32)
            squares += jnp.sum(widened * widened, axis=1, keepdims=True)
        factor = lax.rsqrt(squares / model + 1e-05)
        lines = span // HEAD
        for c in range(SENDS):
            cols = slice(c * span, (c + 1) * span)
            gains = gain_ref[c * lines : (c + 1) * lines, :].astype(jnp.float32)
            gain = jnp.concatenate([gains[i : i + 1] for i in range(lines)], axis=1)
            normed = (hidden_ref[:, cols].astype(jnp.float32) * factor * gain).astype(jnp.bfloat16)
            outgoing = jnp.dot(dispatch, normed, preferred_element_type=jnp.float32)
            out_buf[c] = outgoing.astype(jnp.bfloat16).reshape(wide_count, capacity, span)
            for peer in peers:
                out_copy(c, me, peer).start()
            own_copy(c).start()

    def both(phase):
        @pl.when(lane == phase)
        def _():
            finish(phase)

        @pl.when(lane != phase)
        def _():
            lend(phase)

    for load in loads:
        load.wait()
    seg_across = jnp.broadcast_to(seg_ref[...], (rows, rows)).astype(jnp.float32)
    short_visible = (seg_across == seg_across.T) & (col_id <= row_id)

    def attend_short(first, last):
        attend_heads(
            q_buf,
            lambda group: ks_buf[:, group],
            lambda group: vs_buf[:, group],
            short_visible,
            short_rows,
            att_buf,
            1,
            (first, last),
            group_size,
        )

    attend_short(0, 1)
    pl.semaphore_wait(barrier, wide_count)
    for peer in peers:
        for copy in kv_copy(me, peer):
            copy.start()
    for load in w_loads[EARLY:] + [res_load, gain_load] + late_loads:
        load.start()

    attend_short(1, local_kv)
    both(1)

    for load in late_loads:
        load.wait()
    for peer in peers:
        for copy in kv_copy(peer, peer):
            copy.wait_recv()
    spans = span_ref[...]
    wide_ids = lax.broadcasted_iota(jnp.int32, (1, wide_count), 1)
    own_span = jnp.sum(jnp.where(wide_ids == me, spans, 0), axis=1, keepdims=True)
    long_visible = jnp.concatenate(
        [
            (spans[:, b : b + 1] * rows + col_id) <= (own_span * rows + row_id)
            for b in range(wide_count)
        ],
        axis=1,
    )
    attend_heads(
        q_buf,
        lambda group: k_buf[:, :, group].reshape(wide_count * rows, HEAD),
        lambda group: v_buf[:, :, group].reshape(wide_count * rows, HEAD),
        long_visible,
        long_rows,
        att_buf,
        0,
        (0, local_kv),
        group_size,
    )
    both(0)

    for peer in peers:
        for copy in kv_copy(me, peer):
            copy.wait_send()

    def drain_parts(c, carry):
        part_copy(c, 0).wait_send()
        return carry

    lax.fori_loop(0, PIECES, drain_parts, 0)

    def drain_sends(c, carry):
        for peer in peers:
            out_copy(c, me, peer).wait_send()
            out_copy(c, peer, peer).wait_recv()
        own_copy(c).wait()
        return carry

    lax.fori_loop(0, SENDS, drain_sends, 0)


def store_kernel(hidden_ref, ffn_ref, hidden_out, ffn_out, sems):
    parts = ffn_ref.shape[0]
    count = hidden_ref.shape[0] // parts
    half = ffn_ref.shape[1] // 2
    copies = []
    for s in range(parts):
        some = pl.ds(s * count, count)
        copies.append(
            pltpu.make_async_copy(hidden_ref.at[some], hidden_out.at[some], sems.at[3 * s])
        )
        for j in range(2):
            some = pl.ds(j * half, half)
            copies.append(
                pltpu.make_async_copy(
                    ffn_ref.at[s, some], ffn_out.at[s, some], sems.at[3 * s + 1 + j]
                )
            )
    for copy in copies:
        copy.start()
    for copy in copies:
        copy.wait()


def fused_on_device(
    queries, key_rows, value_rows, residual, out_weight, norm_gain, span_map, segments, row_owner
):
    wide_count = lax.axis_size("wide")
    local_heads = queries.shape[1] // HEAD
    local_kv = key_rows.shape[1] // HEAD
    rows, model = residual.shape
    capacity = max(2, 2 * rows // wide_count)
    sizes = (wide_count, capacity, local_kv, local_heads // local_kv)
    bf16 = jnp.bfloat16
    dma = pltpu.SemaphoreType.DMA
    any_spec = pl.BlockSpec(memory_space=pl.ANY)
    vmem_spec = pl.BlockSpec(memory_space=pltpu.VMEM)
    piece, span = model // PIECES, model // SENDS
    hidden, arrived = pl.pallas_call(
        functools.partial(fused_kernel, sizes),
        out_shape=(
            pltpu.VMEM((rows, model), bf16),
            pltpu.VMEM((wide_count, capacity, model), bf16),
        ),
        in_specs=[any_spec] * 9,
        out_specs=(vmem_spec, vmem_spec),
        scratch_shapes=[
            pltpu.VMEM(queries.shape, bf16),
            pltpu.VMEM((rows, key_rows.shape[1]), bf16),
            pltpu.VMEM((rows, key_rows.shape[1]), bf16),
            pltpu.VMEM((wide_count, rows, key_rows.shape[1]), bf16),
            pltpu.VMEM((wide_count, rows, key_rows.shape[1]), bf16),
            pltpu.VMEM((PIECES, out_weight.shape[0], piece), bf16),
            pltpu.VMEM((rows, model), bf16),
            pltpu.VMEM((2, rows, queries.shape[1]), bf16),
            pltpu.VMEM((2, PIECES, rows, piece), bf16),
            pltpu.VMEM((PIECES, rows, piece), bf16),
            pltpu.VMEM((SENDS, wide_count, capacity, span), bf16),
            pltpu.VMEM((model // HEAD, HEAD), bf16),
            pltpu.VMEM((1, wide_count), jnp.int32),
            pltpu.VMEM((1, rows), jnp.int32),
            pltpu.VMEM((1, rows), jnp.int32),
            dma((11,)),
            dma((PIECES,)),
            dma((wide_count,)),
            dma((wide_count,)),
            dma((wide_count,)),
            dma((wide_count,)),
            dma((PIECES,)),
            dma((PIECES,)),
            dma((SENDS, wide_count)),
            dma((SENDS, wide_count)),
            dma((SENDS,)),
        ],
        compiler_params=pltpu.CompilerParams(
            collective_id=0, has_side_effects=True, vmem_limit_bytes=60 * 1024 * 1024
        ),
    )(
        span_map.reshape(1, wide_count),
        segments,
        row_owner.reshape(1, rows),
        queries,
        key_rows,
        value_rows,
        residual,
        out_weight,
        norm_gain.reshape(model // HEAD, HEAD),
    )
    hidden, arrived = pl.pallas_call(
        store_kernel,
        out_shape=(
            jax.ShapeDtypeStruct(hidden.shape, bf16),
            jax.ShapeDtypeStruct(arrived.shape, bf16),
        ),
        in_specs=[any_spec] * 2,
        out_specs=(any_spec, any_spec),
        scratch_shapes=[dma((3 * wide_count,))],
        compiler_params=pltpu.CompilerParams(vmem_limit_bytes=1024 * 1024),
    )(hidden, arrived)
    return hidden, arrived.reshape(1, 1, wide_count, capacity, model)


def on_device(*args):
    queries, residual = args[0], args[3]
    rows, model = residual.shape
    wide_count = lax.axis_size("wide")
    fits = (
        lax.axis_size("narrow") == 2
        and rows == LONG_DEV
        and queries.shape[0] == 2 * LONG_DEV
        and (2 * rows) % (32 * wide_count) == 0
        and rows % (16 * wide_count) == 0
        and model % (PIECES * HEAD) == 0
    )
    return (fused_on_device if fits else general_on_device)(*args)


def solution(mesh):
    placed = (
        P(("rep", "wide"), "narrow"),
        P(("rep", "wide"), "narrow"),
        P(("rep", "wide"), "narrow"),
        P(("rep", "wide", "narrow"), None),
        P("narrow", None),
        P(),
        P(),
        P(("rep", "wide"), None),
        P(("rep", "wide", "narrow"), None),
    )
    return jax.shard_map(
        on_device,
        mesh=mesh,
        in_specs=placed,
        out_specs=(
            P(("rep", "wide", "narrow"), None),
            P(("rep", "wide"), "narrow", None, None, None),
        ),
        check_vma=False,
    )
```

```python
import functools

import jax
import jax.numpy as jnp
from jax import lax
from jax.experimental import pallas as pl
from jax.experimental.pallas import tpu as pltpu
from jax.sharding import PartitionSpec as P

HEAD = 128
LONG_DEV = 128


def attend_block(
    partial_state, long_queries, key_block, value_block, key_pos, query_pos, score_scale
):
    running_max, weight_sum, weighted = partial_state
    scores = (
        jnp.einsum("qgjd,kgd->qgjk", long_queries, key_block, preferred_element_type=jnp.float32)
        * score_scale
    )
    visible = (key_pos[None, :] <= query_pos[:, None])[:, None, None, :]
    masked = jnp.where(visible, scores, -1e30)
    newest = jnp.maximum(running_max, jnp.max(masked, axis=-1))
    weights = jnp.where(visible, jnp.exp(masked - newest[..., None]), 0.0)
    factor = jnp.exp(running_max - newest)
    weight_sum = weight_sum * factor + jnp.sum(weights, axis=-1)
    weighted = weighted * factor[..., None] + jnp.einsum(
        "qgjk,kgd->qgjd",
        weights.astype(jnp.bfloat16),
        value_block,
        preferred_element_type=jnp.float32,
    )
    return (newest, weight_sum, weighted)


def rounded_term(attended, out_weight):
    product = jnp.dot(attended, out_weight, preferred_element_type=jnp.float32)
    return lax.optimization_barrier(product.astype(jnp.bfloat16)).astype(jnp.float32)


def general_on_device(
    queries, key_rows, value_rows, residual, out_weight, norm_gain, span_map, segments, row_owner
):
    wide_count = lax.axis_size("wide")
    narrow_count = lax.axis_size("narrow")
    wide_index = lax.axis_index("wide")
    local_heads = queries.shape[1] // HEAD
    local_kv = key_rows.shape[1] // HEAD
    group_size = local_heads // local_kv
    token_count = queries.shape[0]
    short_count = token_count - LONG_DEV
    score_scale = HEAD ** (-0.5)
    own_span = lax.dynamic_slice_in_dim(span_map, wide_index, 1, 0)[0]
    query_pos = own_span * LONG_DEV + jnp.arange(LONG_DEV, dtype=jnp.int32)
    long_queries = queries[:LONG_DEV].reshape(LONG_DEV, local_kv, group_size, HEAD)
    wide_ids = jnp.arange(wide_count, dtype=jnp.int32)
    start_state = (
        jnp.full((LONG_DEV, local_kv, group_size), -1e30, jnp.float32),
        jnp.zeros((LONG_DEV, local_kv, group_size), jnp.float32),
        jnp.zeros((LONG_DEV, local_kv, group_size, HEAD), jnp.float32),
    )
    key_piece = lax.all_gather(key_rows[:LONG_DEV], "wide", axis=0, tiled=True)
    value_piece = lax.all_gather(value_rows[:LONG_DEV], "wide", axis=0, tiled=True)
    row_count = key_piece.shape[0]
    key_index = jnp.arange(row_count, dtype=jnp.int32)
    holder = key_index // LONG_DEV
    span_of = jnp.sum(jnp.where(holder[:, None] == wide_ids[None, :], span_map[None, :], 0), axis=1)
    key_pos = span_of * LONG_DEV + key_index % LONG_DEV
    key_block = key_piece.reshape(row_count, local_kv, HEAD)
    value_block = value_piece.reshape(row_count, local_kv, HEAD)

    def advance(partial_state):
        if row_count > 512 and row_count % 512 == 0:
            splits = row_count // 512

            def advance_block(inner_state, sliced):
                return (
                    attend_block(
                        inner_state,
                        long_queries,
                        sliced[0],
                        sliced[1],
                        sliced[2],
                        query_pos,
                        score_scale,
                    ),
                    None,
                )

            finished, unused = lax.scan(
                advance_block,
                partial_state,
                (
                    key_block.reshape(splits, 512, local_kv, HEAD),
                    value_block.reshape(splits, 512, local_kv, HEAD),
                    key_pos.reshape(splits, 512),
                ),
            )
            return finished
        return attend_block(
            partial_state, long_queries, key_block, value_block, key_pos, query_pos, score_scale
        )

    running_max, weight_sum, weighted = advance(start_state)
    long_out = (
        (weighted / weight_sum[..., None])
        .astype(jnp.bfloat16)
        .reshape(LONG_DEV, local_heads * HEAD)
    )
    short_queries = queries[LONG_DEV:].reshape(short_count, local_kv, group_size, HEAD)
    short_keys = key_rows[LONG_DEV:].reshape(short_count, local_kv, HEAD)
    short_values = value_rows[LONG_DEV:].reshape(short_count, local_kv, HEAD)
    documents = segments[0]
    positions = jnp.arange(short_count, dtype=jnp.int32)
    visible = (
        (documents[None, :] == documents[:, None]) & (positions[None, :] <= positions[:, None])
    )[:, None, None, :]
    scores = (
        jnp.einsum("qgjd,kgd->qgjk", short_queries, short_keys, preferred_element_type=jnp.float32)
        * score_scale
    )
    masked = jnp.where(visible, scores, -1e30)
    row_max = jnp.max(masked, axis=-1, keepdims=True)
    weights = jnp.where(visible, jnp.exp(masked - row_max), 0.0)
    short_sum = jnp.sum(weights, axis=-1)
    mixed = jnp.einsum(
        "qgjk,kgd->qgjd",
        weights.astype(jnp.bfloat16),
        short_values,
        preferred_element_type=jnp.float32,
    )
    short_out = (
        (mixed / short_sum[..., None]).astype(jnp.bfloat16).reshape(short_count, local_heads * HEAD)
    )
    attended = jnp.concatenate([long_out, short_out], axis=0)
    rows_dev = token_count // narrow_count
    sliced = attended
    summed = lax.psum_scatter(
        rounded_term(sliced, out_weight).astype(jnp.bfloat16),
        "narrow",
        scatter_dimension=0,
        tiled=True,
    ).astype(jnp.float32)
    hidden = (residual.astype(jnp.float32) + summed).astype(jnp.bfloat16)
    widened = hidden.astype(jnp.float32)
    normed = (
        widened
        * lax.rsqrt(jnp.mean(widened * widened, axis=1, keepdims=True) + 1e-05)
        * norm_gain.astype(jnp.float32)
    ).astype(jnp.bfloat16)
    capacity = max(2, 2 * rows_dev // wide_count)
    owners = row_owner[:, 0]
    chosen = (owners[:, None] == wide_ids[None, :]).astype(jnp.int32)
    earlier = jnp.cumsum(chosen, axis=0) - chosen
    slot_index = jnp.sum(earlier * chosen, axis=1)
    target = owners * capacity + slot_index
    dispatch = (
        target[None, :] == jnp.arange(wide_count * capacity, dtype=jnp.int32)[:, None]
    ).astype(jnp.bfloat16)
    outgoing = jnp.dot(dispatch, normed, preferred_element_type=jnp.float32).astype(jnp.bfloat16)
    outgoing = outgoing.reshape(wide_count, 1, 1, capacity, normed.shape[1])
    arrived = lax.all_to_all(outgoing, "wide", split_axis=0, concat_axis=2, tiled=True)
    return (hidden, arrived)


PIECES = 8
SENDS = 4
EARLY = 3
MESH = pl.DeviceIdType.MESH


def attend_heads(q_buf, keys, values, visible, rows, out_buf, lane, local_kv, group_size):
    score_scale = HEAD ** (-0.5)
    count = rows.stop - rows.start
    tiled = jnp.concatenate([visible] * group_size, axis=0)

    def attend_group(g, carry):
        heads = [
            pl.ds(pl.multiple_of((g * group_size + j) * HEAD, HEAD), HEAD) for j in range(group_size)
        ]
        group = pl.ds(pl.multiple_of(g * HEAD, HEAD), HEAD)
        stacked = jnp.concatenate([q_buf[rows, h] for h in heads], axis=0)
        scores = (
            lax.dot_general(
                stacked, keys(group), (((1,), (1,)), ((), ())), preferred_element_type=jnp.float32
            )
            * score_scale
        )
        masked = jnp.where(tiled, scores, -1e30)
        weights = jnp.exp(masked - jnp.max(masked, axis=1, keepdims=True))
        total = jnp.sum(weights, axis=1, keepdims=True)
        mixed = jnp.dot(
            weights.astype(jnp.bfloat16), values(group), preferred_element_type=jnp.float32
        )
        mixed = (mixed / total).astype(jnp.bfloat16)
        for j, h in enumerate(heads):
            out_buf[lane, :, h] = mixed[j * count : (j + 1) * count]
        return carry

    lax.fori_loop(0, local_kv, attend_group, 0, unroll=True)


def fused_kernel(
    sizes,
    span_hbm,
    seg_hbm,
    owner_hbm,
    q_hbm,
    k_hbm,
    v_hbm,
    res_hbm,
    w_hbm,
    gain_hbm,
    hidden_ref,
    ffn_ref,
    q_buf,
    ks_buf,
    vs_buf,
    k_buf,
    v_buf,
    w_buf,
    res_buf,
    att_buf,
    part_buf,
    recv_buf,
    out_buf,
    gain_ref,
    span_ref,
    seg_ref,
    owner_ref,
    in_sem,
    w_sem,
    k_send,
    k_recv,
    v_send,
    v_recv,
    p_send,
    p_recv,
    o_send,
    o_recv,
    own_sem,
):
    wide_count, capacity, local_kv, group_size = sizes
    rows, model = res_hbm.shape
    piece = model // PIECES
    span = model // SENDS
    me = lax.axis_index("wide")
    lane = lax.axis_index("narrow")
    other = 1 - lane
    peers = [lax.rem(me + k, wide_count) for k in range(1, wide_count)]
    long_rows, short_rows = slice(0, rows), slice(rows, 2 * rows)

    barrier = pltpu.get_barrier_semaphore()
    for peer in peers:
        pl.semaphore_signal(barrier, inc=1, device_id={"wide": peer}, device_id_type=MESH)
    pl.semaphore_signal(barrier, inc=1, device_id={"narrow": other}, device_id_type=MESH)

    loads = [
        pltpu.make_async_copy(q_hbm.at[pl.ds(rows, rows)], q_buf.at[pl.ds(rows, rows)], in_sem.at[0]),
        pltpu.make_async_copy(k_hbm.at[pl.ds(rows, rows)], ks_buf, in_sem.at[1]),
        pltpu.make_async_copy(v_hbm.at[pl.ds(rows, rows)], vs_buf, in_sem.at[2]),
        pltpu.make_async_copy(seg_hbm, seg_ref, in_sem.at[6]),
    ]
    owner_load = pltpu.make_async_copy(owner_hbm, owner_ref, in_sem.at[7])
    gain_load = pltpu.make_async_copy(gain_hbm, gain_ref, in_sem.at[9])
    late_loads = [
        pltpu.make_async_copy(k_hbm.at[pl.ds(0, rows)], k_buf.at[me], in_sem.at[3]),
        pltpu.make_async_copy(v_hbm.at[pl.ds(0, rows)], v_buf.at[me], in_sem.at[4]),
        pltpu.make_async_copy(span_hbm, span_ref, in_sem.at[8]),
        pltpu.make_async_copy(q_hbm.at[pl.ds(0, rows)], q_buf.at[pl.ds(0, rows)], in_sem.at[10]),
    ]
    res_load = pltpu.make_async_copy(res_hbm, res_buf, in_sem.at[5])
    w_loads = [
        pltpu.make_async_copy(
            w_hbm.at[:, pl.ds(c * piece, piece)], w_buf.at[c], w_sem.at[c]
        )
        for c in range(PIECES)
    ]
    for load in loads + [owner_load] + w_loads[:EARLY]:
        load.start()

    pl.semaphore_wait(barrier, wide_count)

    def kv_copy(source, peer):
        return [
            pltpu.make_async_remote_copy(
                src_ref=hbm.at[pl.ds(0, rows)],
                dst_ref=buf.at[source],
                send_sem=send.at[peer],
                recv_sem=recv.at[source],
                device_id={"wide": peer},
                device_id_type=MESH,
            )
            for hbm, buf, send, recv in (
                (k_hbm, k_buf, k_send, k_recv),
                (v_hbm, v_buf, v_send, v_recv),
            )
        ]

    for peer in peers:
        for copy in kv_copy(me, peer):
            copy.start()
    for load in w_loads[EARLY:] + [res_load, gain_load] + late_loads:
        load.start()

    row_id = lax.broadcasted_iota(jnp.int32, (rows, rows), 0)
    col_id = lax.broadcasted_iota(jnp.int32, (rows, rows), 1)

    owner_load.wait()
    owner_across = jnp.broadcast_to(owner_ref[...], (rows, rows)).astype(jnp.float32)
    owner_down = owner_across.T
    same = jnp.where((owner_down == owner_across) & (row_id < col_id), 1.0, 0.0)
    slot = jnp.sum(same, axis=0, keepdims=True)
    target = (owner_across[0:1] * capacity + slot).astype(jnp.int32)
    slots = lax.broadcasted_iota(jnp.int32, (wide_count * capacity, rows), 0)
    dispatch = jnp.where(slots == target, 1.0, 0.0).astype(jnp.bfloat16)

    def part_copy(c, phase):
        return pltpu.make_async_remote_copy(
            src_ref=part_buf.at[phase, c],
            dst_ref=recv_buf.at[c],
            send_sem=p_send.at[c],
            recv_sem=p_recv.at[c],
            device_id={"narrow": other},
            device_id_type=MESH,
        )

    def project(phase, c):
        if phase == 1:
            w_loads[c].wait()
        product = jnp.dot(att_buf[phase], w_buf[c], preferred_element_type=jnp.float32)
        part_buf[phase, c] = product.astype(jnp.bfloat16)

    def lend(phase):
        for c in range(PIECES):
            project(phase, c)
            part_copy(c, phase).start()

    def out_copy(c, source, peer):
        return pltpu.make_async_remote_copy(
            src_ref=out_buf.at[c, peer],
            dst_ref=ffn_ref.at[source, :, pl.ds(pl.multiple_of(c * span, span), span)],
            send_sem=o_send.at[c, peer],
            recv_sem=o_recv.at[c, source],
            device_id={"wide": peer},
            device_id_type=MESH,
        )

    def own_copy(c):
        return pltpu.make_async_copy(
            out_buf.at[c, me],
            ffn_ref.at[me, :, pl.ds(pl.multiple_of(c * span, span), span)],
            own_sem.at[c],
        )

    def finish(phase):
        res_load.wait()
        gain_load.wait()
        squares = jnp.zeros((rows, 1), jnp.float32)
        for step in range(PIECES + 1):
            if step < PIECES:
                project(phase, step)
            if step == 0:
                continue
            c = step - 1
            part_copy(c, phase).wait_recv()
            cols = slice(c * piece, (c + 1) * piece)
            summed = part_buf[phase, c].astype(jnp.float32) + recv_buf[c].astype(jnp.float32)
            hidden = (res_buf[:, cols].astype(jnp.float32) + summed).astype(jnp.bfloat16)
            hidden_ref[:, cols] = hidden
            widened = hidden.astype(jnp.float32)
            squares += jnp.sum(widened * widened, axis=1, keepdims=True)
        factor = lax.rsqrt(squares / model + 1e-05)
        lines = span // HEAD
        for c in range(SENDS):
            cols = slice(c * span, (c + 1) * span)
            gains = gain_ref[c * lines : (c + 1) * lines, :].astype(jnp.float32)
            gain = jnp.concatenate([gains[i : i + 1] for i in range(lines)], axis=1)
            normed = (hidden_ref[:, cols].astype(jnp.float32) * factor * gain).astype(jnp.bfloat16)
            outgoing = jnp.dot(dispatch, normed, preferred_element_type=jnp.float32)
            out_buf[c] = outgoing.astype(jnp.bfloat16).reshape(wide_count, capacity, span)
            for peer in peers:
                out_copy(c, me, peer).start()
            own_copy(c).start()

    def both(phase):
        @pl.when(lane == phase)
        def _():
            finish(phase)

        @pl.when(lane != phase)
        def _():
            lend(phase)

    for load in loads:
        load.wait()
    seg_across = jnp.broadcast_to(seg_ref[...], (rows, rows)).astype(jnp.float32)
    short_visible = (seg_across == seg_across.T) & (col_id <= row_id)
    attend_heads(
        q_buf,
        lambda group: ks_buf[:, group],
        lambda group: vs_buf[:, group],
        short_visible,
        short_rows,
        att_buf,
        1,
        local_kv,
        group_size,
    )
    both(1)

    for load in late_loads:
        load.wait()
    for peer in peers:
        for copy in kv_copy(peer, peer):
            copy.wait_recv()
    spans = span_ref[...]
    wide_ids = lax.broadcasted_iota(jnp.int32, (1, wide_count), 1)
    own_span = jnp.sum(jnp.where(wide_ids == me, spans, 0), axis=1, keepdims=True)
    long_visible = jnp.concatenate(
        [
            (spans[:, b : b + 1] * rows + col_id) <= (own_span * rows + row_id)
            for b in range(wide_count)
        ],
        axis=1,
    )
    attend_heads(
        q_buf,
        lambda group: k_buf[:, :, group].reshape(wide_count * rows, HEAD),
        lambda group: v_buf[:, :, group].reshape(wide_count * rows, HEAD),
        long_visible,
        long_rows,
        att_buf,
        0,
        local_kv,
        group_size,
    )
    both(0)

    for peer in peers:
        for copy in kv_copy(me, peer):
            copy.wait_send()

    def drain_parts(c, carry):
        part_copy(c, 0).wait_send()
        return carry

    lax.fori_loop(0, PIECES, drain_parts, 0)

    def drain_sends(c, carry):
        for peer in peers:
            out_copy(c, me, peer).wait_send()
            out_copy(c, peer, peer).wait_recv()
        own_copy(c).wait()
        return carry

    lax.fori_loop(0, SENDS, drain_sends, 0)


def store_kernel(hidden_ref, ffn_ref, hidden_out, ffn_out, sems):
    parts = ffn_ref.shape[0]
    count = hidden_ref.shape[0] // parts
    half = ffn_ref.shape[1] // 2
    copies = []
    for s in range(parts):
        some = pl.ds(s * count, count)
        copies.append(
            pltpu.make_async_copy(hidden_ref.at[some], hidden_out.at[some], sems.at[3 * s])
        )
        for j in range(2):
            some = pl.ds(j * half, half)
            copies.append(
                pltpu.make_async_copy(
                    ffn_ref.at[s, some], ffn_out.at[s, some], sems.at[3 * s + 1 + j]
                )
            )
    for copy in copies:
        copy.start()
    for copy in copies:
        copy.wait()


def fused_on_device(
    queries, key_rows, value_rows, residual, out_weight, norm_gain, span_map, segments, row_owner
):
    wide_count = lax.axis_size("wide")
    local_heads = queries.shape[1] // HEAD
    local_kv = key_rows.shape[1] // HEAD
    rows, model = residual.shape
    capacity = max(2, 2 * rows // wide_count)
    sizes = (wide_count, capacity, local_kv, local_heads // local_kv)
    bf16 = jnp.bfloat16
    dma = pltpu.SemaphoreType.DMA
    any_spec = pl.BlockSpec(memory_space=pl.ANY)
    vmem_spec = pl.BlockSpec(memory_space=pltpu.VMEM)
    piece, span = model // PIECES, model // SENDS
    hidden, arrived = pl.pallas_call(
        functools.partial(fused_kernel, sizes),
        out_shape=(
            pltpu.VMEM((rows, model), bf16),
            pltpu.VMEM((wide_count, capacity, model), bf16),
        ),
        in_specs=[any_spec] * 9,
        out_specs=(vmem_spec, vmem_spec),
        scratch_shapes=[
            pltpu.VMEM(queries.shape, bf16),
            pltpu.VMEM((rows, key_rows.shape[1]), bf16),
            pltpu.VMEM((rows, key_rows.shape[1]), bf16),
            pltpu.VMEM((wide_count, rows, key_rows.shape[1]), bf16),
            pltpu.VMEM((wide_count, rows, key_rows.shape[1]), bf16),
            pltpu.VMEM((PIECES, out_weight.shape[0], piece), bf16),
            pltpu.VMEM((rows, model), bf16),
            pltpu.VMEM((2, rows, queries.shape[1]), bf16),
            pltpu.VMEM((2, PIECES, rows, piece), bf16),
            pltpu.VMEM((PIECES, rows, piece), bf16),
            pltpu.VMEM((SENDS, wide_count, capacity, span), bf16),
            pltpu.VMEM((model // HEAD, HEAD), bf16),
            pltpu.VMEM((1, wide_count), jnp.int32),
            pltpu.VMEM((1, rows), jnp.int32),
            pltpu.VMEM((1, rows), jnp.int32),
            dma((11,)),
            dma((PIECES,)),
            dma((wide_count,)),
            dma((wide_count,)),
            dma((wide_count,)),
            dma((wide_count,)),
            dma((PIECES,)),
            dma((PIECES,)),
            dma((SENDS, wide_count)),
            dma((SENDS, wide_count)),
            dma((SENDS,)),
        ],
        compiler_params=pltpu.CompilerParams(
            collective_id=0, has_side_effects=True, vmem_limit_bytes=60 * 1024 * 1024
        ),
    )(
        span_map.reshape(1, wide_count),
        segments,
        row_owner.reshape(1, rows),
        queries,
        key_rows,
        value_rows,
        residual,
        out_weight,
        norm_gain.reshape(model // HEAD, HEAD),
    )
    hidden, arrived = pl.pallas_call(
        store_kernel,
        out_shape=(
            jax.ShapeDtypeStruct(hidden.shape, bf16),
            jax.ShapeDtypeStruct(arrived.shape, bf16),
        ),
        in_specs=[any_spec] * 2,
        out_specs=(any_spec, any_spec),
        scratch_shapes=[dma((3 * wide_count,))],
        compiler_params=pltpu.CompilerParams(vmem_limit_bytes=1024 * 1024),
    )(hidden, arrived)
    return hidden, arrived.reshape(1, 1, wide_count, capacity, model)


def on_device(*args):
    queries, residual = args[0], args[3]
    rows, model = residual.shape
    wide_count = lax.axis_size("wide")
    fits = (
        lax.axis_size("narrow") == 2
        and rows == LONG_DEV
        and queries.shape[0] == 2 * LONG_DEV
        and (2 * rows) % (32 * wide_count) == 0
        and rows % (16 * wide_count) == 0
        and model % (PIECES * HEAD) == 0
    )
    return (fused_on_device if fits else general_on_device)(*args)


def solution(mesh):
    placed = (
        P(("rep", "wide"), "narrow"),
        P(("rep", "wide"), "narrow"),
        P(("rep", "wide"), "narrow"),
        P(("rep", "wide", "narrow"), None),
        P("narrow", None),
        P(),
        P(),
        P(("rep", "wide"), None),
        P(("rep", "wide", "narrow"), None),
    )
    return jax.shard_map(
        on_device,
        mesh=mesh,
        in_specs=placed,
        out_specs=(
            P(("rep", "wide", "narrow"), None),
            P(("rep", "wide"), "narrow", None, None, None),
        ),
        check_vma=False,
    )
```
